32 devices in a mesh: head: 4 (over z), wide: 8 (over y, x, core).
Axes of the slice: x: 2, y: 2, z: 4, core: 2. Of those that a mesh axis runs over, the one named last changes fastest.
Arguments:
- hidden_in: bfloat16 [3, 8, 512, 1024], P(None, 'wide', 'head'), may hold values from -6 to 6
- cotangent: bfloat16 [3, 8, 512, 1024], P(None, 'wide', 'head'), may hold values from -6 to 6
- doc_starts: int32 [3, 4], replicated, may hold values from 0 to 4095, as said below
- gain_in: bfloat16 [1024], P(('head', 'wide')), may hold values from 0.5 to 1.5
- mamba_gate_w: bfloat16 [1024, 1536], P(('head', 'wide')), may hold values from -0.1875 to 0.1875
- mamba_in_w: bfloat16 [1024, 1536], P(('head', 'wide')), may hold values from -0.1875 to 0.1875
- mamba_bc_w: bfloat16 [1024, 256], P(('head', 'wide')), may hold values from -0.09375 to 0.09375
- mamba_dt_w: bfloat16 [1024, 24], P(('head', 'wide')), may hold values from -0.1875 to 0.1875
- dt_bias: float32 [24], replicated, may hold values from -0.5 to 1
- a_log: float32 [24], replicated, may hold values from -16 to 0
- d_skip: float32 [24], replicated, may hold values from 0.5 to 2
- conv_x: bfloat16 [4, 1536], P(None, ('head', 'wide')), may hold values from -3 to 3
- conv_bc: bfloat16 [4, 256], P(None, ('head', 'wide')), may hold values from -1.5 to 1.5
- mamba_gain: bfloat16 [1536], P(('head', 'wide')), may hold values from 0.5 to 1.5
- attn_q_w: bfloat16 [1024, 512], P(('head', 'wide')), may hold values from -0.1875 to 0.1875
- attention_key_value_weight: bfloat16 [1024, 256], P(('head', 'wide')), may hold values from -0.1875 to 0.1875
- mamba_out_w: bfloat16 [1536, 1024], P(('head', 'wide')), may hold values from -0.15625 to 0.15625
- attn_out_w: bfloat16 [512, 1024], P(('head', 'wide')), may hold values from -2 to 2
- gain_ffn: bfloat16 [1024], P(('head', 'wide')), may hold values from 0.5 to 1.5
- ffn_gate_w: bfloat16 [1024, 2048], P(('head', 'wide')), may hold values from -0.1875 to 0.1875
- ffn_up_w: bfloat16 [1024, 2048], P(('head', 'wide')), may hold values from -0.1875 to 0.1875
- ffn_down_w: bfloat16 [2048, 1024], P(('head', 'wide')), may hold values from -0.125 to 0.125
Outputs:
- out: bfloat16 [3, 8, 512, 1024], P(None, 'wide', 'head')
- grad_x: bfloat16 [3, 8, 512, 1024], P(None, 'wide', 'head')
- grad_gain_in: float32 [1024], P(('head', 'wide'))
- grad_mamba_gate_w: float32 [1024, 1536], P(('head', 'wide'))
- grad_mamba_in_w: float32 [1024, 1536], P(('head', 'wide'))
- grad_mamba_bc_w: float32 [1024, 256], P(('head', 'wide'))
- grad_mamba_dt_w: float32 [1024, 24], P(('head', 'wide'))
- grad_dt_bias: float32 [24], replicated
- grad_a_log: float32 [24], replicated
- grad_d_skip: float32 [24], replicated
- grad_conv_x: float32 [4, 1536], P(None, ('head', 'wide'))
- grad_conv_bc: float32 [4, 256], P(None, ('head', 'wide'))
- grad_mamba_gain: float32 [1536], P(('head', 'wide'))
- grad_attn_q_w: float32 [1024, 512], P(('head', 'wide'))
- grad_attn_kv_w: float32 [1024, 256], P(('head', 'wide'))
- grad_mamba_out_w: float32 [1536, 1024], P(('head', 'wide'))
- grad_attn_out_w: float32 [512, 1024], P(('head', 'wide'))
- grad_gain_ffn: float32 [1024], P(('head', 'wide'))
- grad_ffn_gate_w: float32 [1024, 2048], P(('head', 'wide'))
- grad_ffn_up_w: float32 [1024, 2048], P(('head', 'wide'))
- grad_ffn_down_w: float32 [2048, 1024], P(('head', 'wide'))
The draws below stay inside these ranges and needn't reach their ends.
Inputs may be any that keep to these rules, and one draw needn't show every extreme that they name: `doc_starts`: each row holds 4 increasing start positions: the first 0, the second in 1 .. 511, the third in 3585 .. 3840, the fourth in 3841 .. 4095; so the second document runs from the first wide block into the last.
All inputs are finite; a program needn't handle non-finite values.
Results may differ from the reference program's by a relative error of at most 0.035.
Values may be sent and summed in bfloat16 or wider, within the bound.
No kernel may reach another device: no remote copies, remote signals or barrier semaphores. Data moves between devices by JAX's collectives and lax.ppermute only.
A program may use at most 320 MiB of HBM per device.

```python
import math
from functools import partial
import jax
import jax.numpy as jnp
from jax import lax

MODEL_WIDTH = 1024
FF = 2048
HM = 24
P_SIZE = 64
N = 128
KC = 4
QUERY_HEADS = 8
KEY_VALUE_HEADS = 2
HEAD_SIZE = 64
MB = 3
DI = 1536
BLOCK_TOK = 512
BLOCKS = 8
TOKENS = 4096
N_HEAD = 4


def draw_doc_starts(key, part):
    key = jax.random.fold_in(key, 11)
    subkeys = jax.random.split(key, 3)
    opening = jnp.zeros((MB, 1), jnp.int32)
    long_start = jax.random.randint(subkeys[0], (MB, 1), 1, BLOCK_TOK)
    tail_start = jax.random.randint(subkeys[1], (MB, 1), TOKENS - BLOCK_TOK + 1, TOKENS - BLOCK_TOK // 2 + 1)
    last_start = jax.random.randint(subkeys[2], (MB, 1), TOKENS - BLOCK_TOK // 2 + 1, TOKENS)
    return jnp.concatenate([opening, long_start, tail_start, last_start], axis=1).astype(jnp.int32)


def draw_a_log(key, part):
    key = jax.random.fold_in(key, 23)
    spread = jax.random.uniform(key, (HM,), jnp.float32)
    lower = math.log(0.2 / TOKENS)
    upper = math.log(0.08)
    return (lower + (upper - lower) * spread).astype(jnp.float32)


def block_levels(stream_key, shape, cuts, least, largest):
    level, own = 1.0, jax.random.fold_in(stream_key, 6)
    for axis_at, blocks in cuts:
        draws = jnp.exp(jax.random.uniform(jax.random.fold_in(own, axis_at), (blocks,), jnp.float32, least / len(cuts), largest / len(cuts)))
        level = level * jnp.repeat(draws, shape[axis_at] // blocks).reshape([-1 if axis == axis_at else 1 for axis in range(len(shape))])
    return level


def normal_values(rng, extent, scale, most, pieces=(), kind=jnp.bfloat16):
    values = scale * jax.random.normal(rng, extent, jnp.float32)
    if pieces:
        values = values * block_levels(rng, extent, pieces, -0.22, 0.18)
    return jnp.clip(values, -most, most).astype(kind)


def setup_inputs(seed: int = 0) -> dict:
    streams_of = jax.random.split(jax.random.key(seed), 23)
    return {
        "hidden_in": normal_values(streams_of[0], (MB, BLOCKS, BLOCK_TOK, MODEL_WIDTH), 1.0, 6.0, ((1, 8), (2, 4))),
        "cotangent": normal_values(streams_of[1], (MB, BLOCKS, BLOCK_TOK, MODEL_WIDTH), 1.0, 6.0, ((1, 8), (2, 4))),
        "doc_starts": draw_doc_starts(jax.random.fold_in(streams_of[22], 71), 0),
        "gain_in": jnp.clip(1.0 + 0.1 * jax.random.normal(streams_of[3], (MODEL_WIDTH,), jnp.float32), 0.5, 1.5).astype(jnp.bfloat16),
        "mamba_gate_w": normal_values(streams_of[4], (MODEL_WIDTH, DI), MODEL_WIDTH ** -0.5, 0.1875, ((0, 32),)),
        "mamba_in_w": normal_values(streams_of[5], (MODEL_WIDTH, DI), MODEL_WIDTH ** -0.5, 0.1875, ((0, 32),)),
        "mamba_bc_w": normal_values(streams_of[6], (MODEL_WIDTH, 2 * N), (4 * MODEL_WIDTH) ** -0.5, 0.09375, ((0, 32),)),
        "mamba_dt_w": normal_values(streams_of[7], (MODEL_WIDTH, HM), MODEL_WIDTH ** -0.5, 0.1875, ((0, 32),)),
        "dt_bias": jnp.clip(jax.random.uniform(streams_of[8], (HM,), jnp.float32, -0.5, 1.0), -0.5, 1.0),
        "a_log": draw_a_log(jax.random.fold_in(streams_of[22], 71), 0),
        "d_skip": jnp.clip(jax.random.uniform(streams_of[10], (HM,), jnp.float32, 0.5, 2.0), 0.5, 2.0),
        "conv_x": normal_values(streams_of[11], (KC, DI), KC ** -0.5, 3.0, ((1, 32),)),
        "conv_bc": normal_values(streams_of[12], (KC, 2 * N), (4 * KC) ** -0.5, 1.5, ((1, 32),)),
        "mamba_gain": jnp.clip(1.0 + 0.1 * jax.random.normal(streams_of[13], (DI,), jnp.float32), 0.5, 1.5).astype(jnp.bfloat16),
        "attn_q_w": normal_values(streams_of[14], (MODEL_WIDTH, QUERY_HEADS * HEAD_SIZE), MODEL_WIDTH ** -0.5, 0.1875, ((0, 32),)),
        "attention_key_value_weight": normal_values(streams_of[15], (MODEL_WIDTH, 2 * KEY_VALUE_HEADS * HEAD_SIZE), MODEL_WIDTH ** -0.5, 0.1875, ((0, 32),)),
        "mamba_out_w": normal_values(streams_of[16], (DI, MODEL_WIDTH), DI ** -0.5, 0.15625, ((0, 32),)),
        "attn_out_w": normal_values(streams_of[17], (QUERY_HEADS * HEAD_SIZE, MODEL_WIDTH), (max(1, QUERY_HEADS * HEAD_SIZE * 64 // TOKENS)) ** -0.5, 2.0, ((0, 32),)),
        "gain_ffn": jnp.clip(1.0 + 0.1 * jax.random.normal(streams_of[18], (MODEL_WIDTH,), jnp.float32), 0.5, 1.5).astype(jnp.bfloat16),
        "ffn_gate_w": normal_values(streams_of[19], (MODEL_WIDTH, FF), MODEL_WIDTH ** -0.5, 0.1875, ((0, 32),)),
        "ffn_up_w": normal_values(streams_of[20], (MODEL_WIDTH, FF), MODEL_WIDTH ** -0.5, 0.1875, ((0, 32),)),
        "ffn_down_w": normal_values(streams_of[21], (FF, MODEL_WIDTH), FF ** -0.5, 0.125, ((0, 32),)),
    }


epsilon = 1e-05
highest = lax.Precision.HIGHEST

@jax.custom_vjp
def low(v):
    return lax.optimization_barrier(v.astype(jnp.bfloat16)).astype(jnp.float32)

@jax.custom_vjp
def low_back(v):
    return v

def low_keep(v):
    return (low(v), None)

def low_pass(kept, grad):
    return (grad,)

def back_keep(v):
    return (v, None)

def back_low(kept, grad):
    return (low(grad),)
low.defvjp(low_keep, low_pass)
low_back.defvjp(back_keep, back_low)

def product(left, right):
    return jnp.dot(left, right, precision=highest)

def rms_scale(values, scales):
    return values * lax.rsqrt(lax.optimization_barrier(jnp.mean(values * values, axis=-1, keepdims=True)) + epsilon) * scales

def doc_index(starts, positions):
    passed = (starts[None, :] <= positions[:, None]).astype(jnp.int32)
    return lax.optimization_barrier(jnp.sum(passed, axis=1)).astype(jnp.int32) - 1

def conv_mix(extended, taps_w, doc_ext, doc_here):
    length = doc_here.shape[0]
    result = jnp.zeros((length, extended.shape[1]), jnp.float32)
    for offset in range(taps_w.shape[0]):
        window = extended[offset:offset + length]
        same_doc = (doc_ext[offset:offset + length] == doc_here).astype(jnp.float32)
        result = result + taps_w[offset][None, :] * window * same_doc[:, None]
    return result

def mamba_block(state_in, inputs):
    x_act, b_grp, c_grp, step_size, log_rate, doc_here, prev_doc = inputs
    length = doc_here.shape[0]
    per_group = HM // N_HEAD
    cum_log = jnp.cumsum(log_rate, axis=0)
    index_row = jnp.arange(length)
    allowed = (index_row[:, None] >= index_row[None, :]) & (doc_here[:, None] == doc_here[None, :])
    gram_cb = jnp.einsum('tgn,sgn->gts', c_grp, b_grp, precision=highest)
    gram_heads = jnp.repeat(gram_cb, per_group, axis=0)
    log_gaps = cum_log.T[:, :, None] - cum_log.T[:, None, :]
    weights = jnp.exp(jnp.where(allowed[None], log_gaps, -1e+30)) * gram_heads * step_size.T[:, None, :]
    inside = jnp.einsum('hts,shp->thp', weights, x_act, precision=highest)
    c_heads = jnp.repeat(c_grp, per_group, axis=1)
    b_heads = jnp.repeat(b_grp, per_group, axis=1)
    entering = (doc_here == prev_doc).astype(jnp.float32)[:, None] * jnp.exp(cum_log)
    carried = jnp.einsum('thn,hpn->thp', c_heads, state_in, precision=highest) * entering[:, :, None]
    last_same = (doc_here == doc_here[length - 1]).astype(jnp.float32)
    tail_weight = jnp.exp(cum_log[length - 1][None, :] - cum_log) * step_size * last_same[:, None]
    state_loc = jnp.einsum('sh,shp,shn->hpn', tail_weight, x_act, b_heads, precision=highest)
    block_decay = jnp.where(doc_here[length - 1] == prev_doc, jnp.exp(cum_log[length - 1]), 0.0)
    return (block_decay[:, None, None] * state_in + state_loc, inside + carried)

def attend_rows(inputs, keys_heads, vals_heads, key_pos, key_docs, score_scale):
    q_rows, row_pos, row_doc = inputs
    scores = low_back(jnp.einsum('qhd,khd->hqk', q_rows, keys_heads, precision=highest) * score_scale)
    allowed = (key_pos[None, :] <= row_pos[:, None]) & (key_docs[None, :] == row_doc[:, None])
    masked = jnp.where(allowed[None], scores, -1e+30)
    probs = low(jax.nn.softmax(masked, axis=-1))
    return low(low_back(jnp.einsum('hqk,khd->qhd', probs, vals_heads, precision=highest)))

def layer(x_in, params, starts):
    gain_in, gate_zw, input_w, bc_w, dt_w, dt_bias, a_log, d_skip, conv_x, conv_bc, mamba_gain, query_w, kv_w, out_mw, out_aw, gain_ffn, gate_w, up_w, down_w = params
    positions = jnp.arange(TOKENS, dtype=jnp.int32)
    docs = doc_index(starts, positions)
    normed = low(rms_scale(x_in, gain_in))
    gate_z = low_back(product(normed, gate_zw))
    x_raw = low_back(product(normed, input_w))
    dt_raw = low_back(product(normed, dt_w))
    queries = low(low_back(product(normed, query_w)))
    query_group_size = QUERY_HEADS // N_HEAD
    pad_docs = jnp.concatenate([-jnp.ones((KC - 1,), jnp.int32), docs])
    x_act = jax.nn.silu(conv_mix(jnp.concatenate([jnp.zeros((KC - 1, DI), jnp.float32), x_raw]), conv_x, pad_docs, docs))
    b_list = []
    c_list = []
    kv_list = []
    for query_grouping in range(N_HEAD):
        bc_raw = low_back(product(normed, bc_w))
        bc_act = jax.nn.silu(conv_mix(jnp.concatenate([jnp.zeros((KC - 1, 2 * N), jnp.float32), bc_raw]), conv_bc, pad_docs, docs))
        b_list.append(bc_act[:, :N])
        c_list.append(bc_act[:, N:])
        key_value_head = query_grouping * query_group_size // (QUERY_HEADS // KEY_VALUE_HEADS)
        kv_list.append(low(low_back(product(normed, kv_w[:, 2 * HEAD_SIZE * key_value_head:2 * HEAD_SIZE * (key_value_head + 1)]))))
    step_size = jax.nn.softplus(dt_raw + dt_bias[None, :])
    log_rate = -jnp.exp(a_log)[None, :] * step_size
    blocks = TOKENS // BLOCK_TOK
    prev_docs = doc_index(starts, jnp.arange(blocks, dtype=jnp.int32) * BLOCK_TOK - 1)
    scanned = (x_act.reshape(blocks, BLOCK_TOK, HM, P_SIZE), jnp.stack(b_list, axis=1).reshape(blocks, BLOCK_TOK, N_HEAD, N), jnp.stack(c_list, axis=1).reshape(blocks, BLOCK_TOK, N_HEAD, N), step_size.reshape(blocks, BLOCK_TOK, HM), log_rate.reshape(blocks, BLOCK_TOK, HM), docs.reshape(blocks, BLOCK_TOK), prev_docs)
    mamba_y = lax.scan(jax.checkpoint(mamba_block), jnp.zeros((HM, P_SIZE, N), jnp.float32), scanned)[1]
    mixed = mamba_y.reshape(TOKENS, HM, P_SIZE) + d_skip[None, :, None] * x_act.reshape(TOKENS, HM, P_SIZE)
    gated_y = mixed * jax.nn.silu(gate_z).reshape(TOKENS, HM, P_SIZE)
    mamba_low = low(rms_scale(gated_y, mamba_gain.reshape(HM, P_SIZE)).reshape(TOKENS, DI))
    kv_stack = jnp.stack(kv_list, axis=1)
    keys_heads = jnp.repeat(kv_stack[:, :, :HEAD_SIZE], query_group_size, axis=1)
    vals_heads = jnp.repeat(kv_stack[:, :, HEAD_SIZE:], query_group_size, axis=1)
    rows_q = min(512, TOKENS)
    attend = jax.checkpoint(partial(attend_rows, keys_heads=keys_heads, vals_heads=vals_heads, key_pos=positions, key_docs=docs, score_scale=HEAD_SIZE ** (-0.5)))
    attn = lax.map(attend, (queries.reshape(TOKENS // rows_q, rows_q, QUERY_HEADS, HEAD_SIZE), positions.reshape(TOKENS // rows_q, rows_q), docs.reshape(TOKENS // rows_q, rows_q)))
    attn = attn.reshape(TOKENS, QUERY_HEADS * HEAD_SIZE)
    mix = low_back(product(mamba_low, out_mw) + product(attn, out_aw))
    resid = x_in + mix
    ffn_in = low(rms_scale(resid, gain_ffn))
    gate_val = low_back(product(ffn_in, gate_w))
    up_val = low_back(product(ffn_in, up_w))
    act_low = low(jax.nn.silu(gate_val) * up_val)
    return resid + low_back(product(act_low, down_w))

def reference(hidden_in, cotangent, doc_starts, gain_in, mamba_gate_w, mamba_in_w, mamba_bc_w, mamba_dt_w, dt_bias, a_log, d_skip, conv_x, conv_bc, mamba_gain, attn_q_w, attention_key_value_weight, mamba_out_w, attn_out_w, gain_ffn, ffn_gate_w, ffn_up_w, ffn_down_w):
    params = tuple((weight_arg.astype(jnp.float32) for weight_arg in (gain_in, mamba_gate_w, mamba_in_w, mamba_bc_w, mamba_dt_w, dt_bias, a_log, d_skip, conv_x, conv_bc, mamba_gain, attn_q_w, attention_key_value_weight, mamba_out_w, attn_out_w, gain_ffn, ffn_gate_w, ffn_up_w, ffn_down_w)))
    outputs = []
    input_grads = []
    totals = None
    for micro in range(MB):
        x_in = hidden_in[micro].reshape(TOKENS, MODEL_WIDTH).astype(jnp.float32)
        result, pullback = jax.vjp(partial(layer, starts=doc_starts[micro]), x_in, params)
        grad_in, grad_params = pullback(cotangent[micro].reshape(TOKENS, MODEL_WIDTH).astype(jnp.float32))
        outputs.append(result.astype(jnp.bfloat16).reshape(BLOCKS, BLOCK_TOK, MODEL_WIDTH))
        input_grads.append(grad_in.astype(jnp.bfloat16).reshape(BLOCKS, BLOCK_TOK, MODEL_WIDTH))
        totals = grad_params if totals is None else jax.tree.map(jnp.add, totals, grad_params)
    return (jnp.stack(outputs), jnp.stack(input_grads), totals[0], totals[1], totals[2], totals[3], totals[4], totals[5], totals[6], totals[7], totals[8], totals[9], totals[10], totals[11], totals[12], totals[13], totals[14], totals[15], totals[16], totals[17], totals[18])
```

```python
from functools import partial

import jax
import jax.numpy as jnp
from jax import lax
from jax.experimental import pallas as pl
from jax.experimental.pallas import tpu as pltpu
from jax.sharding import PartitionSpec as P

QUERY_HEADS = 8
KEY_VALUE_HEADS = 2
HEAD_SIZE = 64
GROUP = QUERY_HEADS // KEY_VALUE_HEADS
LANES = 128
LOW = jnp.bfloat16
FAR = -1e30
ALL = ("head", "wide")

epsilon = 1e-05
highest = lax.Precision.HIGHEST


def nn(left, right):
    return jnp.dot(left, right, preferred_element_type=jnp.float32)


def nt(left, right):
    return lax.dot_general(left, right, (((1,), (1,)), ((), ())), preferred_element_type=jnp.float32)


def tn(left, right):
    return lax.dot_general(left, right, (((0,), (0,)), ((), ())), preferred_element_type=jnp.float32)


def split_low(value, parts):
    terms = []
    for _ in range(parts):
        term = value.astype(LOW)
        terms.append(term)
        value = value - term.astype(jnp.float32)
    return terms


def shape(dims, kind=jnp.float32):
    return jax.ShapeDtypeStruct(dims, kind)


def shifted(value, axis, steps):
    count = lax.axis_size(axis)
    initial, last = (max(0, -steps), min(count, count - steps))
    return lax.ppermute(value, axis, [(source, source + steps) for source in range(initial, last)])


def swapped(value, axis, bit):
    count = lax.axis_size(axis)
    return lax.ppermute(value, axis, [(i, i ^ bit) for i in range(count)])


def pick(array, index, axis=0):
    return lax.dynamic_index_in_dim(array, index, axis, False)


def guess(us):
    return pl.CostEstimate(flops=int(us * 1e9), bytes_accessed=int(us * 3e6), transcendentals=0)


def gather_head(own, receivers, when=()):
    count = lax.axis_size("head")
    place = lax.axis_index("head")
    both = jnp.zeros((count,) + own.shape, own.dtype)
    both = lax.dynamic_update_index_in_dim(both, own, place, 0)
    for step in range(1, count):
        pairs = [(i, (i + step) % count) for i in range(count) if (i + step) % count < receivers]
        got = after(lax.ppermute(own, "head", pairs), *when)
        both = lax.dynamic_update_index_in_dim(both, got, (place - step) % count, 0)
    return both.reshape(-1, own.shape[1])


def after(value, *others):
    return lax.optimization_barrier((value,) + others)[0] if others else value


def to_blocks(pieces, when=()):
    count = lax.axis_size("head")
    place = lax.axis_index("head")
    micro_count = pieces.shape[0]

    def of(target):
        return pick(pieces, jnp.minimum(target, micro_count - 1))

    own = jnp.where(place < micro_count, of(place), jnp.zeros_like(pieces[0]))
    block = jnp.zeros((count,) + pieces.shape[1:], pieces.dtype)
    block = lax.dynamic_update_index_in_dim(block, own, place, 0)
    for step in range(1, count):
        pairs = [(i, (i + step) % count) for i in range(count) if (i + step) % count < micro_count]
        got = after(lax.ppermute(of((place + step) % count), "head", pairs), *when)
        block = lax.dynamic_update_index_in_dim(block, got, (place - step) % count, 0)
    return block.reshape(count * pieces.shape[1], pieces.shape[2])


def from_blocks(block, micro_count, when=()):
    count = lax.axis_size("head")
    place = lax.axis_index("head")
    parts = block.reshape(count, block.shape[0] // count, block.shape[1])
    pieces = jnp.zeros_like(parts)
    pieces = lax.dynamic_update_index_in_dim(pieces, pick(parts, place), place, 0)
    for step in range(1, count):
        pairs = [(i, (i + step) % count) for i in range(min(micro_count, count))]
        got = after(lax.ppermute(pick(parts, (place + step) % count), "head", pairs), *when)
        pieces = lax.dynamic_update_index_in_dim(pieces, got, (place - step) % count, 0)
    return pieces[:micro_count]


def sum_everywhere(value):
    for axis in ALL:
        step = 1
        while step < lax.axis_size(axis):
            value = value + swapped(value, axis, step)
            step *= 2
    return value


def wide_bits():
    bits = []
    while 1 << (len(bits) + 1) <= lax.axis_size("wide"):
        bits.append(1 << len(bits))
    return bits


class Gathered:
    def __init__(self, own):
        bits = wide_bits()
        half = own.shape[1] // 2
        self.parts = [own[:, :half], own[:, half:]]
        self.left = [bits[1:], bits[:0:-1]]
        self.done = [[], []]

    def step(self):
        place = lax.axis_index("wide")
        for i in range(2):
            bit = self.left[i].pop(0)
            array = self.parts[i]
            got = swapped(array, "wide", bit)
            mine = (place // bit) % 2
            self.parts[i] = jnp.where(mine == 0, jnp.stack([array, got]), jnp.stack([got, array]))
            self.done[i].insert(0, bit)

    def rest(self):
        while self.left[0]:
            self.step()
        arrays = []
        for array, done in zip(self.parts, self.done):
            ranks = [done.index(bit) for bit in sorted(done, reverse=True)]
            arrays.append(array.transpose(ranks + [len(done), len(done) + 1]))
        both = jnp.concatenate(arrays, axis=-1)
        got = swapped(both, "wide", 1)
        mine = lax.axis_index("wide") % 2
        stacked = jnp.where(mine == 0, jnp.stack([both, got], axis=-3), jnp.stack([got, both], axis=-3))
        return stacked.reshape(-1, both.shape[-1])


class Reduced:
    def __init__(self, array):
        self.bits = wide_bits()
        self.orders = [self.bits[1:], self.bits[:0:-1]]
        self.parts = [array.reshape((array.shape[0], -1, 2) + array.shape[2:])]
        self.axes = [[1]]
        self.steps = len(self.bits)

    def begin(self):
        self.moves = []
        for i, part in enumerate(self.parts):
            bit = 1 if len(self.parts) == 1 else self.orders[i].pop(0)
            axis = 2 if len(self.parts) == 1 else 1 + self.axes[i].index(bit)
            mine = (lax.axis_index("wide") // bit) % 2
            send = pick(part, 1 - mine, axis)
            self.moves.append((bit, pick(part, mine, axis), send, swapped(send, "wide", bit)))
        return [send for _, _, send, _ in self.moves]

    def end(self, *when):
        parts = []
        for bit, kept, _, got in self.moves:
            parts.append((kept.astype(jnp.float32) + after(got, *when).astype(jnp.float32)).astype(kept.dtype))
        if len(parts) == 1:
            half = parts[0].shape[0] // 2
            self.axes = [list(self.bits[:0:-1]) for _ in range(2)]
            parts = [
                part.reshape((half,) + (2,) * len(axes) + part.shape[2:])
                for part, axes in zip((parts[0][:half], parts[0][half:]), self.axes)
            ]
        else:
            for axes, (bit, _, _, _) in zip(self.axes, self.moves):
                axes.remove(bit)
        self.parts = parts
        self.steps -= 1

    def rest(self):
        while self.steps:
            self.begin()
            self.end()
        return jnp.concatenate(self.parts, axis=0)


def reduce_head(array, sources, when=()):
    count = lax.axis_size("head")
    place = lax.axis_index("head")
    total = jnp.where(place < sources, pick(array, place).astype(jnp.float32), 0.0)
    for step in range(1, count):
        pairs = [(i, (i + step) % count) for i in range(min(sources, count))]
        got = after(lax.ppermute(pick(array, (place + step) % count), "head", pairs), *when)
        total = total + got.astype(jnp.float32)
    return total


def sum_wide(array):
    return lax.psum_scatter(array, "wide", scatter_dimension=0, tiled=True)


def owned(part, sources, when=()):
    return reduce_head(part.reshape(lax.axis_size("head"), -1, part.shape[1]), sources, when)


class Carried:
    def __init__(self, sent, total, rows, backward):
        self.sent, self.total, self.rows = sent, total, rows
        self.state = jnp.zeros_like(total)
        self.backward = backward
        self.left = wide_bits()

    def step(self, *when):
        bit = self.left.pop(0)
        got = after(swapped(self.sent, "wide", bit), *when)
        mine = (lax.axis_index("wide") // bit) % 2
        ahead = 1 - mine if self.backward else mine
        self.total, self.state, self.rows, self.sent = join(
            self.total, self.state, self.rows, got, jnp.reshape(ahead, (1,)).astype(jnp.int32)
        )

    def rest(self, *when):
        while self.left:
            self.step(*when)
        return self.state


def rms_scale(values, scales):
    return values * lax.rsqrt(jnp.mean(values * values, axis=-1, keepdims=True) + epsilon) * scales


def doc_index(starts, positions):
    passed = (starts[None, :] <= positions[:, None]).astype(jnp.int32)
    return jnp.sum(passed, axis=1) - 1


def split_at(array, sizes, axis):
    out, at = [], 0
    for size in sizes:
        out.append(lax.slice_in_dim(array, at, at + size, axis=axis))
        at += size
    return out


def packed(parts, rows):
    flat = jnp.concatenate([part.reshape(-1) for part in parts])
    columns = -(-flat.shape[0] // rows)
    return jnp.pad(flat, (0, rows * columns - flat.shape[0])).reshape(rows, columns)


CHUNK = 128
EXTRA = 16


def spread(value, spread_ref):
    return nn(jnp.concatenate(split_low(value, 2), axis=1), spread_ref[...])


def gathered(value, gather_ref):
    return nn(value.astype(LOW), gather_ref[...])


def gathered_fine(value, gather_ref):
    high, rest = split_low(value, 2)
    return nn(high, gather_ref[...]) + nn(rest, gather_ref[...])


def with_decay(state, decay):
    terms = split_low(decay, 3) + [jnp.zeros((EXTRA - 3, decay.shape[1]), LOW)]
    return jnp.concatenate([state.astype(LOW)] + terms, axis=0)


def silu_parts(value):
    sigma = jax.nn.sigmoid(value)
    return value * sigma, sigma * (1.0 + value * (1.0 - sigma))


def local_kernel(
    x_ref, xp_ref, bc_ref, bcp_ref, rimx_ref, rimb_ref, dt_ref, marks_ref, tapx_ref, tapb_ref, bias_ref, rate_ref, spread_ref,
    act_ref, slope_ref, bcact_ref, bcslope_ref, step_ref, cum_ref, sent_ref, state_ref, decay_ref,
):
    part = pl.program_id(0)
    marks = marks_ref[...]

    def conv(raw_ref, prev_ref, rim_ref, tap_ref):
        before = jnp.where(part == 0, rim_ref[...], prev_ref[...])
        both = jnp.concatenate([before, raw_ref[...]], axis=0)
        taps = 4
        total = None
        for i in range(taps):
            term = both[8 - taps + 1 + i : 8 - taps + 1 + i + CHUNK] * tap_ref[i : i + 1, :] * marks[:, i : i + 1]
            total = term if total is None else total + term
        return silu_parts(total)

    act, slope = conv(x_ref, xp_ref, rimx_ref, tapx_ref)
    act_ref[...] = act
    slope_ref[...] = slope.astype(LOW)
    bc, bc_slope = conv(bc_ref, bcp_ref, rimb_ref, tapb_ref)
    bcact_ref[...] = bc.astype(LOW)
    bcslope_ref[...] = bc_slope.astype(LOW)
    lane = lax.broadcasted_iota(jnp.int32, (CHUNK, LANES), 1)
    value = dt_ref[...] + bias_ref[0:1, :]
    softplus = jnp.maximum(value, 0.0) + jnp.log1p(jnp.exp(-jnp.abs(value)))
    step = jnp.where(rate_ref[0:1, :] < 0.0, softplus, 0.0)
    row = lax.broadcasted_iota(jnp.int32, (CHUNK, CHUNK), 0)
    col = lax.broadcasted_iota(jnp.int32, (CHUNK, CHUNK), 1)
    cum = jnp.dot((col <= row).astype(jnp.float32), step * rate_ref[0:1, :], precision=highest, preferred_element_type=jnp.float32)
    step_ref[...] = step
    cum_ref[...] = cum
    tail = jnp.exp(cum[CHUNK - 1 :] - cum) * marks[:, 5:6] * step
    weighted = (act * spread(tail, spread_ref)).astype(LOW)
    decay = spread(jnp.exp(cum[CHUNK - 8 :]) * marks[CHUNK - 8 :, 7:8], spread_ref)[7:8]
    own = tn(bc[:, :LANES].astype(LOW), weighted)

    @pl.when(part == 0)
    def _():
        state_ref[...] = own
        decay_ref[...] = jnp.ones_like(decay_ref)
        decay_ref[0:1, :] = decay

    @pl.when(part > 0)
    def _():
        state_ref[...] = state_ref[...] * decay + own
        decay_ref[0:1, :] = decay_ref[0:1, :] * decay

    @pl.when(part == pl.num_programs(0) - 1)
    def _():
        sent_ref[...] = with_decay(state_ref[...], decay_ref[0:1, :])


def join_kernel(ahead_ref, total_ref, state_ref, rows_ref, got_ref, total_out, state_out, rows_out, sent_out):
    size = total_ref.shape[0]
    got = got_ref[:size, :].astype(jnp.float32)
    extra = got_ref[size:, :].astype(jnp.float32)
    got_decay = extra[0:1] + extra[1:2] + extra[2:3]
    decay, sweep = rows_ref[0:1, :], rows_ref[1:2, :]
    rows_out[...] = jnp.ones_like(rows_out)
    rows_out[0:1, :] = decay * got_decay

    @pl.when(ahead_ref[0] == 1)
    def _():
        state_out[...] = state_ref[...] + sweep * got
        rows_out[1:2, :] = sweep * got_decay
        total_out[...] = total_ref[...] + decay * got

    @pl.when(ahead_ref[0] == 0)
    def _():
        state_out[...] = state_ref[...]
        rows_out[1:2, :] = sweep
        total_out[...] = got + got_decay * total_ref[...]

    sent_out[...] = with_decay(total_out[...], decay * got_decay)


def mix_kernel(
    act_ref, bcact_ref, z_ref, step_ref, cum_ref, marks_ref, docs_ref, first_ref, skip_ref, gain_ref, spread_ref, gather_ref,
    ym_ref, y_ref, entry_ref, state_ref, inner_ref,
):
    part = pl.program_id(0)

    @pl.when(part == 0)
    def _():
        state_ref[...] = first_ref[...]

    marks = marks_ref[...]
    cum = cum_ref[...]
    cum_rows = cum.T
    step = step_ref[...]
    b_mat = bcact_ref[:, :LANES]
    c_mat = bcact_ref[:, LANES:]
    act = act_ref[...]
    stepped = act * spread(step, spread_ref)
    low_stepped = stepped.astype(LOW)
    row = lax.broadcasted_iota(jnp.int32, (CHUNK, CHUNK), 0)
    col = lax.broadcasted_iota(jnp.int32, (CHUNK, CHUNK), 1)
    allowed = (row >= col) & (marks[:, 6:7] == docs_ref[0:1, :])
    gram = jnp.where(allowed, nt(c_mat, b_mat), 0.0)
    first = lax.broadcasted_iota(jnp.int32, (CHUNK, LANES), 1) < LANES // 2
    pairs = act.shape[1] // LANES
    for pair in range(pairs):
        parts = []
        for head in (2 * pair, 2 * pair + 1):
            gaps = jnp.minimum(cum[:, head : head + 1] - cum_rows[head : head + 1, :], 0.0)
            parts.append((jnp.exp(gaps) * gram).astype(LOW))
        values = low_stepped[:, pair * LANES : (pair + 1) * LANES]
        zero = jnp.zeros_like(values)
        inner_ref[:, pair * LANES : (pair + 1) * LANES] = nn(
            jnp.concatenate(parts, axis=1),
            jnp.concatenate([jnp.where(first, values, zero), jnp.where(first, zero, values)], axis=0),
        )
    state = state_ref[...]
    low_state = state.astype(LOW)
    entry_ref[0] = low_state
    entering = spread(jnp.exp(cum) * marks[:, 4:5], spread_ref)
    y = inner_ref[...] + nn(c_mat, low_state) * entering + skip_ref[0:1, :] * act
    y_ref[...] = y
    gated = y * silu_parts(z_ref[...])[0]
    scale = lax.rsqrt(gathered(gated * gated, gather_ref) * (2.0 / LANES) + epsilon)
    ym_ref[...] = (gated * spread(scale, spread_ref) * gain_ref[0:1, :]).astype(LOW)
    tail = jnp.exp(cum[CHUNK - 1 :] - cum) * marks[:, 5:6]
    weighted = (stepped * spread(tail, spread_ref)).astype(LOW)
    decay = spread(jnp.exp(cum[CHUNK - 8 :]) * marks[CHUNK - 8 :, 7:8], spread_ref)[7:8]
    state_ref[...] = state * decay + tn(b_mat, weighted)


def gate_back_kernel(
    dym_ref, y_ref, z_ref, bcact_ref, cum_ref, marks_ref, gain_ref, spread_ref, gather_ref,
    dz_ref, dy_ref, dgain_ref, sent_ref, state_ref, decay_ref,
):
    part = pl.program_id(0)
    marks = marks_ref[...]
    cum = cum_ref[...]
    y = y_ref[...]
    silu, slope = silu_parts(z_ref[...])
    gated = y * silu
    scale = lax.rsqrt(gathered(gated * gated, gather_ref) * (2.0 / LANES) + epsilon)
    wide_scale = spread(scale, spread_ref)
    d_normed = dym_ref[...]
    d_gain = jnp.sum(d_normed * gated * wide_scale, axis=0, keepdims=True)
    u = d_normed * gain_ref[0:1, :]
    inner = gathered(u * gated, gather_ref) * (2.0 / LANES) * scale * scale * scale
    d_gated = u * wide_scale - gated * spread(inner, spread_ref)
    dz_ref[...] = (d_gated * y * slope).astype(LOW)
    dy = d_gated * silu
    dy_ref[...] = dy
    entering = spread(jnp.exp(cum) * marks[:, 4:5], spread_ref)
    own = tn(bcact_ref[:, LANES:], (dy * entering).astype(LOW))
    decay = spread(jnp.exp(cum[CHUNK - 8 :]) * marks[CHUNK - 8 :, 7:8], spread_ref)[7:8]

    @pl.when(part == 0)
    def _():
        state_ref[...] = own
        decay_ref[...] = jnp.ones_like(decay_ref)
        decay_ref[0:1, :] = decay
        dgain_ref[0:1, :] = d_gain

    @pl.when(part > 0)
    def _():
        state_ref[...] = state_ref[...] * decay + own
        decay_ref[0:1, :] = decay_ref[0:1, :] * decay
        dgain_ref[0:1, :] += d_gain

    @pl.when(part == pl.num_programs(0) - 1)
    def _():
        sent_ref[...] = with_decay(state_ref[...], decay_ref[0:1, :])


def scan_back_kernel(
    act_ref, slope_ref, bcact_ref, bcslope_ref, dt_ref, step_ref, cum_ref, marks_ref, docs_ref, dy_ref, entry_ref, first_ref,
    skip_ref, bias_ref, rate_ref, spread_ref, gather_ref, x_ref, xp_ref, bc_ref, bcp_ref, rimx_ref, rimb_ref, tapx_ref, tapb_ref,
    dscan_ref, dskip_ref, dhead_ref, dtap_ref, rim_ref, edge_ref, state_ref, inner_ref, rows_ref, next_ref, nextm_ref,
):
    part = pl.program_id(0)

    @pl.when(part == 0)
    def _():
        state_ref[...] = first_ref[...]
        rows_ref[...] = jnp.zeros_like(rows_ref)
        dskip_ref[...] = jnp.zeros_like(dskip_ref)
        dhead_ref[...] = jnp.zeros_like(dhead_ref)
        dtap_ref[...] = jnp.zeros_like(dtap_ref)
        next_ref[...] = jnp.zeros_like(next_ref)
        nextm_ref[...] = jnp.zeros_like(nextm_ref)

    marks = marks_ref[...]
    cum = cum_ref[...]
    cum_rows = cum.T
    step = step_ref[...]
    b_mat = bcact_ref[:, :LANES]
    c_mat = bcact_ref[:, LANES:]
    act = act_ref[...]
    wide_step = spread(step, spread_ref)
    stepped = act * wide_step
    low_stepped = stepped.astype(LOW)
    dy = dy_ref[...]
    low_dy = dy.astype(LOW)
    row = lax.broadcasted_iota(jnp.int32, (CHUNK, CHUNK), 0)
    col = lax.broadcasted_iota(jnp.int32, (CHUNK, CHUNK), 1)
    allowed = (row <= col) & (marks[:, 6:7] == docs_ref[0:1, :])
    gram = jnp.where(allowed, nt(b_mat, c_mat), 0.0)
    first = lax.broadcasted_iota(jnp.int32, (CHUNK, LANES), 1) < LANES // 2
    lane = lax.broadcasted_iota(jnp.int32, (CHUNK, LANES), 1)
    pairs = act.shape[1] // LANES
    d_gram = jnp.zeros((CHUNK, CHUNK), jnp.float32)
    leaving = jnp.zeros((CHUNK, LANES), jnp.float32)
    for pair in range(pairs):
        cols = slice(pair * LANES, (pair + 1) * LANES)
        values, grads = low_stepped[:, cols], low_dy[:, cols]
        zero = jnp.zeros_like(values)
        d_weights = nt(jnp.concatenate([jnp.where(first, values, zero), jnp.where(first, zero, values)], axis=0), grads)
        parts = []
        for i, head in enumerate((2 * pair, 2 * pair + 1)):
            fade = jnp.exp(jnp.minimum(cum_rows[head : head + 1, :] - cum[:, head : head + 1], 0.0))
            d_weight = d_weights[i * CHUNK : (i + 1) * CHUNK]
            weight = fade * gram
            d_gram = d_gram + d_weight * fade
            moved = d_weight * weight
            rows_ref[head : head + 1, :] = jnp.sum(moved, axis=0, keepdims=True)
            leaving = jnp.where(lane == head, jnp.sum(moved, axis=1, keepdims=True), leaving)
            parts.append(weight.astype(LOW))
        inner_ref[:, cols] = nn(
            jnp.concatenate(parts, axis=1),
            jnp.concatenate([jnp.where(first, grads, zero), jnp.where(first, zero, grads)], axis=0),
        )
    d_state = state_ref[...]
    low_d_state = d_state.astype(LOW)
    entry = entry_ref[0]
    entering = spread(jnp.exp(cum) * marks[:, 4:5], spread_ref)
    tail = spread(jnp.exp(cum[CHUNK - 1 :] - cum) * marks[:, 5:6], spread_ref)
    from_state = nn(b_mat, low_d_state) * tail
    d_stepped = inner_ref[...] + from_state
    out_moved = gathered_fine(stepped * from_state, gather_ref)
    entering_dy = dy * entering
    in_moved = gathered_fine(entering_dy * nn(c_mat, entry), gather_ref)
    low_entering_dy = entering_dy.astype(LOW)
    low_gram = jnp.where(allowed, d_gram, 0.0).astype(LOW)
    d_b = nt((stepped * tail).astype(LOW), low_d_state) + nn(low_gram, c_mat)
    d_c = nt(low_entering_dy, entry) + tn(low_gram, b_mat)
    decay_small = jnp.exp(cum[CHUNK - 8 :]) * marks[CHUNK - 8 :, 7:8]
    decay = spread(decay_small, spread_ref)[7:8]
    overlap = jnp.sum(d_state * entry.astype(jnp.float32), axis=0, keepdims=True)
    d_decay = nn(jnp.concatenate(split_low(jnp.broadcast_to(overlap, (8, overlap.shape[1])), 2), axis=0), gather_ref[...])
    at_end = jnp.sum(out_moved, axis=0, keepdims=True) + (d_decay[0:1] + d_decay[8:9]) * decay_small[7:8]
    d_cum = rows_ref[...].T - leaving + in_moved - out_moved
    d_cum = d_cum + jnp.where(lax.broadcasted_iota(jnp.int32, d_cum.shape, 0) == CHUNK - 1, at_end, 0.0)
    d_log = jnp.dot((row <= col).astype(jnp.float32), d_cum, precision=highest, preferred_element_type=jnp.float32)
    rate = rate_ref[0:1, :]
    d_step = gathered_fine(act * d_stepped, gather_ref) + d_log * rate
    d_dt = d_step * jax.nn.sigmoid(dt_ref[...] + bias_ref[0:1, :])
    d_dt = jnp.where(rate < 0.0, d_dt, 0.0)
    inner = act.shape[1]
    scan = inner + 2 * LANES
    dscan_ref[:, scan:] = d_dt.astype(LOW)
    dhead_ref[0:1, :] += jnp.sum(d_dt, axis=0, keepdims=True)
    dhead_ref[1:2, :] += jnp.sum(d_log * rate * step, axis=0, keepdims=True)
    dskip_ref[0:1, :] += jnp.sum(dy * act, axis=0, keepdims=True)
    taps = 4
    marks_ext = jnp.concatenate([marks, nextm_ref[...]], axis=0)

    def conv_back(d_pre, lanes, raw_ref, prev_ref, edge_raw_ref, tap_ref):
        before = jnp.where(part == pl.num_programs(0) - 1, edge_raw_ref[...], prev_ref[...])
        raw = jnp.concatenate([before, raw_ref[...]], axis=0)
        ext = jnp.concatenate([d_pre, next_ref[:, lanes]], axis=0)
        top = jnp.concatenate([jnp.zeros_like(ext[:8]), d_pre[:8]], axis=0)
        top_marks = jnp.concatenate([marks[:8], marks[:8]], axis=0)
        d_raw, rim = None, None
        for i in range(taps):
            ahead = taps - 1 - i
            tap = tap_ref[i : i + 1, :]
            masked = d_pre * marks[:, i : i + 1]
            dtap_ref[i : i + 1, lanes] += jnp.sum(masked * raw[8 - ahead : 8 - ahead + CHUNK], axis=0, keepdims=True)
            term = (ext * marks_ext[:, i : i + 1])[ahead : ahead + CHUNK] * tap
            d_raw = term if d_raw is None else d_raw + term
            if ahead:
                term = (top * top_marks[:, i : i + 1])[ahead : ahead + 8] * tap
                rim = term if rim is None else rim + term
        next_ref[:, lanes] = d_pre[:8]
        dscan_ref[:, lanes] = d_raw.astype(LOW)
        rim_ref[:, lanes] = rim

        @pl.when(part == 0)
        def _():
            edge_ref[:, lanes] = d_raw[CHUNK - 8 :]

    conv_back(
        (d_stepped * wide_step + dy * skip_ref[0:1, :]) * slope_ref[...].astype(jnp.float32),
        slice(0, inner), x_ref, xp_ref, rimx_ref, tapx_ref,
    )
    conv_back(
        jnp.concatenate([d_b, d_c], axis=1) * bcslope_ref[...].astype(jnp.float32),
        slice(inner, scan), bc_ref, bcp_ref, rimb_ref, tapb_ref,
    )
    nextm_ref[...] = marks[:8]
    state_ref[...] = d_state * decay + tn(c_mat, low_entering_dy)


def head_matrices(inner, heads):
    owner = jnp.arange(inner, dtype=jnp.int32) // (inner // heads)
    gather_m = (owner[:, None] == jnp.arange(LANES, dtype=jnp.int32)[None, :]).astype(LOW)
    return jnp.concatenate([gather_m.T, gather_m.T], axis=0), gather_m


def lanes_row(vector):
    return jnp.pad(vector, (0, LANES - vector.shape[0]))[None, :]


def call(kernel, name, us, parts, ins, outs, scratch, reverse=False):
    def spec(block, how):
        if how == "part":
            how = lambda c: (c,) + (0,) * (len(block) - 1)
        elif how == "whole":
            how = lambda c: (0,) * len(block)
        elif isinstance(how, int):
            column = how
            how = lambda c: (c, column)

        def index(c):
            return how(parts - 1 - c if reverse else c)

        return pl.BlockSpec(block, index)

    return pl.pallas_call(
        kernel,
        grid=(parts,),
        in_specs=[spec(block, how) for _, block, how in ins],
        out_specs=[spec(block, how) for _, block, how in outs],
        scratch_shapes=scratch,
        out_shape=[shape for shape, _, _ in outs],
        compiler_params=pltpu.CompilerParams(vmem_limit_bytes=56 * 2**20),
        cost_estimate=guess(us),
        name=name,
    )(*[array for array, _, _ in ins])


def mamba_local(raw, rim, marks, taps, bias, rate, cols, mats):
    length = raw.shape[0]
    parts = length // CHUNK
    inner, n2, x_at, bc_at, dt_at = cols
    before = CHUNK // 8

    def prev(column):
        return lambda c: (jnp.maximum(c * before - 1, 0), column)

    return call(
        local_kernel,
        "mamba_local",
        11,
        parts,
        [
            (raw, (CHUNK, inner), x_at),
            (raw, (8, inner), prev(x_at)),
            (raw, (CHUNK, n2), bc_at),
            (raw, (8, n2), prev(bc_at)),
            (rim[:, :inner], (8, inner), "whole"),
            (rim[:, inner:], (8, n2), "whole"),
            (raw, (CHUNK, LANES), dt_at),
            (marks, (CHUNK, LANES), "part"),
            (taps[:, :inner], (8, inner), "whole"),
            (taps[:, inner:], (8, n2), "whole"),
            (bias, (1, LANES), "whole"),
            (rate, (1, LANES), "whole"),
            (mats[0], mats[0].shape, "whole"),
        ],
        [
            (shape((length, inner)), (CHUNK, inner), "part"),
            (shape((length, inner), LOW), (CHUNK, inner), "part"),
            (shape((length, n2), LOW), (CHUNK, n2), "part"),
            (shape((length, n2), LOW), (CHUNK, n2), "part"),
            (shape((length, LANES)), (CHUNK, LANES), "part"),
            (shape((length, LANES)), (CHUNK, LANES), "part"),
            (shape((n2 // 2 + EXTRA, inner), LOW), (n2 // 2 + EXTRA, inner), "whole"),
            (shape((n2 // 2, inner)), (n2 // 2, inner), "whole"),
            (shape((8, inner)), (8, inner), "whole"),
        ],
        [],
    )


def mamba_mix(feats, raw, marks, docs, state, skip, gain, mats):
    act, slope, bcact, bcslope, step, cum = feats
    length, inner = act.shape
    parts = length // CHUNK
    n2 = bcact.shape[1]
    return call(
        mix_kernel,
        "mamba_mix",
        11,
        parts,
        [
            (act, (CHUNK, inner), "part"),
            (bcact, (CHUNK, n2), "part"),
            (raw, (CHUNK, inner), 0),
            (step, (CHUNK, LANES), "part"),
            (cum, (CHUNK, LANES), "part"),
            (marks, (CHUNK, LANES), "part"),
            (docs, (8, CHUNK), lambda c: (0, c)),
            (state, state.shape, "whole"),
            (skip, (1, inner), "whole"),
            (gain, (1, inner), "whole"),
            (mats[0], mats[0].shape, "whole"),
            (mats[1], mats[1].shape, "whole"),
        ],
        [
            (shape((length, inner), LOW), (CHUNK, inner), "part"),
            (shape((length, inner)), (CHUNK, inner), "part"),
            (shape((parts, n2 // 2, inner), LOW), (1, n2 // 2, inner), "part"),
        ],
        [pltpu.VMEM((n2 // 2, inner), jnp.float32), pltpu.VMEM((CHUNK, inner), jnp.float32)],
    )


def mamba_gate_back(d_normed, y, raw, feats, marks, gain, mats):
    act, slope, bcact, bcslope, step, cum = feats
    length, inner = act.shape
    parts = length // CHUNK
    n2 = bcact.shape[1]
    return call(
        gate_back_kernel,
        "mamba_gate_back",
        11,
        parts,
        [
            (d_normed, (CHUNK, inner), "part"),
            (y, (CHUNK, inner), "part"),
            (raw, (CHUNK, inner), 0),
            (bcact, (CHUNK, n2), "part"),
            (cum, (CHUNK, LANES), "part"),
            (marks, (CHUNK, LANES), "part"),
            (gain, (1, inner), "whole"),
            (mats[0], mats[0].shape, "whole"),
            (mats[1], mats[1].shape, "whole"),
        ],
        [
            (shape((length, inner), LOW), (CHUNK, inner), "part"),
            (shape((length, inner)), (CHUNK, inner), "part"),
            (shape((8, inner)), (8, inner), "whole"),
            (shape((n2 // 2 + EXTRA, inner), LOW), (n2 // 2 + EXTRA, inner), "whole"),
            (shape((n2 // 2, inner)), (n2 // 2, inner), "whole"),
            (shape((8, inner)), (8, inner), "whole"),
        ],
        [],
        reverse=True,
    )


def mamba_scan_back(feats, raw, rim, taps, marks, docs, dy, entry, state, skip, bias, rate, cols, mats):
    act, slope, bcact, bcslope, step, cum = feats
    length, inner = act.shape
    parts = length // CHUNK
    n2 = bcact.shape[1]
    x_at, bc_at, dt_at = cols[2:]
    scan = inner + n2

    def prev(column):
        return lambda c: (jnp.maximum(c * (CHUNK // 8) - 1, 0), column)

    return call(
        scan_back_kernel,
        "mamba_scan_back",
        23,
        parts,
        [
            (act, (CHUNK, inner), "part"),
            (slope, (CHUNK, inner), "part"),
            (bcact, (CHUNK, n2), "part"),
            (bcslope, (CHUNK, n2), "part"),
            (raw, (CHUNK, LANES), dt_at),
            (step, (CHUNK, LANES), "part"),
            (cum, (CHUNK, LANES), "part"),
            (marks, (CHUNK, LANES), "part"),
            (docs, (8, CHUNK), lambda c: (0, c)),
            (dy, (CHUNK, inner), "part"),
            (entry, (1, n2 // 2, inner), "part"),
            (state, state.shape, "whole"),
            (skip, (1, inner), "whole"),
            (bias, (1, LANES), "whole"),
            (rate, (1, LANES), "whole"),
            (mats[0], mats[0].shape, "whole"),
            (mats[1], mats[1].shape, "whole"),
            (raw, (CHUNK, inner), x_at),
            (raw, (8, inner), prev(x_at)),
            (raw, (CHUNK, n2), bc_at),
            (raw, (8, n2), prev(bc_at)),
            (rim[:, :inner], (8, inner), "whole"),
            (rim[:, inner:], (8, n2), "whole"),
            (taps[:, :inner], (8, inner), "whole"),
            (taps[:, inner:], (8, n2), "whole"),
        ],
        [
            (shape((length, scan + LANES), LOW), (CHUNK, scan + LANES), "part"),
            (shape((8, inner)), (8, inner), "whole"),
            (shape((8, LANES)), (8, LANES), "whole"),
            (shape((8, scan)), (8, scan), "whole"),
            (shape((8, scan)), (8, scan), "whole"),
            (shape((8, scan)), (8, scan), "whole"),
        ],
        [
            pltpu.VMEM((n2 // 2, inner), jnp.float32),
            pltpu.VMEM((CHUNK, inner), jnp.float32),
            pltpu.VMEM((LANES, CHUNK), jnp.float32),
            pltpu.VMEM((8, scan), jnp.float32),
            pltpu.VMEM((8, LANES), jnp.float32),
        ],
        reverse=True,
    )


def join(total, state, rows, got, ahead):
    whole = pl.BlockSpec(memory_space=pltpu.VMEM)
    return pl.pallas_call(
        join_kernel,
        in_specs=[pl.BlockSpec(memory_space=pltpu.SMEM)] + [whole] * 4,
        out_specs=[whole] * 4,
        out_shape=[shape(total.shape), shape(total.shape), shape(rows.shape), shape(got.shape, LOW)],
        compiler_params=pltpu.CompilerParams(vmem_limit_bytes=32 * 2**20),
        cost_estimate=guess(2),
        name="join",
    )(ahead, total, state, rows, got)


BOTH = 2
ONES = 16


def causal(scores):
    key_row = lax.broadcasted_iota(jnp.int32, scores.shape, 0)
    query = lax.broadcasted_iota(jnp.int32, scores.shape, 1)
    return jnp.where(key_row <= query, scores, FAR)


def attend_kernel(place_ref, q_ref, far_ref, kv_ref, extra_ref, o_ref, qb_ref, keys_ref, values_ref, acc_ref):
    blk = q_ref.shape[2]
    last = place_ref[0]

    @pl.when(pl.program_id(0) == 0)
    def _():
        first = lax.broadcasted_iota(jnp.int32, (blk, LANES), 1) < HEAD_SIZE

        @pl.loop(0, last + 1)
        def _(block):
            rows = pl.ds(pl.multiple_of(block * blk, blk), blk)
            both = kv_ref[rows, :]
            keys_ref[rows, :] = jnp.where(first, both, extra_ref[rows, :])
            values_ref[:ONES, rows] = jnp.ones((ONES, blk), LOW)
            values_ref[ONES:, rows] = both.astype(jnp.float32).T[HEAD_SIZE:].astype(LOW)

    queries = [
        jnp.concatenate([q_ref[i] * jnp.asarray(HEAD_SIZE ** (-0.5), LOW), far_ref[...]], axis=0)
        for i in range(BOTH)
    ]
    acc_ref[...] = jnp.zeros_like(acc_ref)

    def step(block, tops, diagonal):
        rows = pl.ds(pl.multiple_of(block * blk, blk), blk)
        keys, values = keys_ref[rows, :], values_ref[:, rows]
        new_tops = []
        for i in range(BOTH):
            scores = nn(keys, queries[i])
            if diagonal:
                scores = causal(scores)
            new_top = jnp.maximum(tops[i], jnp.max(scores, axis=0, keepdims=True))
            probs = jnp.exp(scores - new_top).astype(LOW)
            acc_ref[i] = acc_ref[i] * jnp.exp(tops[i] - new_top) + nn(values, probs)
            new_tops.append(new_top)
        return tuple(new_tops)

    tops = (jnp.full((1, blk), FAR, jnp.float32),) * BOTH
    tops = lax.fori_loop(0, last, lambda block, tops: step(block, tops, False), tops)
    tops = step(last, tops, True)
    row = lax.broadcasted_iota(jnp.int32, (HEAD_SIZE, blk), 0)
    for i in range(BOTH):
        total = acc_ref[i, 0:1, :]
        o_ref[i] = acc_ref[i, ONES:, :] / total
        extra = far_ref[...].astype(jnp.float32)
        for at, term in enumerate(split_low(-(tops[i] + jnp.log(total)), 3)):
            extra = jnp.where(row == 4 + at, term.astype(jnp.float32), extra)
        qb_ref[i] = jnp.concatenate([queries[i][:HEAD_SIZE], extra.astype(LOW)], axis=0)


def attend_back_kernel(place_ref, qb_ref, dot_ref, o_ref, kv_ref, extra_ref, dq_ref, dkv_ref, keys_ref, rows_ref, values_ref, acc_ref, dqa_ref):
    blk = qb_ref.shape[2]
    last = place_ref[0]
    member = pl.program_id(0)

    @pl.when(member == 0)
    def _():
        acc_ref[...] = jnp.zeros_like(acc_ref)
        lane = lax.broadcasted_iota(jnp.int32, (blk, LANES), 1)
        ones = jnp.where(lane < 3, 1.0, 0.0).astype(LOW)

        @pl.loop(0, last + 1)
        def _(block):
            rows = pl.ds(pl.multiple_of(block * blk, blk), blk)
            both = kv_ref[rows, :]
            keys_ref[rows, :] = jnp.where(lane < HEAD_SIZE, both, extra_ref[rows, :])
            values_ref[rows, :] = jnp.where(lane < HEAD_SIZE, ones, both)
            rows_ref[:, rows] = both.astype(jnp.float32).T[:HEAD_SIZE].astype(LOW)

    row = lax.broadcasted_iota(jnp.int32, (HEAD_SIZE, blk), 0)
    none = jnp.zeros((HEAD_SIZE, blk), jnp.float32)
    queries, d_outs, pairs = [], [], []
    for i in range(BOTH):
        queries.append(qb_ref[i])
        d_out = dot_ref[i].astype(jnp.float32)
        row_dot = jnp.sum(d_out * o_ref[i], axis=0, keepdims=True)
        extra = none
        for at, term in enumerate(split_low(-row_dot, 3)):
            extra = jnp.where(row == at, term.astype(jnp.float32), extra)
        d_outs.append(jnp.concatenate([extra, d_out], axis=0).astype(LOW))
        q_part = jnp.concatenate([qb_ref[i, :HEAD_SIZE, :].astype(jnp.float32), none], axis=0)
        pairs.append(jnp.concatenate([q_part.T, jnp.concatenate([none, d_out], axis=0).T], axis=0).astype(LOW))
    dqa_ref[...] = jnp.zeros_like(dqa_ref)

    def step(block, diagonal):
        rows = pl.ds(pl.multiple_of(block * blk, blk), blk)
        keys, values, key_rows = keys_ref[rows, :], values_ref[rows, :], rows_ref[:, rows]
        total = acc_ref[rows, :]
        for i in range(BOTH):
            logs = nn(keys, queries[i])
            if diagonal:
                logs = causal(logs)
            probs = jnp.exp(logs)
            d_scores = (probs * nn(values, d_outs[i])).astype(LOW)
            total = total + nn(jnp.concatenate([d_scores, probs.astype(LOW)], axis=1), pairs[i])
            dqa_ref[i] += nn(key_rows, d_scores)
        acc_ref[rows, :] = total

    @pl.loop(0, last)
    def _(block):
        step(block, False)

    step(last, True)
    dq_ref[...] = (dqa_ref[...] * HEAD_SIZE ** (-0.5)).astype(LOW)

    @pl.when(member == GROUP // BOTH - 1)
    def _():
        dkv_ref[...] = acc_ref[...].astype(LOW)


def attend_back_more(place_ref, qb_ref, dot_ref, o_ref, kv_ref, extra_ref, _, *refs):
    attend_back_kernel(place_ref, qb_ref, dot_ref, o_ref, kv_ref, extra_ref, *refs)


def attend_specs(blk, total, group):
    mine = group * (GROUP // BOTH)
    return dict(
        narrow=pl.BlockSpec((BOTH, HEAD_SIZE, blk), lambda r, p: (mine + r, 0, 0)),
        own_narrow=pl.BlockSpec((BOTH, HEAD_SIZE, blk), lambda r, p: (r, 0, 0)),
        own_broad=pl.BlockSpec((BOTH, LANES, blk), lambda r, p: (r, 0, 0)),
        kv=pl.BlockSpec((total, LANES), lambda r, p: (0, group)),
        extra=pl.BlockSpec((total, LANES), lambda r, p: (0, 0)),
        far=pl.BlockSpec((HEAD_SIZE, blk), lambda r, p: (0, 0)),
    )


def attend_masks(doc_here, key_doc, doc_count):
    docs = jnp.arange(HEAD_SIZE, dtype=jnp.int32)
    far = jnp.where((docs[:, None] != doc_here[None, :]) & (docs[:, None] < doc_count), FAR, 0.0).astype(LOW)
    lane = jnp.arange(LANES, dtype=jnp.int32)[None, :] - HEAD_SIZE
    extra = ((key_doc[:, None] == lane) | ((lane >= doc_count) & (lane < doc_count + 3))).astype(LOW)
    return far, extra


def attend(group, q_rows, key_all, masks, place):
    blk = q_rows.shape[2]
    total = key_all.shape[0]
    specs = attend_specs(blk, total, group)
    return pl.pallas_call(
        attend_kernel,
        grid_spec=pltpu.PrefetchScalarGridSpec(
            num_scalar_prefetch=1,
            grid=(GROUP // BOTH,),
            in_specs=[specs["narrow"], specs["far"], specs["kv"], specs["extra"]],
            out_specs=[specs["own_narrow"], specs["own_broad"]],
            scratch_shapes=[
                pltpu.VMEM((total, LANES), LOW),
                pltpu.VMEM((HEAD_SIZE + ONES, total), LOW),
                pltpu.VMEM((BOTH, HEAD_SIZE + ONES, blk), jnp.float32),
            ],
        ),
        out_shape=[shape((GROUP, HEAD_SIZE, blk)), shape((GROUP, LANES, blk), LOW)],
        compiler_params=pltpu.CompilerParams(vmem_limit_bytes=56 * 2**20),
        cost_estimate=guess(17),
        name="attend",
    )(place, q_rows, masks[0], key_all, masks[1])


def attend_back(group, q_back, out, d_rows, key_all, masks, place, d_kv=None):
    blk = d_rows.shape[2]
    total = key_all.shape[0]
    specs = attend_specs(blk, total, group)
    more = [] if d_kv is None else [d_kv]
    return pl.pallas_call(
        attend_back_kernel if d_kv is None else attend_back_more,
        grid_spec=pltpu.PrefetchScalarGridSpec(
            num_scalar_prefetch=1,
            grid=(GROUP // BOTH,),
            in_specs=[specs["own_broad"], specs["narrow"], specs["own_narrow"], specs["kv"], specs["extra"]]
            + [pl.BlockSpec(memory_space=pl.ANY)] * len(more),
            out_specs=[specs["own_narrow"], specs["kv"]],
            scratch_shapes=[
                pltpu.VMEM((total, LANES), LOW),
                pltpu.VMEM((HEAD_SIZE, total), LOW),
                pltpu.VMEM((total, LANES), LOW),
                pltpu.VMEM((total, LANES), jnp.float32),
                pltpu.VMEM((BOTH, HEAD_SIZE, blk), jnp.float32),
            ],
        ),
        out_shape=[shape((GROUP, HEAD_SIZE, blk), LOW), shape((total, key_all.shape[1]), LOW)],
        input_output_aliases={6: 1} if more else {},
        compiler_params=pltpu.CompilerParams(vmem_limit_bytes=60 * 2**20),
        cost_estimate=guess(27),
        name="attend_back",
    )(place, q_back, d_rows, out, key_all, masks[1], *more)


PIECE = 256


def feed_kernel(x_ref, gy_ref, plain_ref, w_ref, out_ref, dx_ref, grad_ref, xt_ref):
    fold = w_ref.shape[1] // 3

    @pl.when(pl.program_id(0) == 0)
    def _():
        out_ref[...] = jnp.zeros_like(out_ref)
        dx_ref[...] = jnp.zeros_like(dx_ref)
        xt_ref[...] = x_ref[...].astype(jnp.float32).T.astype(LOW)

    @pl.loop(0, fold // PIECE)
    def _(piece):
        at = pl.multiple_of(piece * PIECE, PIECE)
        gate_cols = pl.ds(at, PIECE)
        up_cols = pl.ds(pl.multiple_of(fold + at, PIECE), PIECE)
        down_cols = pl.ds(2 * fold, fold)
        w_gate, w_up, w_down = w_ref[:, gate_cols], w_ref[:, up_cols], w_ref[gate_cols, down_cols]
        x, gy = x_ref[...], gy_ref[...]
        gate, up = nn(x, w_gate), nn(x, w_up)
        sigma = jax.nn.sigmoid(gate)
        silu = gate * sigma
        act = silu * up
        d_act = nt(gy, w_down)
        d_gate = (d_act * up * sigma * (1.0 + gate * (1.0 - sigma))).astype(LOW)
        d_up = (d_act * silu).astype(LOW)
        out_ref[...] += nn(act.astype(LOW), w_down)
        dx_ref[...] += nt(d_gate, w_gate) + nt(d_up, w_up)
        x_t = xt_ref[...]
        grad_ref[:, gate_cols] = nn(x_t, d_gate).astype(LOW)
        grad_ref[:, up_cols] = nn(x_t, d_up).astype(LOW)
        grad_ref[gate_cols, down_cols] = nn(act.T.astype(LOW), plain_ref[...]).astype(LOW)


def feed_forward(x, gy, plain, w, folds, fold):
    tokens, width = x.shape
    whole = pl.BlockSpec((tokens, width), lambda j: (0, 0))
    return pl.pallas_call(
        feed_kernel,
        grid=(folds,),
        in_specs=[whole, whole, whole, pl.BlockSpec((width, 3 * fold), lambda j: (0, j))],
        out_specs=[whole, whole, pl.BlockSpec((width, 3 * fold), lambda j: (0, j))],
        out_shape=[
            shape((tokens, width)),
            shape((tokens, width)),
            shape((width, 3 * fold * folds), LOW),
        ],
        scratch_shapes=[pltpu.VMEM((width, tokens), LOW)],
        compiler_params=pltpu.CompilerParams(vmem_limit_bytes=60 * 2**20),
        cost_estimate=guess(35),
        name="feed_forward",
    )(x, gy, plain, w)


def last_grads_kernel(x_ref, scan_ref, query_ref, kv_ref, small_ref, grad_ref):
    x_t = x_ref[...].astype(jnp.float32).T.astype(LOW)
    scan = scan_ref.shape[1]
    query = query_ref.shape[1]
    grad_ref[:, : scan - LANES] = nn(x_t, scan_ref[:, : scan - LANES]).astype(LOW)
    grad_ref[:, scan - LANES : scan] = (nn(x_t, scan_ref[:, scan - LANES :]) + small_ref[...]).astype(LOW)
    grad_ref[:, scan : scan + query] = nn(x_t, query_ref[...]).astype(LOW)
    grad_ref[:, scan + query :] = nn(x_t, kv_ref[...]).astype(LOW)


def last_grads(x, d_scan, d_query, d_kv, small):
    tokens, width = x.shape
    count = d_scan.shape[1] + d_query.shape[1] + d_kv.shape[1]
    return pl.pallas_call(
        last_grads_kernel,
        out_shape=shape((width, count), LOW),
        compiler_params=pltpu.CompilerParams(vmem_limit_bytes=56 * 2**20),
        cost_estimate=guess(8),
        name="last_grads",
    )(x, d_scan, d_query, d_kv, small)


def tap_marks(starts, first, length, taps):
    ext = doc_index(starts, first - (taps - 1) + jnp.arange(length + taps - 1, dtype=jnp.int32))
    return jnp.stack([(ext[i : i + length] == ext[taps - 1 :]).astype(jnp.float32) for i in range(taps)], axis=1)


def marks_of(starts, block_base, length, taps):
    ext = doc_index(starts, block_base - (taps - 1) + jnp.arange(length + taps - 1, dtype=jnp.int32))
    here = ext[taps - 1 :]
    chunks = here.reshape(-1, CHUNK)
    ahead = ext[taps - 2 : taps - 2 + length].reshape(-1, CHUNK)[:, :1]
    last = chunks[:, -1:]
    columns = [ext[i : i + length] == here for i in range(taps)] + [
        (chunks == ahead).reshape(-1),
        (chunks == last).reshape(-1),
        here,
        jnp.broadcast_to(last == ahead, chunks.shape).reshape(-1),
    ]
    marks = jnp.stack([column.astype(jnp.float32) for column in columns], axis=1)
    marks = jnp.pad(marks, ((0, 0), (0, LANES - len(columns))))
    return marks, jnp.broadcast_to(here.astype(jnp.float32)[None], (8, length)), here


def per_device(
    hidden_in,
    cotangent,
    doc_starts,
    gain_in,
    mamba_gate_w,
    mamba_in_w,
    mamba_bc_w,
    mamba_dt_w,
    dt_bias,
    a_log,
    d_skip,
    conv_x,
    conv_bc,
    mamba_gain,
    attn_q_w,
    attention_key_value_weight,
    mamba_out_w,
    attn_out_w,
    gain_ffn,
    ffn_gate_w,
    ffn_up_w,
    ffn_down_w,
):
    devices = lax.axis_size("head") * lax.axis_size("wide")
    wide_id = lax.axis_index("wide")
    micro_count = hidden_in.shape[0]
    block_tok = hidden_in.shape[2] * lax.axis_size("head")
    taps = conv_x.shape[0]
    heads = dt_bias.shape[0]
    rows, inner = mamba_gate_w.shape
    width = rows * devices
    bc_cols = mamba_bc_w.shape[1]
    query_cols = attn_q_w.shape[1]
    kv_cols = attention_key_value_weight.shape[1]
    hidden = ffn_gate_w.shape[1]
    out_rows = mamba_out_w.shape[0]
    attn_rows = attn_out_w.shape[0]
    chan = conv_x.shape[1]
    chan_bc = conv_bc.shape[1]

    scan_cols = inner + bc_cols
    first_cols = scan_cols + LANES

    heads_dev, wide_dev = lax.axis_size("head"), lax.axis_size("wide")
    folds = hidden // width
    feature = jnp.arange(width, dtype=jnp.int32)
    inside = (feature // rows) % wide_dev * heads_dev + feature // (rows * wide_dev)
    order = (inside[:, None] * rows + (feature % rows)[:, None] == feature[None, :]).astype(LOW)

    def mixed(array):
        return nn(array.reshape(-1, width), order).astype(LOW).reshape(array.shape)

    def plain(array):
        return nt(array.reshape(-1, width), order).astype(LOW).reshape(array.shape)

    def by_place(array):
        return array.reshape((heads_dev, wide_dev) + array.shape[1:]).swapaxes(0, 1).reshape(array.shape)

    def by_owner(array):
        return array.reshape((wide_dev, heads_dev) + array.shape[1:]).swapaxes(0, 1).reshape(array.shape)

    def folded(weight):
        return weight.reshape(rows, heads_dev, wide_dev, folds, rows).transpose(0, 3, 2, 1, 4).reshape(rows, folds, width)

    def unfolded(parts):
        unit = jnp.arange(hidden, dtype=jnp.int32)
        owner, fold, row = unit // (folds * rows), unit // rows % folds, unit % rows
        at = (owner % wide_dev * heads_dev + owner // wide_dev) * rows + row
        total = 0.0
        for i, part in enumerate(parts):
            one_hot = ((feature[:, None] == at[None, :]) & (fold == i)[None, :]).astype(LOW)
            total = total + nn(jnp.concatenate(split_low(part, 3), axis=0), one_hot)
        high, middle, low = split_at(total, (rows,) * 3, 0)
        return high + (middle + low)

    small = packed([gain_in, gain_ffn, mamba_gain, conv_x, conv_bc], rows)
    small_cols = small.shape[1]
    pad = jnp.zeros((rows, LANES - heads - small_cols), LOW)
    in_shard = jnp.concatenate(
        [mamba_in_w, mamba_bc_w, mamba_dt_w, small, pad, mamba_gate_w, attn_q_w, attention_key_value_weight], axis=1
    )
    in_rows = gather_head(in_shard, micro_count)
    w_in = lax.all_gather(in_rows, "wide", axis=0, tiled=True)
    x_low = to_blocks(after(mixed(hidden_in[:, 0]), in_rows))
    gy_pieces = cotangent[:, 0]
    to_width = mixed(jnp.concatenate([ffn_down_w, mamba_out_w, attn_out_w], axis=0)).reshape(-1, rows, width)
    gate_folds, up_folds = folded(ffn_gate_w), folded(ffn_up_w)
    late_parts = []
    for i in range(folds):
        late_parts += [gate_folds[:, i], up_folds[:, i], to_width[i]]
    late_parts += [to_width[i] for i in range(folds, to_width.shape[0])]
    late_shard = after(jnp.concatenate(late_parts, axis=1), x_low)
    micro = jnp.minimum(lax.axis_index("head"), micro_count - 1)
    starts = pick(doc_starts, micro)
    block_base = wide_id * block_tok
    marks, docs_row, doc_here = marks_of(starts, block_base, block_tok, taps)
    key_doc = doc_index(starts, jnp.arange(block_tok * lax.axis_size("wide"), dtype=jnp.int32))
    masks = attend_masks(doc_here, key_doc, doc_starts.shape[1])
    mats = head_matrices(inner, heads)
    bias_row = lanes_row(dt_bias)
    rate_row = lanes_row(-jnp.exp(a_log))
    skip_row = jnp.repeat(d_skip, inner // heads)[None]
    x_low, marks, docs_row, masks, mats, bias_row, rate_row, skip_row = lax.optimization_barrier(
        (x_low, marks, docs_row, masks, mats, bias_row, rate_row, skip_row)
    )
    x_tokens = x_low.astype(jnp.float32)

    small_at = scan_cols + heads
    w_scan, w_gate, w_qkv = split_at(w_in, (first_cols, inner, query_cols + kv_cols), 1)
    small_all = w_scan[:, small_at : small_at + small_cols].reshape(devices, -1).astype(jnp.float32)
    g_in, g_ffn, g_mamba, c_x, c_bc = split_at(
        small_all, (rows, rows, chan, taps * chan, taps * chan_bc), 1
    )
    gain_in_all = g_in.reshape(-1)
    gain_ffn_all = g_ffn.reshape(-1)
    g_mamba, c_x, c_bc = by_owner(g_mamba), by_owner(c_x), by_owner(c_bc)
    gain_mamba_row = g_mamba.reshape(1, -1)
    taps_all = jnp.concatenate(
        [
            c_x.reshape(devices, taps, chan).transpose(1, 0, 2).reshape(taps, -1),
            c_bc.reshape(devices, taps, chan_bc).transpose(1, 0, 2).reshape(taps, -1),
        ],
        axis=1,
    )
    cols = (inner, bc_cols, 0, inner // bc_cols, scan_cols // LANES)
    place = jnp.reshape(wide_id, (1,)).astype(jnp.int32)


    normed_in, pull_in = jax.vjp(rms_scale, x_tokens, gain_in_all)
    block_in = normed_in.astype(LOW)
    raw_qkv = nn(block_in, w_qkv).astype(LOW)
    keys = Gathered(raw_qkv[:, query_cols:])
    raw_scan = nn(after(block_in, raw_qkv), w_scan)
    rim = shifted(raw_scan[block_tok - 8 :, :scan_cols], "wide", 1)
    rim = jnp.where(jnp.arange(8)[:, None] > 8 - taps, rim, 0.0)
    raw_gate = nn(after(block_in, raw_scan), w_gate)
    keys.step()
    taps_ext = jnp.pad(taps_all, ((0, 8 - taps), (0, 0)))
    *feats, sent, total, decay_rows = mamba_local(
        raw_scan, after(rim, *keys.parts), marks, taps_ext, bias_row, rate_row, cols, mats
    )
    late_rows = gather_head(late_shard, micro_count, (sent,))
    w_late = lax.all_gather(late_rows, "wide", axis=0, tiled=True)
    q_rows = raw_qkv[:, :query_cols].T.reshape(QUERY_HEADS, HEAD_SIZE, block_tok)
    key_all = keys.rest()
    forward = Carried(sent, total, decay_rows, False)
    forward.step()
    out_0, q_back_0 = attend(0, after(q_rows, forward.sent), key_all, masks, place)
    forward.step(out_0)
    out_1, q_back_1 = attend(1, after(q_rows, forward.sent, out_0), key_all, masks, place)
    attn_low = jnp.concatenate([out_0, out_1], axis=0).reshape(query_cols, block_tok).astype(LOW)
    mamba_low, y_low, entry = mamba_mix(
        feats, raw_gate, marks, docs_row, forward.rest(out_1), skip_row, gain_mamba_row, mats
    )
    gy_plain = to_blocks(after(gy_pieces, raw_scan), (out_0,))
    d_out_low = mixed(gy_plain)
    out_at = 3 * hidden
    out_both = jnp.concatenate(
        [w_late[:, i : i + width].reshape(devices, rows, width) for i in range(out_at, w_late.shape[1], width)], axis=1
    )
    out_both = by_owner(out_both)
    w_mamba_out = out_both[:, :out_rows].reshape(-1, width)
    w_attn_out = out_both[:, out_rows:].reshape(-1, width)

    resid = x_tokens + nn(mamba_low, w_mamba_out) + tn(attn_low, w_attn_out)
    normed_ffn, pull_ffn = jax.vjp(rms_scale, resid, gain_ffn_all)
    ffn_in = normed_ffn.astype(LOW)
    fed, d_ffn_in, grad_ffn = feed_forward(ffn_in, d_out_low, gy_plain, w_late, folds, width)
    part_ffn = sum_wide(grad_ffn)
    d_resid_norm, grad_gain_ffn = pull_ffn(d_ffn_in)
    d_resid = d_out_low.astype(jnp.float32) + d_resid_norm

    d_mix = d_resid.astype(LOW)
    d_gate_z, dy_low, grad_gain_m, sent_back, total, decay_rows = mamba_gate_back(
        nt(d_mix, w_mamba_out), y_low, raw_gate, feats, marks, gain_mamba_row, mats
    )
    backward = Carried(sent_back, total, decay_rows, True)
    backward.step()
    d_attn = nt(w_attn_out, after(d_mix, backward.sent)).astype(LOW).reshape(QUERY_HEADS, HEAD_SIZE, block_tok)
    d_query_0, d_kv_0 = attend_back(0, q_back_0, out_0, d_attn, key_all, masks, place)
    backward.step(d_query_0)
    d_query_1, d_kv_all = attend_back(
        1, q_back_1, out_1, after(d_attn, backward.sent, d_kv_0), key_all, masks, place, d_kv_0
    )
    d_kv_sum = Reduced(d_kv_all.reshape(-1, 2, block_tok // 2, kv_cols).swapaxes(0, 1))
    d_kv_sent = d_kv_sum.begin()
    d_query = jnp.concatenate([d_query_0, d_query_1], axis=0).reshape(query_cols, block_tok).T
    d_mix_plain = plain(after(d_mix, *d_kv_sent))
    grad_out = jnp.concatenate(
        [
            tn(mamba_low, d_mix_plain).astype(LOW).reshape(devices, out_rows, width),
            nn(attn_low, d_mix_plain).astype(LOW).reshape(devices, attn_rows, width),
        ],
        axis=1,
    ).reshape(devices, -1, rows, width)
    grad_out = by_place(grad_out)
    grad_gate = tn(after(block_in, *d_kv_sent), d_gate_z).astype(LOW)
    early = jnp.concatenate(
        [grad_out[:, i].reshape(width, width) for i in range(grad_out.shape[1])] + [grad_gate], axis=1
    )
    d_kv_sum.end(early)
    d_kv_sent = d_kv_sum.begin()
    part_early = sum_wide(after(early, part_ffn))
    d_state = backward.rest(early)
    d_scan, grad_skip, grad_head, grad_taps, rim_back, edge = mamba_scan_back(
        feats, raw_scan, rim, taps_ext, marks, docs_row, dy_low, entry, after(d_state, part_ffn, *d_kv_sent),
        skip_row, bias_row, rate_row, cols, mats,
    )
    d_kv_sum.end(d_scan)
    own_ffn = owned(part_ffn, micro_count, (d_scan,))
    d_kv = d_kv_sum.rest().reshape(block_tok, kv_cols)
    rim_came = shifted(rim_back, "wide", -1)
    d_scan = lax.dynamic_update_slice(d_scan, (edge + rim_came).astype(LOW), (block_tok - 8, 0))
    grad_small = jnp.concatenate(
        [
            jnp.zeros((devices, rows), jnp.float32),
            grad_gain_ffn.reshape(devices, rows),
            by_place(grad_gain_m[0].reshape(devices, chan)),
            by_place(grad_taps[:taps, :inner].reshape(taps, devices, chan).transpose(1, 0, 2).reshape(devices, -1)),
            by_place(grad_taps[:taps, inner:].reshape(taps, devices, chan_bc).transpose(1, 0, 2).reshape(devices, -1)),
        ],
        axis=1,
    )
    grad_small = jnp.pad(grad_small, ((0, 0), (0, rows * small_cols - grad_small.shape[1])))
    grad_small = jnp.pad(
        grad_small.reshape(width, small_cols), ((0, 0), (heads, LANES - heads - small_cols))
    )
    late = last_grads(after(block_in, own_ffn), d_scan, d_query, d_kv, grad_small)

    d_late = after(jnp.concatenate([d_query, d_kv], axis=1), late)
    d_x_norm, grad_gain_in = pull_in(nt(d_gate_z, w_gate) + nt(d_late, w_qkv) + nt(d_scan, w_scan))
    grad_x = (d_resid + d_x_norm).astype(LOW)
    part_late = sum_wide(after(late, part_early))
    own_early = owned(after(part_early, late), micro_count, (grad_x,))
    results = from_blocks(
        jnp.concatenate([plain((resid + fed).astype(LOW)), plain(grad_x)], axis=1), micro_count
    )
    summed = sum_everywhere(
        jnp.concatenate(
            [grad_head[:2, :heads].reshape(-1), jnp.sum(grad_skip[0].reshape(heads, -1), axis=1), grad_gain_in]
        )
    )
    per_head = summed[: 3 * heads].reshape(3, heads)
    inside_place = wide_id * heads_dev + lax.axis_index("head")
    o_gain_in = lax.dynamic_slice_in_dim(summed[3 * heads :], inside_place * rows, rows)
    own_late = owned(part_late, micro_count)

    g_x, g_bc, g_dt, g_small, _, g_q, g_kv = split_at(
        own_late, (inner, bc_cols, heads, small_cols, LANES - heads - small_cols, query_cols, kv_cols), 1
    )
    *g_out, g_gate = split_at(own_early, (width,) * ((out_rows + attn_rows) // rows) + (inner,), 1)
    _, o_gain_ffn, o_gain_m, o_conv_x, o_conv_bc = split_at(
        g_small.reshape(-1), (rows, rows, chan, taps * chan, taps * chan_bc), 0
    )
    g_mamba_out, g_attn_out = split_at(jnp.concatenate(g_out, axis=0), (out_rows, attn_rows), 0)
    g_ffn = split_at(own_ffn, (width,) * (3 * folds), 1)
    return (
        results[:, None, :, :width],
        results[:, None, :, width:],
        o_gain_in,
        g_gate,
        g_x,
        g_bc,
        g_dt,
        per_head[0],
        per_head[1],
        per_head[2],
        o_conv_x.reshape(taps, chan),
        o_conv_bc.reshape(taps, chan_bc),
        o_gain_m,
        g_q,
        g_kv,
        g_mamba_out,
        g_attn_out,
        o_gain_ffn,
        unfolded(g_ffn[0::3]),
        unfolded(g_ffn[1::3]),
        jnp.concatenate(g_ffn[2::3], axis=0),
    )


def solution(mesh):
    tokens = P(None, "wide", "head", None)
    matrix = P(ALL, None)
    vector = P(ALL)
    taps = P(None, ALL)
    in_specs = (
        (tokens, tokens, P(), vector)
        + (matrix,) * 4
        + (P(),) * 3
        + (taps, taps, vector)
        + (matrix,) * 4
        + (vector,)
        + (matrix,) * 3
    )
    out_specs = (
        (tokens, tokens, vector)
        + (matrix,) * 4
        + (P(),) * 3
        + (taps, taps, vector)
        + (matrix,) * 4
        + (vector,)
        + (matrix,) * 3
    )
    return jax.shard_map(
        per_device, mesh=mesh, in_specs=in_specs, out_specs=out_specs, check_vma=False
    )
```

```python
from functools import partial

import jax
import jax.numpy as jnp
from jax import lax
from jax.experimental import pallas as pl
from jax.experimental.pallas import tpu as pltpu
from jax.sharding import PartitionSpec as P

QUERY_HEADS = 8
KEY_VALUE_HEADS = 2
HEAD_SIZE = 64
GROUP = QUERY_HEADS // KEY_VALUE_HEADS
LANES = 128
LOW = jnp.bfloat16
FAR = -1e30
ALL = ("head", "wide")

epsilon = 1e-05
highest = lax.Precision.HIGHEST


def nn(left, right):
    return jnp.dot(left, right, preferred_element_type=jnp.float32)


def nt(left, right):
    return lax.dot_general(left, right, (((1,), (1,)), ((), ())), preferred_element_type=jnp.float32)


def tn(left, right):
    return lax.dot_general(left, right, (((0,), (0,)), ((), ())), preferred_element_type=jnp.float32)


def split_low(value, parts):
    terms = []
    for _ in range(parts):
        term = value.astype(LOW)
        terms.append(term)
        value = value - term.astype(jnp.float32)
    return terms


def shape(dims, kind=jnp.float32):
    return jax.ShapeDtypeStruct(dims, kind)


def shifted(value, axis, steps):
    count = lax.axis_size(axis)
    initial, last = (max(0, -steps), min(count, count - steps))
    return lax.ppermute(value, axis, [(source, source + steps) for source in range(initial, last)])


def swapped(value, axis, bit):
    count = lax.axis_size(axis)
    return lax.ppermute(value, axis, [(i, i ^ bit) for i in range(count)])


def pick(array, index, axis=0):
    return lax.dynamic_index_in_dim(array, index, axis, False)


def guess(us):
    return pl.CostEstimate(flops=int(us * 1e9), bytes_accessed=int(us * 3e6), transcendentals=0)


def tied(*values):
    return lax.optimization_barrier(values)


def sent_on(pieces, sources, receivers):
    count = lax.axis_size("head")
    place = lax.axis_index("head")
    got = []
    for step in range(1, count):
        pairs = [(i, (i + step) % count) for i in range(count)]
        pairs = [(i, k) for i, k in pairs if i < sources and k < receivers]
        got.append(lax.ppermute(pieces((place + step) % count), "head", pairs))
    return got


def put_together(own, got):
    place = lax.axis_index("head")
    count = len(got) + 1
    whole = lax.dynamic_update_index_in_dim(jnp.zeros((count,) + own.shape, own.dtype), own, place, 0)
    for step, array in enumerate(got, 1):
        whole = lax.dynamic_update_index_in_dim(whole, array, (place - step) % count, 0)
    return whole


class HeadRows:
    def __init__(self, own, receivers):
        self.own = own
        self.got = sent_on(lambda target: own, lax.axis_size("head"), receivers)

    def end(self):
        return put_together(self.own, self.got).reshape(-1, self.own.shape[1])


class ToBlocks:
    def __init__(self, pieces):
        micro_count = pieces.shape[0]
        place = lax.axis_index("head")

        def of(target):
            return pick(pieces, jnp.minimum(target, micro_count - 1))

        self.own = jnp.where(place < micro_count, of(place), jnp.zeros_like(pieces[0]))
        self.got = sent_on(of, lax.axis_size("head"), micro_count)

    def end(self):
        return put_together(self.own, self.got).reshape(-1, self.own.shape[1])


class FromBlocks:
    def __init__(self, block, micro_count):
        count = lax.axis_size("head")
        parts = block.reshape(count, block.shape[0] // count, block.shape[1])
        self.micro_count = micro_count
        self.own = pick(parts, lax.axis_index("head"))
        self.got = sent_on(lambda target: pick(parts, target), micro_count, count)

    def end(self):
        return put_together(self.own, self.got)[: self.micro_count]


class HeadSum:
    def __init__(self, part, sources, block=None):
        count = lax.axis_size("head")
        place = lax.axis_index("head")
        array = part.reshape(count, -1, part.shape[1])
        self.width = array.shape[2]
        self.sources = sources
        if block is not None:
            self.block_shape = (block.shape[0] // count, block.shape[1])
            array = jnp.concatenate([array, block.reshape(count, array.shape[1], -1)], axis=2)
        self.own = pick(array, place)
        self.got = sent_on(lambda target: pick(array, target), sources, count)

    def end(self, sizes=None):
        place = lax.axis_index("head")
        at, out = 0, []
        for size in sizes or (self.width,):
            cut = [array[:, at : at + size].astype(jnp.float32) for array in [self.own] + self.got]
            total = jnp.where(place < self.sources, cut[0], 0.0)
            for term in cut[1:]:
                total = total + term
            out.append(total)
            at += size
        return out if sizes else out[0]

    def end_block(self):
        own, got = self.own[:, self.width :], [array[:, self.width :] for array in self.got]
        whole = put_together(own, got)
        return whole.reshape((whole.shape[0],) + self.block_shape)[: self.sources]


def wide_bits():
    bits = []
    while 1 << (len(bits) + 1) <= lax.axis_size("wide"):
        bits.append(1 << len(bits))
    return bits


class EverySum:
    def __init__(self, value):
        self.value = value
        self.left = [("wide", bit) for bit in wide_bits()]
        bit = 1
        while bit < lax.axis_size("head"):
            self.left.append(("head", bit))
            bit *= 2

    def begin(self):
        self.got = swapped(self.value, *self.left.pop(0))

    def end(self):
        self.value = self.value + self.got

    def rest(self):
        while self.left:
            self.begin()
            self.end()
        return self.value


class Gathered:
    def __init__(self, own):
        bits = wide_bits()
        half = own.shape[1] // 2
        self.parts = [own[:, :half], own[:, half:]]
        self.left = [bits[1:], bits[:0:-1]]
        self.done = [[], []]

    def begin(self):
        self.got = [swapped(array, "wide", left[0]) for array, left in zip(self.parts, self.left)]

    def end(self):
        place = lax.axis_index("wide")
        for i, got in enumerate(self.got):
            bit = self.left[i].pop(0)
            mine = (place // bit) % 2
            array = self.parts[i]
            self.parts[i] = jnp.where(mine == 0, jnp.stack([array, got]), jnp.stack([got, array]))
            self.done[i].insert(0, bit)

    def rest(self):
        while self.left[0]:
            self.begin()
            self.end()
        arrays = []
        for array, done in zip(self.parts, self.done):
            ranks = [done.index(bit) for bit in sorted(done, reverse=True)]
            arrays.append(array.transpose(ranks + [len(done), len(done) + 1]))
        both = jnp.concatenate(arrays, axis=-1)
        got = swapped(both, "wide", 1)
        mine = lax.axis_index("wide") % 2
        stacked = jnp.where(mine == 0, jnp.stack([both, got], axis=-3), jnp.stack([got, both], axis=-3))
        return stacked.reshape(-1, both.shape[-1])


class CoreSum:
    def __init__(self, part):
        count = lax.axis_size("wide")
        mine = lax.axis_index("wide") % 2
        part = part.reshape(count // 2, 2, -1, part.shape[1])
        self.own = pick(part, mine, 1)
        self.got = swapped(pick(part, 1 - mine, 1), "wide", 1)

    def end(self):
        return (self.own.astype(jnp.float32) + self.got.astype(jnp.float32)).astype(self.own.dtype)


class ChipSum:
    def __init__(self, array):
        chip = lax.axis_index("wide") // 2
        self.own = pick(array, chip)
        self.got = [swapped(pick(array, chip ^ other), "wide", 2 * other) for other in range(1, array.shape[0])]

    def end(self):
        total = self.own.astype(jnp.float32)
        for array in self.got:
            total = total + array.astype(jnp.float32)
        return total.astype(self.own.dtype)


def sum_wide(array):
    return lax.psum_scatter(array, "wide", scatter_dimension=0, tiled=True)


def gather_wide(array):
    return lax.all_gather(array, "wide", axis=0, tiled=True)


class Carried:
    def __init__(self, sent, total, rows, backward):
        self.sent, self.total, self.rows = sent, total, rows
        self.state = jnp.zeros_like(total)
        self.backward = backward
        self.left = wide_bits()

    def begin(self):
        self.got = swapped(self.sent, "wide", self.left[0])

    def end(self):
        bit = self.left.pop(0)
        mine = (lax.axis_index("wide") // bit) % 2
        ahead = 1 - mine if self.backward else mine
        self.total, self.state, self.rows, self.sent = join(
            self.total, self.state, self.rows, self.got, jnp.reshape(ahead, (1,)).astype(jnp.int32)
        )

    def last(self):
        self.end()
        while self.left:
            self.begin()
            self.end()
        return self.state


def rms_scale(values, scales):
    return values * lax.rsqrt(jnp.mean(values * values, axis=-1, keepdims=True) + epsilon) * scales


def doc_index(starts, positions):
    passed = (starts[None, :] <= positions[:, None]).astype(jnp.int32)
    return jnp.sum(passed, axis=1) - 1


def split_at(array, sizes, axis):
    out, at = [], 0
    for size in sizes:
        out.append(lax.slice_in_dim(array, at, at + size, axis=axis))
        at += size
    return out


def packed(parts, rows):
    flat = jnp.concatenate([part.reshape(-1) for part in parts])
    columns = -(-flat.shape[0] // rows)
    return jnp.pad(flat, (0, rows * columns - flat.shape[0])).reshape(rows, columns)


CHUNK = 128
EXTRA = 16


def spread(value, spread_ref):
    return nn(jnp.concatenate(split_low(value, 2), axis=1), spread_ref[...])


def gathered(value, gather_ref):
    return nn(value.astype(LOW), gather_ref[...])


def gathered_fine(value, gather_ref):
    high, rest = split_low(value, 2)
    return nn(high, gather_ref[...]) + nn(rest, gather_ref[...])


def with_decay(state, decay):
    terms = split_low(decay, 3) + [jnp.zeros((EXTRA - 3, decay.shape[1]), LOW)]
    return jnp.concatenate([state.astype(LOW)] + terms, axis=0)


def silu_parts(value):
    sigma = jax.nn.sigmoid(value)
    return value * sigma, sigma * (1.0 + value * (1.0 - sigma))


def local_kernel(
    x_ref, xp_ref, bc_ref, bcp_ref, rimx_ref, rimb_ref, dt_ref, marks_ref, tapx_ref, tapb_ref, bias_ref, rate_ref, spread_ref,
    act_ref, slope_ref, bcact_ref, bcslope_ref, step_ref, cum_ref, sent_ref, state_ref, decay_ref,
):
    part = pl.program_id(0)
    marks = marks_ref[...]

    def conv(raw_ref, prev_ref, rim_ref, tap_ref):
        before = jnp.where(part == 0, rim_ref[...], prev_ref[...])
        both = jnp.concatenate([before, raw_ref[...]], axis=0)
        taps = 4
        total = None
        for i in range(taps):
            term = both[8 - taps + 1 + i : 8 - taps + 1 + i + CHUNK] * tap_ref[i : i + 1, :] * marks[:, i : i + 1]
            total = term if total is None else total + term
        return silu_parts(total)

    act, slope = conv(x_ref, xp_ref, rimx_ref, tapx_ref)
    act_ref[...] = act
    slope_ref[...] = slope.astype(LOW)
    bc, bc_slope = conv(bc_ref, bcp_ref, rimb_ref, tapb_ref)
    bcact_ref[...] = bc.astype(LOW)
    bcslope_ref[...] = bc_slope.astype(LOW)
    lane = lax.broadcasted_iota(jnp.int32, (CHUNK, LANES), 1)
    value = dt_ref[...] + bias_ref[0:1, :]
    softplus = jnp.maximum(value, 0.0) + jnp.log1p(jnp.exp(-jnp.abs(value)))
    step = jnp.where(rate_ref[0:1, :] < 0.0, softplus, 0.0)
    row = lax.broadcasted_iota(jnp.int32, (CHUNK, CHUNK), 0)
    col = lax.broadcasted_iota(jnp.int32, (CHUNK, CHUNK), 1)
    cum = jnp.dot((col <= row).astype(jnp.float32), step * rate_ref[0:1, :], precision=highest, preferred_element_type=jnp.float32)
    step_ref[...] = step
    cum_ref[...] = cum
    tail = jnp.exp(cum[CHUNK - 1 :] - cum) * marks[:, 5:6] * step
    weighted = (act * spread(tail, spread_ref)).astype(LOW)
    decay = spread(jnp.exp(cum[CHUNK - 8 :]) * marks[CHUNK - 8 :, 7:8], spread_ref)[7:8]
    own = tn(bc[:, :LANES].astype(LOW), weighted)

    @pl.when(part == 0)
    def _():
        state_ref[...] = own
        decay_ref[...] = jnp.ones_like(decay_ref)
        decay_ref[0:1, :] = decay

    @pl.when(part > 0)
    def _():
        state_ref[...] = state_ref[...] * decay + own
        decay_ref[0:1, :] = decay_ref[0:1, :] * decay

    @pl.when(part == pl.num_programs(0) - 1)
    def _():
        sent_ref[...] = with_decay(state_ref[...], decay_ref[0:1, :])


def join_kernel(ahead_ref, total_ref, state_ref, rows_ref, got_ref, total_out, state_out, rows_out, sent_out):
    size = total_ref.shape[0]
    got = got_ref[:size, :].astype(jnp.float32)
    extra = got_ref[size:, :].astype(jnp.float32)
    got_decay = extra[0:1] + extra[1:2] + extra[2:3]
    decay, sweep = rows_ref[0:1, :], rows_ref[1:2, :]
    rows_out[...] = jnp.ones_like(rows_out)
    rows_out[0:1, :] = decay * got_decay

    @pl.when(ahead_ref[0] == 1)
    def _():
        state_out[...] = state_ref[...] + sweep * got
        rows_out[1:2, :] = sweep * got_decay
        total_out[...] = total_ref[...] + decay * got

    @pl.when(ahead_ref[0] == 0)
    def _():
        state_out[...] = state_ref[...]
        rows_out[1:2, :] = sweep
        total_out[...] = got + got_decay * total_ref[...]

    sent_out[...] = with_decay(total_out[...], decay * got_decay)


def mix_kernel(
    act_ref, bcact_ref, z_ref, step_ref, cum_ref, marks_ref, docs_ref, first_ref, skip_ref, gain_ref, spread_ref, gather_ref,
    ym_ref, y_ref, entry_ref, state_ref, inner_ref,
):
    part = pl.program_id(0)

    @pl.when(part == 0)
    def _():
        state_ref[...] = first_ref[...]

    marks = marks_ref[...]
    cum = cum_ref[...]
    cum_rows = cum.T
    step = step_ref[...]
    b_mat = bcact_ref[:, :LANES]
    c_mat = bcact_ref[:, LANES:]
    act = act_ref[...]
    stepped = act * spread(step, spread_ref)
    low_stepped = stepped.astype(LOW)
    row = lax.broadcasted_iota(jnp.int32, (CHUNK, CHUNK), 0)
    col = lax.broadcasted_iota(jnp.int32, (CHUNK, CHUNK), 1)
    allowed = (row >= col) & (marks[:, 6:7] == docs_ref[0:1, :])
    gram = jnp.where(allowed, nt(c_mat, b_mat), 0.0)
    first = lax.broadcasted_iota(jnp.int32, (CHUNK, LANES), 1) < LANES // 2
    pairs = act.shape[1] // LANES
    for pair in range(pairs):
        parts = []
        for head in (2 * pair, 2 * pair + 1):
            gaps = jnp.minimum(cum[:, head : head + 1] - cum_rows[head : head + 1, :], 0.0)
            parts.append((jnp.exp(gaps) * gram).astype(LOW))
        values = low_stepped[:, pair * LANES : (pair + 1) * LANES]
        zero = jnp.zeros_like(values)
        inner_ref[:, pair * LANES : (pair + 1) * LANES] = nn(
            jnp.concatenate(parts, axis=1),
            jnp.concatenate([jnp.where(first, values, zero), jnp.where(first, zero, values)], axis=0),
        )
    state = state_ref[...]
    low_state = state.astype(LOW)
    entry_ref[0] = low_state
    entering = spread(jnp.exp(cum) * marks[:, 4:5], spread_ref)
    y = inner_ref[...] + nn(c_mat, low_state) * entering + skip_ref[0:1, :] * act
    y_ref[...] = y
    gated = y * silu_parts(z_ref[...])[0]
    scale = lax.rsqrt(gathered(gated * gated, gather_ref) * (2.0 / LANES) + epsilon)
    ym_ref[...] = (gated * spread(scale, spread_ref) * gain_ref[0:1, :]).astype(LOW)
    tail = jnp.exp(cum[CHUNK - 1 :] - cum) * marks[:, 5:6]
    weighted = (stepped * spread(tail, spread_ref)).astype(LOW)
    decay = spread(jnp.exp(cum[CHUNK - 8 :]) * marks[CHUNK - 8 :, 7:8], spread_ref)[7:8]
    state_ref[...] = state * decay + tn(b_mat, weighted)


def gate_back_kernel(
    dym_ref, y_ref, z_ref, bcact_ref, cum_ref, marks_ref, gain_ref, spread_ref, gather_ref,
    dz_ref, dy_ref, sent_ref, state_ref, decay_ref,
):
    part = pl.program_id(0)
    marks = marks_ref[...]
    cum = cum_ref[...]
    y = y_ref[...]
    silu, slope = silu_parts(z_ref[...])
    gated = y * silu
    scale = lax.rsqrt(gathered(gated * gated, gather_ref) * (2.0 / LANES) + epsilon)
    wide_scale = spread(scale, spread_ref)
    d_normed = dym_ref[...]
    u = d_normed * gain_ref[0:1, :]
    inner = gathered(u * gated, gather_ref) * (2.0 / LANES) * scale * scale * scale
    d_gated = u * wide_scale - gated * spread(inner, spread_ref)
    dz_ref[...] = (d_gated * y * slope).astype(LOW)
    dy = d_gated * silu
    dy_ref[...] = dy
    entering = spread(jnp.exp(cum) * marks[:, 4:5], spread_ref)
    own = tn(bcact_ref[:, LANES:], (dy * entering).astype(LOW))
    decay = spread(jnp.exp(cum[CHUNK - 8 :]) * marks[CHUNK - 8 :, 7:8], spread_ref)[7:8]

    @pl.when(part == 0)
    def _():
        state_ref[...] = own
        decay_ref[...] = jnp.ones_like(decay_ref)
        decay_ref[0:1, :] = decay

    @pl.when(part > 0)
    def _():
        state_ref[...] = state_ref[...] * decay + own
        decay_ref[0:1, :] = decay_ref[0:1, :] * decay

    @pl.when(part == pl.num_programs(0) - 1)
    def _():
        sent_ref[...] = with_decay(state_ref[...], decay_ref[0:1, :])


def scan_back_kernel(
    act_ref, slope_ref, bcact_ref, bcslope_ref, dt_ref, step_ref, cum_ref, marks_ref, docs_ref, dy_ref, entry_ref, first_ref,
    skip_ref, bias_ref, rate_ref, spread_ref, gather_ref, x_ref, xp_ref, bc_ref, bcp_ref, rimx_ref, rimb_ref, tapx_ref, tapb_ref,
    dscan_ref, dskip_ref, dhead_ref, dtap_ref, rim_ref, edge_ref, state_ref, inner_ref, rows_ref, next_ref, nextm_ref,
):
    part = pl.program_id(0)

    @pl.when(part == 0)
    def _():
        state_ref[...] = first_ref[...]
        rows_ref[...] = jnp.zeros_like(rows_ref)
        dskip_ref[...] = jnp.zeros_like(dskip_ref)
        dhead_ref[...] = jnp.zeros_like(dhead_ref)
        dtap_ref[...] = jnp.zeros_like(dtap_ref)
        next_ref[...] = jnp.zeros_like(next_ref)
        nextm_ref[...] = jnp.zeros_like(nextm_ref)

    marks = marks_ref[...]
    cum = cum_ref[...]
    cum_rows = cum.T
    step = step_ref[...]
    b_mat = bcact_ref[:, :LANES]
    c_mat = bcact_ref[:, LANES:]
    act = act_ref[...]
    wide_step = spread(step, spread_ref)
    stepped = act * wide_step
    low_stepped = stepped.astype(LOW)
    dy = dy_ref[...]
    low_dy = dy.astype(LOW)
    row = lax.broadcasted_iota(jnp.int32, (CHUNK, CHUNK), 0)
    col = lax.broadcasted_iota(jnp.int32, (CHUNK, CHUNK), 1)
    allowed = (row <= col) & (marks[:, 6:7] == docs_ref[0:1, :])
    gram = jnp.where(allowed, nt(b_mat, c_mat), 0.0)
    first = lax.broadcasted_iota(jnp.int32, (CHUNK, LANES), 1) < LANES // 2
    lane = lax.broadcasted_iota(jnp.int32, (CHUNK, LANES), 1)
    pairs = act.shape[1] // LANES
    d_gram = jnp.zeros((CHUNK, CHUNK), jnp.float32)
    leaving = jnp.zeros((CHUNK, LANES), jnp.float32)
    for pair in range(pairs):
        cols = slice(pair * LANES, (pair + 1) * LANES)
        values, grads = low_stepped[:, cols], low_dy[:, cols]
        zero = jnp.zeros_like(values)
        d_weights = nt(jnp.concatenate([jnp.where(first, values, zero), jnp.where(first, zero, values)], axis=0), grads)
        parts = []
        for i, head in enumerate((2 * pair, 2 * pair + 1)):
            fade = jnp.exp(jnp.minimum(cum_rows[head : head + 1, :] - cum[:, head : head + 1], 0.0))
            d_weight = d_weights[i * CHUNK : (i + 1) * CHUNK]
            weight = fade * gram
            d_gram = d_gram + d_weight * fade
            moved = d_weight * weight
            rows_ref[head : head + 1, :] = jnp.sum(moved, axis=0, keepdims=True)
            leaving = jnp.where(lane == head, jnp.sum(moved, axis=1, keepdims=True), leaving)
            parts.append(weight.astype(LOW))
        inner_ref[:, cols] = nn(
            jnp.concatenate(parts, axis=1),
            jnp.concatenate([jnp.where(first, grads, zero), jnp.where(first, zero, grads)], axis=0),
        )
    d_state = state_ref[...]
    low_d_state = d_state.astype(LOW)
    entry = entry_ref[0]
    entering = spread(jnp.exp(cum) * marks[:, 4:5], spread_ref)
    tail = spread(jnp.exp(cum[CHUNK - 1 :] - cum) * marks[:, 5:6], spread_ref)
    from_state = nn(b_mat, low_d_state) * tail
    d_stepped = inner_ref[...] + from_state
    out_moved = gathered_fine(stepped * from_state, gather_ref)
    entering_dy = dy * entering
    in_moved = gathered_fine(entering_dy * nn(c_mat, entry), gather_ref)
    low_entering_dy = entering_dy.astype(LOW)
    low_gram = jnp.where(allowed, d_gram, 0.0).astype(LOW)
    d_b = nt((stepped * tail).astype(LOW), low_d_state) + nn(low_gram, c_mat)
    d_c = nt(low_entering_dy, entry) + tn(low_gram, b_mat)
    decay_small = jnp.exp(cum[CHUNK - 8 :]) * marks[CHUNK - 8 :, 7:8]
    decay = spread(decay_small, spread_ref)[7:8]
    overlap = jnp.sum(d_state * entry.astype(jnp.float32), axis=0, keepdims=True)
    d_decay = nn(jnp.concatenate(split_low(jnp.broadcast_to(overlap, (8, overlap.shape[1])), 2), axis=0), gather_ref[...])
    at_end = jnp.sum(out_moved, axis=0, keepdims=True) + (d_decay[0:1] + d_decay[8:9]) * decay_small[7:8]
    d_cum = rows_ref[...].T - leaving + in_moved - out_moved
    d_cum = d_cum + jnp.where(lax.broadcasted_iota(jnp.int32, d_cum.shape, 0) == CHUNK - 1, at_end, 0.0)
    d_log = jnp.dot((row <= col).astype(jnp.float32), d_cum, precision=highest, preferred_element_type=jnp.float32)
    rate = rate_ref[0:1, :]
    d_step = gathered_fine(act * d_stepped, gather_ref) + d_log * rate
    d_dt = d_step * jax.nn.sigmoid(dt_ref[...] + bias_ref[0:1, :])
    d_dt = jnp.where(rate < 0.0, d_dt, 0.0)
    inner = act.shape[1]
    scan = inner + 2 * LANES
    dscan_ref[:, scan:] = d_dt.astype(LOW)
    dhead_ref[0:1, :] += jnp.sum(d_dt, axis=0, keepdims=True)
    dhead_ref[1:2, :] += jnp.sum(d_log * rate * step, axis=0, keepdims=True)
    dskip_ref[0:1, :] += jnp.sum(dy * act, axis=0, keepdims=True)
    taps = 4
    marks_ext = jnp.concatenate([marks, nextm_ref[...]], axis=0)

    def conv_back(d_pre, lanes, raw_ref, prev_ref, edge_raw_ref, tap_ref):
        before = jnp.where(part == pl.num_programs(0) - 1, edge_raw_ref[...], prev_ref[...])
        raw = jnp.concatenate([before, raw_ref[...]], axis=0)
        ext = jnp.concatenate([d_pre, next_ref[:, lanes]], axis=0)
        top = jnp.concatenate([jnp.zeros_like(ext[:8]), d_pre[:8]], axis=0)
        top_marks = jnp.concatenate([marks[:8], marks[:8]], axis=0)
        d_raw, rim = None, None
        for i in range(taps):
            ahead = taps - 1 - i
            tap = tap_ref[i : i + 1, :]
            masked = d_pre * marks[:, i : i + 1]
            dtap_ref[i : i + 1, lanes] += jnp.sum(masked * raw[8 - ahead : 8 - ahead + CHUNK], axis=0, keepdims=True)
            term = (ext * marks_ext[:, i : i + 1])[ahead : ahead + CHUNK] * tap
            d_raw = term if d_raw is None else d_raw + term
            if ahead:
                term = (top * top_marks[:, i : i + 1])[ahead : ahead + 8] * tap
                rim = term if rim is None else rim + term
        next_ref[:, lanes] = d_pre[:8]
        dscan_ref[:, lanes] = d_raw.astype(LOW)
        rim_ref[:, lanes] = rim

        @pl.when(part == 0)
        def _():
            edge_ref[:, lanes] = d_raw[CHUNK - 8 :]

    conv_back(
        (d_stepped * wide_step + dy * skip_ref[0:1, :]) * slope_ref[...].astype(jnp.float32),
        slice(0, inner), x_ref, xp_ref, rimx_ref, tapx_ref,
    )
    conv_back(
        jnp.concatenate([d_b, d_c], axis=1) * bcslope_ref[...].astype(jnp.float32),
        slice(inner, scan), bc_ref, bcp_ref, rimb_ref, tapb_ref,
    )
    nextm_ref[...] = marks[:8]
    state_ref[...] = d_state * decay + tn(c_mat, low_entering_dy)


def head_matrices(inner, heads):
    owner = jnp.arange(inner, dtype=jnp.int32) // (inner // heads)
    gather_m = (owner[:, None] == jnp.arange(LANES, dtype=jnp.int32)[None, :]).astype(LOW)
    return jnp.concatenate([gather_m.T, gather_m.T], axis=0), gather_m


def lanes_row(vector):
    return jnp.pad(vector, (0, LANES - vector.shape[0]))[None, :]


def call(kernel, name, us, parts, ins, outs, scratch, reverse=False):
    def spec(block, how):
        if how == "part":
            how = lambda c: (c,) + (0,) * (len(block) - 1)
        elif how == "whole":
            how = lambda c: (0,) * len(block)
        elif isinstance(how, int):
            column = how
            how = lambda c: (c, column)

        def index(c):
            return how(parts - 1 - c if reverse else c)

        return pl.BlockSpec(block, index)

    return pl.pallas_call(
        kernel,
        grid=(parts,),
        in_specs=[spec(block, how) for _, block, how in ins],
        out_specs=[spec(block, how) for _, block, how in outs],
        scratch_shapes=scratch,
        out_shape=[shape for shape, _, _ in outs],
        compiler_params=pltpu.CompilerParams(vmem_limit_bytes=56 * 2**20),
        cost_estimate=guess(us),
        name=name,
    )(*[array for array, _, _ in ins])


def mamba_local(raw, rim, marks, taps, bias, rate, cols, mats):
    length = raw.shape[0]
    parts = length // CHUNK
    inner, n2, x_at, bc_at, dt_at = cols
    before = CHUNK // 8

    def prev(column):
        return lambda c: (jnp.maximum(c * before - 1, 0), column)

    return call(
        local_kernel,
        "mamba_local",
        11,
        parts,
        [
            (raw, (CHUNK, inner), x_at),
            (raw, (8, inner), prev(x_at)),
            (raw, (CHUNK, n2), bc_at),
            (raw, (8, n2), prev(bc_at)),
            (rim[:, :inner], (8, inner), "whole"),
            (rim[:, inner:], (8, n2), "whole"),
            (raw, (CHUNK, LANES), dt_at),
            (marks, (CHUNK, LANES), "part"),
            (taps[:, :inner], (8, inner), "whole"),
            (taps[:, inner:], (8, n2), "whole"),
            (bias, (1, LANES), "whole"),
            (rate, (1, LANES), "whole"),
            (mats[0], mats[0].shape, "whole"),
        ],
        [
            (shape((length, inner)), (CHUNK, inner), "part"),
            (shape((length, inner), LOW), (CHUNK, inner), "part"),
            (shape((length, n2), LOW), (CHUNK, n2), "part"),
            (shape((length, n2), LOW), (CHUNK, n2), "part"),
            (shape((length, LANES)), (CHUNK, LANES), "part"),
            (shape((length, LANES)), (CHUNK, LANES), "part"),
            (shape((n2 // 2 + EXTRA, inner), LOW), (n2 // 2 + EXTRA, inner), "whole"),
            (shape((n2 // 2, inner)), (n2 // 2, inner), "whole"),
            (shape((8, inner)), (8, inner), "whole"),
        ],
        [],
    )


def mamba_mix(feats, raw, marks, docs, state, skip, gain, mats):
    act, slope, bcact, bcslope, step, cum = feats
    length, inner = act.shape
    parts = length // CHUNK
    n2 = bcact.shape[1]
    return call(
        mix_kernel,
        "mamba_mix",
        11,
        parts,
        [
            (act, (CHUNK, inner), "part"),
            (bcact, (CHUNK, n2), "part"),
            (raw, (CHUNK, inner), 0),
            (step, (CHUNK, LANES), "part"),
            (cum, (CHUNK, LANES), "part"),
            (marks, (CHUNK, LANES), "part"),
            (docs, (8, CHUNK), lambda c: (0, c)),
            (state, state.shape, "whole"),
            (skip, (1, inner), "whole"),
            (gain, (1, inner), "whole"),
            (mats[0], mats[0].shape, "whole"),
            (mats[1], mats[1].shape, "whole"),
        ],
        [
            (shape((length, inner), LOW), (CHUNK, inner), "part"),
            (shape((length, inner)), (CHUNK, inner), "part"),
            (shape((parts, n2 // 2, inner), LOW), (1, n2 // 2, inner), "part"),
        ],
        [pltpu.VMEM((n2 // 2, inner), jnp.float32), pltpu.VMEM((CHUNK, inner), jnp.float32)],
    )


def mamba_gate_back(d_normed, y, raw, feats, marks, gain, mats):
    act, slope, bcact, bcslope, step, cum = feats
    length, inner = act.shape
    parts = length // CHUNK
    n2 = bcact.shape[1]
    return call(
        gate_back_kernel,
        "mamba_gate_back",
        11,
        parts,
        [
            (d_normed, (CHUNK, inner), "part"),
            (y, (CHUNK, inner), "part"),
            (raw, (CHUNK, inner), 0),
            (bcact, (CHUNK, n2), "part"),
            (cum, (CHUNK, LANES), "part"),
            (marks, (CHUNK, LANES), "part"),
            (gain, (1, inner), "whole"),
            (mats[0], mats[0].shape, "whole"),
            (mats[1], mats[1].shape, "whole"),
        ],
        [
            (shape((length, inner), LOW), (CHUNK, inner), "part"),
            (shape((length, inner)), (CHUNK, inner), "part"),
            (shape((n2 // 2 + EXTRA, inner), LOW), (n2 // 2 + EXTRA, inner), "whole"),
            (shape((n2 // 2, inner)), (n2 // 2, inner), "whole"),
            (shape((8, inner)), (8, inner), "whole"),
        ],
        [],
        reverse=True,
    )


def mamba_scan_back(feats, raw, rim, taps, marks, docs, dy, entry, state, skip, bias, rate, cols, mats):
    act, slope, bcact, bcslope, step, cum = feats
    length, inner = act.shape
    parts = length // CHUNK
    n2 = bcact.shape[1]
    x_at, bc_at, dt_at = cols[2:]
    scan = inner + n2

    def prev(column):
        return lambda c: (jnp.maximum(c * (CHUNK // 8) - 1, 0), column)

    return call(
        scan_back_kernel,
        "mamba_scan_back",
        23,
        parts,
        [
            (act, (CHUNK, inner), "part"),
            (slope, (CHUNK, inner), "part"),
            (bcact, (CHUNK, n2), "part"),
            (bcslope, (CHUNK, n2), "part"),
            (raw, (CHUNK, LANES), dt_at),
            (step, (CHUNK, LANES), "part"),
            (cum, (CHUNK, LANES), "part"),
            (marks, (CHUNK, LANES), "part"),
            (docs, (8, CHUNK), lambda c: (0, c)),
            (dy, (CHUNK, inner), "part"),
            (entry, (1, n2 // 2, inner), "part"),
            (state, state.shape, "whole"),
            (skip, (1, inner), "whole"),
            (bias, (1, LANES), "whole"),
            (rate, (1, LANES), "whole"),
            (mats[0], mats[0].shape, "whole"),
            (mats[1], mats[1].shape, "whole"),
            (raw, (CHUNK, inner), x_at),
            (raw, (8, inner), prev(x_at)),
            (raw, (CHUNK, n2), bc_at),
            (raw, (8, n2), prev(bc_at)),
            (rim[:, :inner], (8, inner), "whole"),
            (rim[:, inner:], (8, n2), "whole"),
            (taps[:, :inner], (8, inner), "whole"),
            (taps[:, inner:], (8, n2), "whole"),
        ],
        [
            (shape((length, scan + LANES), LOW), (CHUNK, scan + LANES), "part"),
            (shape((8, inner)), (8, inner), "whole"),
            (shape((8, LANES)), (8, LANES), "whole"),
            (shape((8, scan)), (8, scan), "whole"),
            (shape((8, scan)), (8, scan), "whole"),
            (shape((8, scan)), (8, scan), "whole"),
        ],
        [
            pltpu.VMEM((n2 // 2, inner), jnp.float32),
            pltpu.VMEM((CHUNK, inner), jnp.float32),
            pltpu.VMEM((LANES, CHUNK), jnp.float32),
            pltpu.VMEM((8, scan), jnp.float32),
            pltpu.VMEM((8, LANES), jnp.float32),
        ],
        reverse=True,
    )


def join(total, state, rows, got, ahead):
    whole = pl.BlockSpec(memory_space=pltpu.VMEM)
    return pl.pallas_call(
        join_kernel,
        in_specs=[pl.BlockSpec(memory_space=pltpu.SMEM)] + [whole] * 4,
        out_specs=[whole] * 4,
        out_shape=[shape(total.shape), shape(total.shape), shape(rows.shape), shape(got.shape, LOW)],
        compiler_params=pltpu.CompilerParams(vmem_limit_bytes=32 * 2**20),
        cost_estimate=guess(2),
        name="join",
    )(ahead, total, state, rows, got)


BOTH = 4
ONES = 16


def causal(scores):
    key_row = lax.broadcasted_iota(jnp.int32, scores.shape, 0)
    query = lax.broadcasted_iota(jnp.int32, scores.shape, 1)
    return jnp.where(key_row <= query, scores, FAR)


def attend_kernel(place_ref, q_ref, far_ref, kv_ref, extra_ref, o_ref, qb_ref, keys_ref, values_ref, acc_ref):
    blk = q_ref.shape[2]
    last = place_ref[0]

    @pl.when(pl.program_id(0) == 0)
    def _():
        first = lax.broadcasted_iota(jnp.int32, (blk, LANES), 1) < HEAD_SIZE

        @pl.loop(0, last + 1)
        def _(block):
            rows = pl.ds(pl.multiple_of(block * blk, blk), blk)
            both = kv_ref[rows, :]
            keys_ref[rows, :] = jnp.where(first, both, extra_ref[rows, :])
            values_ref[:ONES, rows] = jnp.ones((ONES, blk), LOW)
            values_ref[ONES:, rows] = both.astype(jnp.float32).T[HEAD_SIZE:].astype(LOW)

    queries = [
        jnp.concatenate([q_ref[i] * jnp.asarray(HEAD_SIZE ** (-0.5), LOW), far_ref[...]], axis=0)
        for i in range(BOTH)
    ]
    acc_ref[...] = jnp.zeros_like(acc_ref)

    def step(block, tops, diagonal):
        rows = pl.ds(pl.multiple_of(block * blk, blk), blk)
        keys, values = keys_ref[rows, :], values_ref[:, rows]
        new_tops = []
        for i in range(BOTH):
            scores = nn(keys, queries[i])
            if diagonal:
                scores = causal(scores)
            new_top = jnp.maximum(tops[i], jnp.max(scores, axis=0, keepdims=True))
            probs = jnp.exp(scores - new_top).astype(LOW)
            acc_ref[i] = acc_ref[i] * jnp.exp(tops[i] - new_top) + nn(values, probs)
            new_tops.append(new_top)
        return tuple(new_tops)

    tops = (jnp.full((1, blk), FAR, jnp.float32),) * BOTH
    tops = lax.fori_loop(0, last, lambda block, tops: step(block, tops, False), tops)
    tops = step(last, tops, True)
    row = lax.broadcasted_iota(jnp.int32, (HEAD_SIZE, blk), 0)
    for i in range(BOTH):
        total = acc_ref[i, 0:1, :]
        o_ref[i] = acc_ref[i, ONES:, :] / total
        extra = far_ref[...].astype(jnp.float32)
        for at, term in enumerate(split_low(-(tops[i] + jnp.log(total)), 3)):
            extra = jnp.where(row == 4 + at, term.astype(jnp.float32), extra)
        qb_ref[i] = jnp.concatenate([queries[i][:HEAD_SIZE], extra.astype(LOW)], axis=0)


def attend_back_kernel(place_ref, qb_ref, dot_ref, o_ref, kv_ref, extra_ref, dq_ref, dkv_ref, keys_ref, rows_ref, values_ref, acc_ref, dqa_ref):
    blk = qb_ref.shape[2]
    last = place_ref[0]
    member = pl.program_id(0)

    @pl.when(member == 0)
    def _():
        acc_ref[...] = jnp.zeros_like(acc_ref)
        lane = lax.broadcasted_iota(jnp.int32, (blk, LANES), 1)
        ones = jnp.where(lane < 3, 1.0, 0.0).astype(LOW)

        @pl.loop(0, last + 1)
        def _(block):
            rows = pl.ds(pl.multiple_of(block * blk, blk), blk)
            both = kv_ref[rows, :]
            keys_ref[rows, :] = jnp.where(lane < HEAD_SIZE, both, extra_ref[rows, :])
            values_ref[rows, :] = jnp.where(lane < HEAD_SIZE, ones, both)
            rows_ref[:, rows] = both.astype(jnp.float32).T[:HEAD_SIZE].astype(LOW)

    row = lax.broadcasted_iota(jnp.int32, (HEAD_SIZE, blk), 0)
    none = jnp.zeros((HEAD_SIZE, blk), jnp.float32)
    queries, d_outs, pairs = [], [], []
    for i in range(BOTH):
        queries.append(qb_ref[i])
        d_out = dot_ref[i].astype(jnp.float32)
        row_dot = jnp.sum(d_out * o_ref[i], axis=0, keepdims=True)
        extra = none
        for at, term in enumerate(split_low(-row_dot, 3)):
            extra = jnp.where(row == at, term.astype(jnp.float32), extra)
        d_outs.append(jnp.concatenate([extra, d_out], axis=0).astype(LOW))
        q_part = jnp.concatenate([qb_ref[i, :HEAD_SIZE, :].astype(jnp.float32), none], axis=0)
        pairs.append(jnp.concatenate([q_part.T, jnp.concatenate([none, d_out], axis=0).T], axis=0).astype(LOW))
    dqa_ref[...] = jnp.zeros_like(dqa_ref)

    def step(block, diagonal):
        rows = pl.ds(pl.multiple_of(block * blk, blk), blk)
        keys, values, key_rows = keys_ref[rows, :], values_ref[rows, :], rows_ref[:, rows]
        total = acc_ref[rows, :]
        for i in range(BOTH):
            logs = nn(keys, queries[i])
            if diagonal:
                logs = causal(logs)
            probs = jnp.exp(logs)
            d_scores = (probs * nn(values, d_outs[i])).astype(LOW)
            total = total + nn(jnp.concatenate([d_scores, probs.astype(LOW)], axis=1), pairs[i])
            dqa_ref[i] += nn(key_rows, d_scores)
        acc_ref[rows, :] = total

    @pl.loop(0, last)
    def _(block):
        step(block, False)

    step(last, True)
    dq_ref[...] = (dqa_ref[...] * HEAD_SIZE ** (-0.5)).astype(LOW)

    @pl.when(member == GROUP // BOTH - 1)
    def _():
        dkv_ref[...] = acc_ref[...].astype(LOW)


def attend_specs(blk, total, group):
    mine = group * (GROUP // BOTH)
    return dict(
        narrow=pl.BlockSpec((BOTH, HEAD_SIZE, blk), lambda r, p: (mine + r, 0, 0)),
        own_narrow=pl.BlockSpec((BOTH, HEAD_SIZE, blk), lambda r, p: (r, 0, 0)),
        own_broad=pl.BlockSpec((BOTH, LANES, blk), lambda r, p: (r, 0, 0)),
        kv=pl.BlockSpec((total, LANES), lambda r, p: (0, group)),
        extra=pl.BlockSpec((total, LANES), lambda r, p: (0, 0)),
        far=pl.BlockSpec((HEAD_SIZE, blk), lambda r, p: (0, 0)),
    )


def attend_masks(doc_here, key_doc, doc_count):
    docs = jnp.arange(HEAD_SIZE, dtype=jnp.int32)
    far = jnp.where((docs[:, None] != doc_here[None, :]) & (docs[:, None] < doc_count), FAR, 0.0).astype(LOW)
    lane = jnp.arange(LANES, dtype=jnp.int32)[None, :] - HEAD_SIZE
    extra = ((key_doc[:, None] == lane) | ((lane >= doc_count) & (lane < doc_count + 3))).astype(LOW)
    return far, extra


def attend(group, q_rows, key_all, masks, place):
    blk = q_rows.shape[2]
    total = key_all.shape[0]
    specs = attend_specs(blk, total, group)
    return pl.pallas_call(
        attend_kernel,
        grid_spec=pltpu.PrefetchScalarGridSpec(
            num_scalar_prefetch=1,
            grid=(GROUP // BOTH,),
            in_specs=[specs["narrow"], specs["far"], specs["kv"], specs["extra"]],
            out_specs=[specs["own_narrow"], specs["own_broad"]],
            scratch_shapes=[
                pltpu.VMEM((total, LANES), LOW),
                pltpu.VMEM((HEAD_SIZE + ONES, total), LOW),
                pltpu.VMEM((BOTH, HEAD_SIZE + ONES, blk), jnp.float32),
            ],
        ),
        out_shape=[shape((GROUP, HEAD_SIZE, blk)), shape((GROUP, LANES, blk), LOW)],
        compiler_params=pltpu.CompilerParams(vmem_limit_bytes=56 * 2**20),
        cost_estimate=guess(17),
        name="attend",
    )(place, q_rows, masks[0], key_all, masks[1])


def attend_back(group, q_back, out, d_rows, key_all, masks, place):
    blk = d_rows.shape[2]
    total = key_all.shape[0]
    specs = attend_specs(blk, total, group)
    return pl.pallas_call(
        attend_back_kernel,
        grid_spec=pltpu.PrefetchScalarGridSpec(
            num_scalar_prefetch=1,
            grid=(GROUP // BOTH,),
            in_specs=[specs["own_broad"], specs["narrow"], specs["own_narrow"], specs["kv"], specs["extra"]],
            out_specs=[specs["own_narrow"], specs["extra"]],
            scratch_shapes=[
                pltpu.VMEM((total, LANES), LOW),
                pltpu.VMEM((HEAD_SIZE, total), LOW),
                pltpu.VMEM((total, LANES), LOW),
                pltpu.VMEM((total, LANES), jnp.float32),
                pltpu.VMEM((BOTH, HEAD_SIZE, blk), jnp.float32),
            ],
        ),
        out_shape=[shape((GROUP, HEAD_SIZE, blk), LOW), shape((total, LANES), LOW)],
        compiler_params=pltpu.CompilerParams(vmem_limit_bytes=60 * 2**20),
        cost_estimate=guess(27),
        name="attend_back",
    )(place, q_back, d_rows, out, key_all, masks[1])


PIECE = 256


def feed_kernel(x_ref, gy_ref, plain_ref, w_ref, out_ref, dx_ref, grad_ref, xt_ref):
    fold = w_ref.shape[1] // 3

    @pl.when(pl.program_id(0) == 0)
    def _():
        out_ref[...] = jnp.zeros_like(out_ref)
        dx_ref[...] = jnp.zeros_like(dx_ref)
        xt_ref[...] = x_ref[...].astype(jnp.float32).T.astype(LOW)

    @pl.loop(0, fold // PIECE)
    def _(piece):
        at = pl.multiple_of(piece * PIECE, PIECE)
        gate_cols = pl.ds(at, PIECE)
        up_cols = pl.ds(pl.multiple_of(fold + at, PIECE), PIECE)
        down_cols = pl.ds(2 * fold, fold)
        w_gate, w_up, w_down = w_ref[:, gate_cols], w_ref[:, up_cols], w_ref[gate_cols, down_cols]
        x, gy = x_ref[...], gy_ref[...]
        gate, up = nn(x, w_gate), nn(x, w_up)
        sigma = jax.nn.sigmoid(gate)
        silu = gate * sigma
        act = silu * up
        d_act = nt(gy, w_down)
        d_gate = (d_act * up * sigma * (1.0 + gate * (1.0 - sigma))).astype(LOW)
        d_up = (d_act * silu).astype(LOW)
        out_ref[...] += nn(act.astype(LOW), w_down)
        dx_ref[...] += nt(d_gate, w_gate) + nt(d_up, w_up)
        x_t = xt_ref[...]
        grad_ref[:, gate_cols] = nn(x_t, d_gate).astype(LOW)
        grad_ref[:, up_cols] = nn(x_t, d_up).astype(LOW)
        grad_ref[gate_cols, down_cols] = nn(act.T.astype(LOW), plain_ref[...]).astype(LOW)


def feed_forward(x, gy, plain, w, folds, fold):
    tokens, width = x.shape
    whole = pl.BlockSpec((tokens, width), lambda j: (0, 0))
    return pl.pallas_call(
        feed_kernel,
        grid=(folds,),
        in_specs=[whole, whole, whole, pl.BlockSpec((width, 3 * fold), lambda j: (0, j))],
        out_specs=[whole, whole, pl.BlockSpec((width, 3 * fold), lambda j: (0, j))],
        out_shape=[
            shape((tokens, width)),
            shape((tokens, width)),
            shape((width, 3 * fold * folds), LOW),
        ],
        scratch_shapes=[pltpu.VMEM((width, tokens), LOW)],
        compiler_params=pltpu.CompilerParams(vmem_limit_bytes=60 * 2**20),
        cost_estimate=guess(35),
        name="feed_forward",
    )(x, gy, plain, w)


def last_grads_kernel(x_ref, scan_ref, query_ref, kv_ref, small_ref, grad_ref):
    x_t = x_ref[...].astype(jnp.float32).T.astype(LOW)
    scan = scan_ref.shape[1]
    query = query_ref.shape[1]
    grad_ref[:, : scan - LANES] = nn(x_t, scan_ref[:, : scan - LANES]).astype(LOW)
    grad_ref[:, scan - LANES : scan] = (nn(x_t, scan_ref[:, scan - LANES :]) + small_ref[...]).astype(LOW)
    grad_ref[:, scan : scan + query] = nn(x_t, query_ref[...]).astype(LOW)
    grad_ref[:, scan + query :] = nn(x_t, kv_ref[...]).astype(LOW)


def last_grads(x, d_scan, d_query, d_kv, small):
    tokens, width = x.shape
    count = d_scan.shape[1] + d_query.shape[1] + d_kv.shape[1]
    return pl.pallas_call(
        last_grads_kernel,
        out_shape=shape((width, count), LOW),
        compiler_params=pltpu.CompilerParams(vmem_limit_bytes=56 * 2**20),
        cost_estimate=guess(8),
        name="last_grads",
    )(x, d_scan, d_query, d_kv, small)


def input_back_kernel(scan_ref, gate_ref, query_ref, kv_ref, w_ref, x_ref, more_ref, gain_ref, dx_ref):
    at, total = 0, None
    for ref in (scan_ref, gate_ref, query_ref, kv_ref):
        term = nt(ref[...], w_ref[:, at : at + ref.shape[1]])
        total = term if total is None else total + term
        at += ref.shape[1]
    x = x_ref[...]
    scale = lax.rsqrt(jnp.mean(x * x, axis=1, keepdims=True) + epsilon)
    u = total * gain_ref[...]
    inner = jnp.mean(u * x, axis=1, keepdims=True) * scale * scale * scale
    dx_ref[...] = (more_ref[...] + u * scale - x * inner).astype(LOW)


def input_back(d_scan, d_gate, d_query, d_kv, w, x, more, gain):
    tokens, width = x.shape
    part = min(2 * CHUNK, tokens)
    rows = lambda array: pl.BlockSpec((part, array.shape[1]), lambda i: (i, 0))
    whole = lambda array: pl.BlockSpec(array.shape, lambda i: (0, 0))
    return pl.pallas_call(
        input_back_kernel,
        grid=(tokens // part,),
        in_specs=[rows(a) for a in (d_scan, d_gate, d_query, d_kv)] + [whole(w), rows(x), rows(more), whole(gain)],
        out_specs=rows(x),
        out_shape=shape((tokens, width), LOW),
        compiler_params=pltpu.CompilerParams(vmem_limit_bytes=56 * 2**20),
        cost_estimate=guess(10),
        name="input_back",
    )(d_scan, d_gate, d_query, d_kv, w, x, more, gain)


def tap_marks(starts, first, length, taps):
    ext = doc_index(starts, first - (taps - 1) + jnp.arange(length + taps - 1, dtype=jnp.int32))
    return jnp.stack([(ext[i : i + length] == ext[taps - 1 :]).astype(jnp.float32) for i in range(taps)], axis=1)


def marks_of(starts, block_base, length, taps):
    ext = doc_index(starts, block_base - (taps - 1) + jnp.arange(length + taps - 1, dtype=jnp.int32))
    here = ext[taps - 1 :]
    chunks = here.reshape(-1, CHUNK)
    ahead = ext[taps - 2 : taps - 2 + length].reshape(-1, CHUNK)[:, :1]
    last = chunks[:, -1:]
    columns = [ext[i : i + length] == here for i in range(taps)] + [
        (chunks == ahead).reshape(-1),
        (chunks == last).reshape(-1),
        here,
        jnp.broadcast_to(last == ahead, chunks.shape).reshape(-1),
    ]
    marks = jnp.stack([column.astype(jnp.float32) for column in columns], axis=1)
    marks = jnp.pad(marks, ((0, 0), (0, LANES - len(columns))))
    return marks, jnp.broadcast_to(here.astype(jnp.float32)[None], (8, length)), here


def per_device(
    hidden_in,
    cotangent,
    doc_starts,
    gain_in,
    mamba_gate_w,
    mamba_in_w,
    mamba_bc_w,
    mamba_dt_w,
    dt_bias,
    a_log,
    d_skip,
    conv_x,
    conv_bc,
    mamba_gain,
    attn_q_w,
    attention_key_value_weight,
    mamba_out_w,
    attn_out_w,
    gain_ffn,
    ffn_gate_w,
    ffn_up_w,
    ffn_down_w,
):
    devices = lax.axis_size("head") * lax.axis_size("wide")
    wide_id = lax.axis_index("wide")
    micro_count = hidden_in.shape[0]
    block_tok = hidden_in.shape[2] * lax.axis_size("head")
    taps = conv_x.shape[0]
    heads = dt_bias.shape[0]
    rows, inner = mamba_gate_w.shape
    width = rows * devices
    bc_cols = mamba_bc_w.shape[1]
    query_cols = attn_q_w.shape[1]
    kv_cols = attention_key_value_weight.shape[1]
    hidden = ffn_gate_w.shape[1]
    out_rows = mamba_out_w.shape[0]
    attn_rows = attn_out_w.shape[0]
    chan = conv_x.shape[1]
    chan_bc = conv_bc.shape[1]

    scan_cols = inner + bc_cols
    first_cols = scan_cols + LANES

    heads_dev, wide_dev = lax.axis_size("head"), lax.axis_size("wide")
    folds = hidden // width
    feature = jnp.arange(width, dtype=jnp.int32)
    inside = (feature // rows) % wide_dev * heads_dev + feature // (rows * wide_dev)
    order = (inside[:, None] * rows + (feature % rows)[:, None] == feature[None, :]).astype(LOW)

    def mixed(array):
        return nn(array.reshape(-1, width), order).astype(LOW).reshape(array.shape)

    def plain(array):
        return nt(array.reshape(-1, width), order).astype(LOW).reshape(array.shape)

    def by_place(array):
        return array.reshape((heads_dev, wide_dev) + array.shape[1:]).swapaxes(0, 1).reshape(array.shape)

    def by_owner(array):
        return array.reshape((wide_dev, heads_dev) + array.shape[1:]).swapaxes(0, 1).reshape(array.shape)

    def folded(weight):
        return weight.reshape(rows, heads_dev, wide_dev, folds, rows).transpose(0, 3, 2, 1, 4).reshape(rows, folds, width)

    def unfolded(parts):
        unit = jnp.arange(hidden, dtype=jnp.int32)
        owner, fold, row = unit // (folds * rows), unit // rows % folds, unit % rows
        at = (owner % wide_dev * heads_dev + owner // wide_dev) * rows + row
        total = 0.0
        for i, part in enumerate(parts):
            one_hot = ((feature[:, None] == at[None, :]) & (fold == i)[None, :]).astype(LOW)
            total = total + nn(jnp.concatenate(split_low(part, 3), axis=0), one_hot)
        high, middle, low = split_at(total, (rows,) * 3, 0)
        return high + (middle + low)

    small = packed([gain_in, gain_ffn, mamba_gain, conv_x, conv_bc], rows)
    small_cols = small.shape[1]
    pad = jnp.zeros((rows, LANES - heads - small_cols), LOW)
    in_shard = jnp.concatenate(
        [mamba_in_w, mamba_bc_w, mamba_dt_w, small, pad, mamba_gate_w, attn_q_w, attention_key_value_weight], axis=1
    )
    to_width = mixed(jnp.concatenate([ffn_down_w, mamba_out_w, attn_out_w], axis=0)).reshape(-1, rows, width)
    gate_folds, up_folds = folded(ffn_gate_w), folded(ffn_up_w)
    ffn_shard = []
    for i in range(folds):
        ffn_shard += [gate_folds[:, i], up_folds[:, i], to_width[i]]
    ffn_shard = jnp.concatenate(ffn_shard, axis=1)
    out_shard = jnp.concatenate([to_width[i] for i in range(folds, to_width.shape[0])], axis=1)
    x_pieces = mixed(hidden_in[:, 0])

    micro = jnp.minimum(lax.axis_index("head"), micro_count - 1)
    starts = pick(doc_starts, micro)
    block_base = wide_id * block_tok
    marks, docs_row, doc_here = marks_of(starts, block_base, block_tok, taps)
    key_doc = doc_index(starts, jnp.arange(block_tok * lax.axis_size("wide"), dtype=jnp.int32))
    masks = attend_masks(doc_here, key_doc, doc_starts.shape[1])
    mats = head_matrices(inner, heads)
    bias_row = lanes_row(dt_bias)
    rate_row = lanes_row(-jnp.exp(a_log))
    skip_row = jnp.repeat(d_skip, inner // heads)[None]
    in_rows = HeadRows(in_shard, micro_count)
    prepared = (marks, docs_row, masks, mats, bias_row, rate_row, skip_row, ffn_shard, out_shard, x_pieces)
    in_rows.got, prepared = tied(in_rows.got, prepared)
    marks, docs_row, masks, mats, bias_row, rate_row, skip_row, ffn_shard, out_shard, x_pieces = prepared
    in_rows, out_shard = tied(in_rows.end(), out_shard)
    w_in = gather_wide(in_rows)
    out_rows_all, x_pieces = tied(HeadRows(out_shard, micro_count).end(), x_pieces)
    x_low, ffn_shard = tied(ToBlocks(x_pieces).end(), ffn_shard)
    ffn_rows = HeadRows(ffn_shard, micro_count)
    w_in, out_rows_all = tied(w_in, out_rows_all)
    w_out = gather_wide(out_rows_all)
    x_tokens = x_low.astype(jnp.float32)

    small_at = scan_cols + heads
    w_scan, w_gate, w_qkv = split_at(w_in, (first_cols, inner, query_cols + kv_cols), 1)
    small_all = w_scan[:, small_at : small_at + small_cols].reshape(devices, -1).astype(jnp.float32)
    g_in, g_ffn, g_mamba, c_x, c_bc = split_at(
        small_all, (rows, rows, chan, taps * chan, taps * chan_bc), 1
    )
    gain_in_all = g_in.reshape(-1)
    gain_ffn_all = g_ffn.reshape(-1)
    g_mamba, c_x, c_bc = by_owner(g_mamba), by_owner(c_x), by_owner(c_bc)
    gain_mamba_row = g_mamba.reshape(1, -1)
    taps_all = jnp.concatenate(
        [
            c_x.reshape(devices, taps, chan).transpose(1, 0, 2).reshape(taps, -1),
            c_bc.reshape(devices, taps, chan_bc).transpose(1, 0, 2).reshape(taps, -1),
        ],
        axis=1,
    )
    cols = (inner, bc_cols, 0, inner // bc_cols, scan_cols // LANES)
    place = jnp.reshape(wide_id, (1,)).astype(jnp.int32)


    block_in = rms_scale(x_tokens, gain_in_all).astype(LOW)
    raw_qkv, block_in = tied(nn(block_in, w_qkv).astype(LOW), block_in)
    keys = Gathered(raw_qkv[:, query_cols:])
    keys.begin()
    keys.got, raw_scan, block_in = tied(keys.got, nn(block_in, w_scan), block_in)
    keys.end()
    rim = shifted(raw_scan[block_tok - 8 :, :scan_cols], "wide", 1)
    keys.begin()
    rim, raw_gate = tied(rim, nn(block_in, w_gate))
    rim = jnp.where(jnp.arange(8)[:, None] > 8 - taps, rim, 0.0)
    taps_ext = jnp.pad(taps_all, ((0, 8 - taps), (0, 0)))
    *feats, sent, total, decay_rows = mamba_local(raw_scan, rim, marks, taps_ext, bias_row, rate_row, cols, mats)
    keys.got, ffn_rows.got, sent = tied(keys.got, ffn_rows.got, sent)
    ffn_rows, w_out = tied(ffn_rows.end(), w_out)
    w_ffn = gather_wide(ffn_rows)
    keys.end()
    forward = Carried(sent, total, decay_rows, False)
    forward.begin()
    key_all = keys.rest()
    forward.end()
    q_rows = raw_qkv[:, :query_cols].T.reshape(QUERY_HEADS, HEAD_SIZE, block_tok)
    gy = ToBlocks(cotangent[:, 0])
    forward.begin()
    out_0, q_back_0 = attend(0, q_rows, key_all, masks, place)
    forward.got, gy.got, out_0, q_rows = tied(forward.got, gy.got, out_0, q_rows)
    forward.end()
    forward.sent, q_rows = tied(forward.sent, q_rows)
    forward.begin()
    out_1, q_back_1 = attend(1, q_rows, key_all, masks, place)
    forward.got, out_1 = tied(forward.got, out_1)
    state_in = forward.last()
    attn_low = jnp.concatenate([out_0, out_1], axis=0).reshape(query_cols, block_tok).astype(LOW)
    mamba_low, y_low, entry = mamba_mix(feats, raw_gate, marks, docs_row, state_in, skip_row, gain_mamba_row, mats)
    gy_plain = gy.end()
    d_out_low = mixed(gy_plain)
    out_both = jnp.concatenate(
        [w_out[:, i : i + width].reshape(devices, rows, width) for i in range(0, w_out.shape[1], width)], axis=1
    )
    out_both = by_owner(out_both)
    w_mamba_out = out_both[:, :out_rows].reshape(-1, width)
    w_attn_out = out_both[:, out_rows:].reshape(-1, width)

    resid = x_tokens + nn(mamba_low, w_mamba_out) + tn(attn_low, w_attn_out)
    normed_ffn, pull_ffn = jax.vjp(lambda values: rms_scale(values, gain_ffn_all), resid)
    ffn_in = normed_ffn.astype(LOW)
    fed, d_ffn_in, grad_ffn = feed_forward(ffn_in, d_out_low, gy_plain, w_ffn, folds, width)
    part_ffn = sum_wide(grad_ffn)
    (d_resid_norm,) = pull_ffn(d_ffn_in)
    d_resid = d_out_low.astype(jnp.float32) + d_resid_norm

    d_mix = d_resid.astype(LOW)
    d_gate_z, dy_low, sent_back, total, decay_rows = mamba_gate_back(
        nt(d_mix, w_mamba_out), y_low, raw_gate, feats, marks, gain_mamba_row, mats
    )
    backward = Carried(sent_back, total, decay_rows, True)
    backward.begin()
    d_attn = nt(w_attn_out, d_mix).astype(LOW).reshape(QUERY_HEADS, HEAD_SIZE, block_tok)
    backward.got, d_attn = tied(backward.got, d_attn)
    backward.end()
    backward.sent, d_attn = tied(backward.sent, d_attn)
    backward.begin()
    d_query_0, d_kv_0 = attend_back(0, q_back_0, out_0, d_attn, key_all, masks, place)
    backward.got, d_query_0, d_kv_0, d_attn = tied(backward.got, d_query_0, d_kv_0, d_attn)
    backward.end()
    backward.sent, d_attn, d_kv_0 = tied(backward.sent, d_attn, d_kv_0)
    backward.begin()
    core_0 = CoreSum(d_kv_0)
    d_query_1, d_kv_1 = attend_back(1, q_back_1, out_1, d_attn, key_all, masks, place)
    backward.got, core_0.got, d_query_1, d_kv_1 = tied(backward.got, core_0.got, d_query_1, d_kv_1)
    d_state = backward.last()
    d_state, d_kv_1, d_mix = tied(d_state, d_kv_1, d_mix)
    core_1 = CoreSum(d_kv_1)
    d_query = jnp.concatenate([d_query_0, d_query_1], axis=0).reshape(query_cols, block_tok).T
    d_mix_plain = plain(d_mix)
    grad_out = jnp.concatenate(
        [
            tn(mamba_low, d_mix_plain).astype(LOW).reshape(devices, out_rows, width),
            nn(attn_low, d_mix_plain).astype(LOW).reshape(devices, attn_rows, width),
        ],
        axis=1,
    ).reshape(devices, -1, rows, width)
    grad_out = by_place(grad_out)
    grad_gate = tn(block_in, d_gate_z).astype(LOW)
    early = jnp.concatenate(
        [grad_out[:, i].reshape(width, width) for i in range(grad_out.shape[1])] + [grad_gate], axis=1
    )
    core_1.got, early = tied(core_1.got, early)
    chip_sum = ChipSum(jnp.concatenate([core_0.end(), core_1.end()], axis=2))
    early, part_ffn = tied(early, part_ffn)
    part_early = sum_wide(early)
    out_plain = plain((resid + fed).astype(LOW))
    own_ffn = HeadSum(part_ffn, micro_count)
    d_scan, grad_skip, grad_head, grad_taps, rim_back, edge = mamba_scan_back(
        feats, raw_scan, rim, taps_ext, marks, docs_row, dy_low, entry, d_state,
        skip_row, bias_row, rate_row, cols, mats,
    )
    chip_sum.got, own_ffn.got, d_scan, edge, rim_back, grad_taps, grad_head, grad_skip, d_query, out_plain = tied(
        chip_sum.got, own_ffn.got, d_scan, edge, rim_back, grad_taps, grad_head, grad_skip, d_query, out_plain
    )
    rim_came = shifted(rim_back, "wide", -1)
    out_back = FromBlocks(out_plain, micro_count)
    d_kv = chip_sum.end()
    own_ffn = own_ffn.end()
    d_scan = lax.dynamic_update_slice(d_scan, (edge + rim_came).astype(LOW), (block_tok - 8, 0))
    grad_small = jnp.concatenate(
        [
            by_place(grad_taps[:taps, :inner].reshape(taps, devices, chan).transpose(1, 0, 2).reshape(devices, -1)),
            by_place(grad_taps[:taps, inner:].reshape(taps, devices, chan_bc).transpose(1, 0, 2).reshape(devices, -1)),
        ],
        axis=1,
    )
    grad_small = jnp.pad(grad_small, ((0, 0), (0, rows * small_cols - grad_small.shape[1])))
    grad_small = jnp.pad(
        grad_small.reshape(width, small_cols), ((0, 0), (heads, LANES - heads - small_cols))
    )
    late = last_grads(block_in, d_scan, d_query, d_kv, grad_small)

    head_sums = jnp.concatenate(
        [grad_head[:2, :heads].reshape(-1), jnp.sum(grad_skip[0].reshape(heads, -1), axis=1)]
    )
    out_back.got, late, part_early, d_scan, own_ffn, head_sums = tied(
        out_back.got, late, part_early, d_scan, own_ffn, head_sums
    )
    part_late = sum_wide(late)
    totals = EverySum(head_sums)
    totals.begin()
    totals.got, part_early, d_scan = tied(totals.got, part_early, d_scan)
    totals.end()
    own_early = HeadSum(part_early, micro_count)
    totals.begin()
    grad_x = input_back(d_scan, d_gate_z, d_query, d_kv, w_in, x_tokens, d_resid, gain_in_all[None])
    own_early.got, own_early.own, totals.got, grad_x = tied(own_early.got, own_early.own, totals.got, grad_x)
    totals.end()
    x_plain, own_ffn = tied(plain(grad_x), own_ffn)
    x_back = FromBlocks(x_plain, micro_count)
    totals.begin()
    g_ffn = split_at(own_ffn, (width,) * (3 * folds), 1)
    g_gate_w, g_up_w = unfolded(g_ffn[0::3]), unfolded(g_ffn[1::3])
    totals.got, g_gate_w, g_up_w = tied(totals.got, g_gate_w, g_up_w)
    totals.end()
    totals.begin()
    x_back.got, own_early.got, own_early.own, part_late, totals.got, g_gate_w, g_up_w = tied(
        x_back.got, own_early.got, own_early.own, part_late, totals.got, g_gate_w, g_up_w
    )
    totals.end()
    own_late = HeadSum(part_late, micro_count)
    summed = totals.rest()
    results = x_back.end()
    own_late.got, results = tied(own_late.got, results)
    per_head = summed[: 3 * heads].reshape(3, heads)
    g_x, g_bc, g_dt, g_small, _, g_q, g_kv = own_late.end(
        (inner, bc_cols, heads, small_cols, LANES - heads - small_cols, query_cols, kv_cols)
    )
    *g_out, g_gate = own_early.end((width,) * ((out_rows + attn_rows) // rows) + (inner,))
    o_conv_x, o_conv_bc, _ = split_at(
        g_small.reshape(-1), (taps * chan, taps * chan_bc, rows * small_cols - taps * (chan + chan_bc)), 0
    )
    g_mamba_out, g_attn_out = split_at(jnp.concatenate(g_out, axis=0), (out_rows, attn_rows), 0)
    def gain_grad(gain, pairs):
        total = 0.0
        for weight, grad in pairs:
            total = total + jnp.sum(weight.astype(jnp.float32) * grad, axis=1)
        return total / gain.astype(jnp.float32)

    o_gain_in = gain_grad(
        gain_in,
        (
            (mamba_in_w, g_x),
            (mamba_bc_w, g_bc),
            (mamba_dt_w, g_dt),
            (mamba_gate_w, g_gate),
            (attn_q_w, g_q),
            (attention_key_value_weight, g_kv),
        ),
    )
    o_gain_ffn = gain_grad(gain_ffn, ((ffn_gate_w, g_gate_w), (ffn_up_w, g_up_w)))
    o_gain_m = gain_grad(mamba_gain, ((mamba_out_w, g_mamba_out),))
    return (
        out_back.end()[:, None],
        results[:, None],
        o_gain_in,
        g_gate,
        g_x,
        g_bc,
        g_dt,
        per_head[0],
        per_head[1],
        per_head[2],
        o_conv_x.reshape(taps, chan),
        o_conv_bc.reshape(taps, chan_bc),
        o_gain_m,
        g_q,
        g_kv,
        g_mamba_out,
        g_attn_out,
        o_gain_ffn,
        g_gate_w,
        g_up_w,
        jnp.concatenate(g_ffn[2::3], axis=0),
    )


def solution(mesh):
    tokens = P(None, "wide", "head", None)
    matrix = P(ALL, None)
    vector = P(ALL)
    taps = P(None, ALL)
    in_specs = (
        (tokens, tokens, P(), vector)
        + (matrix,) * 4
        + (P(),) * 3
        + (taps, taps, vector)
        + (matrix,) * 4
        + (vector,)
        + (matrix,) * 3
    )
    out_specs = (
        (tokens, tokens, vector)
        + (matrix,) * 4
        + (P(),) * 3
        + (taps, taps, vector)
        + (matrix,) * 4
        + (vector,)
        + (matrix,) * 3
    )
    return jax.shard_map(
        per_device, mesh=mesh, in_specs=in_specs, out_specs=out_specs, check_vma=False
    )
```

```python
from functools import partial

import jax
import jax.numpy as jnp
from jax import lax
from jax.experimental import pallas as pl
from jax.experimental.pallas import tpu as pltpu
from jax.sharding import PartitionSpec as P

QUERY_HEADS = 8
KEY_VALUE_HEADS = 2
HEAD_SIZE = 64
GROUP = QUERY_HEADS // KEY_VALUE_HEADS
LANES = 128
LOW = jnp.bfloat16
FAR = -1e30
ALL = ("head", "wide")

epsilon = 1e-05
highest = lax.Precision.HIGHEST


def nn(left, right):
    return jnp.dot(left, right, preferred_element_type=jnp.float32)


def nt(left, right):
    return lax.dot_general(left, right, (((1,), (1,)), ((), ())), preferred_element_type=jnp.float32)


def tn(left, right):
    return lax.dot_general(left, right, (((0,), (0,)), ((), ())), preferred_element_type=jnp.float32)


def split_low(value, parts):
    terms = []
    for _ in range(parts):
        term = value.astype(LOW)
        terms.append(term)
        value = value - term.astype(jnp.float32)
    return terms


def shape(dims, kind=jnp.float32):
    return jax.ShapeDtypeStruct(dims, kind)


def shifted(value, axis, steps):
    count = lax.axis_size(axis)
    initial, last = (max(0, -steps), min(count, count - steps))
    return lax.ppermute(value, axis, [(source, source + steps) for source in range(initial, last)])


def swapped(value, axis, bit):
    count = lax.axis_size(axis)
    return lax.ppermute(value, axis, [(i, i ^ bit) for i in range(count)])


def pick(array, index, axis=0):
    return lax.dynamic_index_in_dim(array, index, axis, False)


def guess(us):
    return pl.CostEstimate(flops=int(us * 1e9), bytes_accessed=int(us * 3e6), transcendentals=0)


def tied(*values):
    return lax.optimization_barrier(values)


def sent_on(pieces, sources, receivers):
    count = lax.axis_size("head")
    place = lax.axis_index("head")
    got = []
    for step in range(1, count):
        pairs = [(i, (i + step) % count) for i in range(count)]
        pairs = [(i, k) for i, k in pairs if i < sources and k < receivers]
        got.append(lax.ppermute(pieces((place + step) % count), "head", pairs))
    return got


def put_together(own, got):
    place = lax.axis_index("head")
    count = len(got) + 1
    whole = lax.dynamic_update_index_in_dim(jnp.zeros((count,) + own.shape, own.dtype), own, place, 0)
    for step, array in enumerate(got, 1):
        whole = lax.dynamic_update_index_in_dim(whole, array, (place - step) % count, 0)
    return whole


class HeadRows:
    def __init__(self, own, receivers):
        self.own = own
        self.got = sent_on(lambda target: own, lax.axis_size("head"), receivers)

    def end(self):
        return put_together(self.own, self.got).reshape(-1, self.own.shape[1])


class ToBlocks:
    def __init__(self, pieces):
        micro_count = pieces.shape[0]
        place = lax.axis_index("head")

        def of(target):
            return pick(pieces, jnp.minimum(target, micro_count - 1))

        self.own = jnp.where(place < micro_count, of(place), jnp.zeros_like(pieces[0]))
        self.got = sent_on(of, lax.axis_size("head"), micro_count)

    def end(self):
        return put_together(self.own, self.got).reshape(-1, self.own.shape[1])


class FromBlocks:
    def __init__(self, block, micro_count):
        count = lax.axis_size("head")
        parts = block.reshape(count, block.shape[0] // count, block.shape[1])
        self.micro_count = micro_count
        self.own = pick(parts, lax.axis_index("head"))
        self.got = sent_on(lambda target: pick(parts, target), micro_count, count)

    def end(self):
        return put_together(self.own, self.got)[: self.micro_count]


class HeadSum:
    def __init__(self, part, sources, block=None):
        count = lax.axis_size("head")
        place = lax.axis_index("head")
        array = part.reshape(count, -1, part.shape[1])
        self.width = array.shape[2]
        self.sources = sources
        if block is not None:
            self.block_shape = (block.shape[0] // count, block.shape[1])
            array = jnp.concatenate([array, block.reshape(count, array.shape[1], -1)], axis=2)
        self.own = pick(array, place)
        self.got = sent_on(lambda target: pick(array, target), sources, count)

    def end(self, sizes=None):
        place = lax.axis_index("head")
        at, out = 0, []
        for size in sizes or (self.width,):
            cut = [array[:, at : at + size].astype(jnp.float32) for array in [self.own] + self.got]
            total = jnp.where(place < self.sources, cut[0], 0.0)
            for term in cut[1:]:
                total = total + term
            out.append(total)
            at += size
        return out if sizes else out[0]

    def end_block(self):
        own, got = self.own[:, self.width :], [array[:, self.width :] for array in self.got]
        whole = put_together(own, got)
        return whole.reshape((whole.shape[0],) + self.block_shape)[: self.sources]


def wide_bits():
    bits = []
    while 1 << (len(bits) + 1) <= lax.axis_size("wide"):
        bits.append(1 << len(bits))
    return bits


class EverySum:
    def __init__(self, value):
        self.value = value
        self.left = [("wide", bit) for bit in wide_bits()]
        bit = 1
        while bit < lax.axis_size("head"):
            self.left.append(("head", bit))
            bit *= 2

    def begin(self):
        self.got = swapped(self.value, *self.left.pop(0))

    def end(self):
        self.value = self.value + self.got

    def rest(self):
        while self.left:
            self.begin()
            self.end()
        return self.value


class Gathered:
    def __init__(self, own):
        bits = wide_bits()
        half = own.shape[1] // 2
        self.parts = [own[:, :half], own[:, half:]]
        self.left = [bits[1:], bits[:0:-1]]
        self.done = [[], []]

    def begin(self):
        self.got = [swapped(array, "wide", left[0]) for array, left in zip(self.parts, self.left)]

    def end(self):
        place = lax.axis_index("wide")
        for i, got in enumerate(self.got):
            bit = self.left[i].pop(0)
            mine = (place // bit) % 2
            array = self.parts[i]
            self.parts[i] = jnp.where(mine == 0, jnp.stack([array, got]), jnp.stack([got, array]))
            self.done[i].insert(0, bit)

    def rest(self):
        while self.left[0]:
            self.begin()
            self.end()
        arrays = []
        for array, done in zip(self.parts, self.done):
            ranks = [done.index(bit) for bit in sorted(done, reverse=True)]
            arrays.append(array.transpose(ranks + [len(done), len(done) + 1]))
        both = jnp.concatenate(arrays, axis=-1)
        got = swapped(both, "wide", 1)
        mine = lax.axis_index("wide") % 2
        stacked = jnp.where(mine == 0, jnp.stack([both, got], axis=-3), jnp.stack([got, both], axis=-3))
        return stacked.reshape(-1, both.shape[-1])


class CoreSum:
    def __init__(self, part):
        count = lax.axis_size("wide")
        mine = lax.axis_index("wide") % 2
        part = part.reshape(count // 2, 2, -1, part.shape[1])
        self.own = pick(part, mine, 1)
        self.got = swapped(pick(part, 1 - mine, 1), "wide", 1)

    def end(self):
        return (self.own.astype(jnp.float32) + self.got.astype(jnp.float32)).astype(self.own.dtype)


class ChipSum:
    def __init__(self, array):
        chip = lax.axis_index("wide") // 2
        self.own = pick(array, chip)
        self.got = [swapped(pick(array, chip ^ other), "wide", 2 * other) for other in range(1, array.shape[0])]

    def end(self):
        total = self.own.astype(jnp.float32)
        for array in self.got:
            total = total + array.astype(jnp.float32)
        return total.astype(self.own.dtype)


def sum_wide(array):
    return lax.psum_scatter(array, "wide", scatter_dimension=0, tiled=True)


def gather_wide(array):
    return lax.all_gather(array, "wide", axis=0, tiled=True)


class Carried:
    def __init__(self, sent, total, rows, backward):
        self.sent, self.total, self.rows = sent, total, rows
        self.state = jnp.zeros_like(total)
        self.backward = backward
        self.left = wide_bits()

    def begin(self):
        self.got = swapped(self.sent, "wide", self.left[0])

    def end(self):
        bit = self.left.pop(0)
        mine = (lax.axis_index("wide") // bit) % 2
        ahead = 1 - mine if self.backward else mine
        self.total, self.state, self.rows, self.sent = join(
            self.total, self.state, self.rows, self.got, jnp.reshape(ahead, (1,)).astype(jnp.int32)
        )

    def last(self):
        self.end()
        while self.left:
            self.begin()
            self.end()
        return self.state


def rms_scale(values, scales):
    return values * lax.rsqrt(jnp.mean(values * values, axis=-1, keepdims=True) + epsilon) * scales


def doc_index(starts, positions):
    passed = (starts[None, :] <= positions[:, None]).astype(jnp.int32)
    return jnp.sum(passed, axis=1) - 1


def split_at(array, sizes, axis):
    out, at = [], 0
    for size in sizes:
        out.append(lax.slice_in_dim(array, at, at + size, axis=axis))
        at += size
    return out


def packed(parts, rows):
    flat = jnp.concatenate([part.reshape(-1) for part in parts])
    columns = -(-flat.shape[0] // rows)
    return jnp.pad(flat, (0, rows * columns - flat.shape[0])).reshape(rows, columns)


CHUNK = 128
EXTRA = 16


def spread(value, spread_ref):
    return nn(jnp.concatenate(split_low(value, 2), axis=1), spread_ref[...])


def gathered(value, gather_ref):
    return nn(value.astype(LOW), gather_ref[...])


def gathered_fine(value, gather_ref):
    high, rest = split_low(value, 2)
    return nn(high, gather_ref[...]) + nn(rest, gather_ref[...])


def with_decay(state, decay):
    terms = split_low(decay, 3) + [jnp.zeros((EXTRA - 3, decay.shape[1]), LOW)]
    return jnp.concatenate([state.astype(LOW)] + terms, axis=0)


def silu_parts(value):
    sigma = jax.nn.sigmoid(value)
    return value * sigma, sigma * (1.0 + value * (1.0 - sigma))


def local_kernel(
    x_ref, xp_ref, bc_ref, bcp_ref, rimx_ref, rimb_ref, dt_ref, marks_ref, tapx_ref, tapb_ref, bias_ref, rate_ref, spread_ref,
    act_ref, slope_ref, bcact_ref, bcslope_ref, step_ref, cum_ref, sent_ref, state_ref, decay_ref,
):
    part = pl.program_id(0)
    marks = marks_ref[...]

    def conv(raw_ref, prev_ref, rim_ref, tap_ref):
        before = jnp.where(part == 0, rim_ref[...], prev_ref[...])
        both = jnp.concatenate([before, raw_ref[...]], axis=0)
        taps = 4
        total = None
        for i in range(taps):
            term = both[8 - taps + 1 + i : 8 - taps + 1 + i + CHUNK] * tap_ref[i : i + 1, :] * marks[:, i : i + 1]
            total = term if total is None else total + term
        return silu_parts(total)

    act, slope = conv(x_ref, xp_ref, rimx_ref, tapx_ref)
    act_ref[...] = act
    slope_ref[...] = slope.astype(LOW)
    bc, bc_slope = conv(bc_ref, bcp_ref, rimb_ref, tapb_ref)
    bcact_ref[...] = bc.astype(LOW)
    bcslope_ref[...] = bc_slope.astype(LOW)
    lane = lax.broadcasted_iota(jnp.int32, (CHUNK, LANES), 1)
    value = dt_ref[...] + bias_ref[0:1, :]
    softplus = jnp.maximum(value, 0.0) + jnp.log1p(jnp.exp(-jnp.abs(value)))
    step = jnp.where(rate_ref[0:1, :] < 0.0, softplus, 0.0)
    row = lax.broadcasted_iota(jnp.int32, (CHUNK, CHUNK), 0)
    col = lax.broadcasted_iota(jnp.int32, (CHUNK, CHUNK), 1)
    cum = jnp.dot((col <= row).astype(jnp.float32), step * rate_ref[0:1, :], precision=highest, preferred_element_type=jnp.float32)
    step_ref[...] = step
    cum_ref[...] = cum
    tail = jnp.exp(cum[CHUNK - 1 :] - cum) * marks[:, 5:6] * step
    weighted = (act * spread(tail, spread_ref)).astype(LOW)
    decay = spread(jnp.exp(cum[CHUNK - 8 :]) * marks[CHUNK - 8 :, 7:8], spread_ref)[7:8]
    own = tn(bc[:, :LANES].astype(LOW), weighted)

    @pl.when(part == 0)
    def _():
        state_ref[...] = own
        decay_ref[...] = jnp.ones_like(decay_ref)
        decay_ref[0:1, :] = decay

    @pl.when(part > 0)
    def _():
        state_ref[...] = state_ref[...] * decay + own
        decay_ref[0:1, :] = decay_ref[0:1, :] * decay

    @pl.when(part == pl.num_programs(0) - 1)
    def _():
        sent_ref[...] = with_decay(state_ref[...], decay_ref[0:1, :])


def join_kernel(ahead_ref, total_ref, state_ref, rows_ref, got_ref, total_out, state_out, rows_out, sent_out):
    size = total_ref.shape[0]
    got = got_ref[:size, :].astype(jnp.float32)
    extra = got_ref[size:, :].astype(jnp.float32)
    got_decay = extra[0:1] + extra[1:2] + extra[2:3]
    decay, sweep = rows_ref[0:1, :], rows_ref[1:2, :]
    rows_out[...] = jnp.ones_like(rows_out)
    rows_out[0:1, :] = decay * got_decay

    @pl.when(ahead_ref[0] == 1)
    def _():
        state_out[...] = state_ref[...] + sweep * got
        rows_out[1:2, :] = sweep * got_decay
        total_out[...] = total_ref[...] + decay * got

    @pl.when(ahead_ref[0] == 0)
    def _():
        state_out[...] = state_ref[...]
        rows_out[1:2, :] = sweep
        total_out[...] = got + got_decay * total_ref[...]

    sent_out[...] = with_decay(total_out[...], decay * got_decay)


def mix_kernel(
    act_ref, bcact_ref, z_ref, step_ref, cum_ref, marks_ref, docs_ref, first_ref, skip_ref, gain_ref, spread_ref, gather_ref,
    ym_ref, y_ref, entry_ref, state_ref, inner_ref,
):
    part = pl.program_id(0)

    @pl.when(part == 0)
    def _():
        state_ref[...] = first_ref[...]

    marks = marks_ref[...]
    cum = cum_ref[...]
    cum_rows = cum.T
    step = step_ref[...]
    b_mat = bcact_ref[:, :LANES]
    c_mat = bcact_ref[:, LANES:]
    act = act_ref[...]
    stepped = act * spread(step, spread_ref)
    low_stepped = stepped.astype(LOW)
    row = lax.broadcasted_iota(jnp.int32, (CHUNK, CHUNK), 0)
    col = lax.broadcasted_iota(jnp.int32, (CHUNK, CHUNK), 1)
    allowed = (row >= col) & (marks[:, 6:7] == docs_ref[0:1, :])
    gram = jnp.where(allowed, nt(c_mat, b_mat), 0.0)
    first = lax.broadcasted_iota(jnp.int32, (CHUNK, LANES), 1) < LANES // 2
    pairs = act.shape[1] // LANES
    for pair in range(pairs):
        parts = []
        for head in (2 * pair, 2 * pair + 1):
            gaps = jnp.minimum(cum[:, head : head + 1] - cum_rows[head : head + 1, :], 0.0)
            parts.append((jnp.exp(gaps) * gram).astype(LOW))
        values = low_stepped[:, pair * LANES : (pair + 1) * LANES]
        zero = jnp.zeros_like(values)
        inner_ref[:, pair * LANES : (pair + 1) * LANES] = nn(
            jnp.concatenate(parts, axis=1),
            jnp.concatenate([jnp.where(first, values, zero), jnp.where(first, zero, values)], axis=0),
        )
    state = state_ref[...]
    low_state = state.astype(LOW)
    entry_ref[0] = low_state
    entering = spread(jnp.exp(cum) * marks[:, 4:5], spread_ref)
    y = inner_ref[...] + nn(c_mat, low_state) * entering + skip_ref[0:1, :] * act
    y_ref[...] = y
    gated = y * silu_parts(z_ref[...])[0]
    scale = lax.rsqrt(gathered(gated * gated, gather_ref) * (2.0 / LANES) + epsilon)
    ym_ref[...] = (gated * spread(scale, spread_ref) * gain_ref[0:1, :]).astype(LOW)
    tail = jnp.exp(cum[CHUNK - 1 :] - cum) * marks[:, 5:6]
    weighted = (stepped * spread(tail, spread_ref)).astype(LOW)
    decay = spread(jnp.exp(cum[CHUNK - 8 :]) * marks[CHUNK - 8 :, 7:8], spread_ref)[7:8]
    state_ref[...] = state * decay + tn(b_mat, weighted)


def gate_back_kernel(
    dym_ref, y_ref, z_ref, bcact_ref, cum_ref, marks_ref, gain_ref, spread_ref, gather_ref,
    dz_ref, dy_ref, sent_ref, state_ref, decay_ref,
):
    part = pl.program_id(0)
    marks = marks_ref[...]
    cum = cum_ref[...]
    y = y_ref[...]
    silu, slope = silu_parts(z_ref[...])
    gated = y * silu
    scale = lax.rsqrt(gathered(gated * gated, gather_ref) * (2.0 / LANES) + epsilon)
    wide_scale = spread(scale, spread_ref)
    d_normed = dym_ref[...]
    u = d_normed * gain_ref[0:1, :]
    inner = gathered(u * gated, gather_ref) * (2.0 / LANES) * scale * scale * scale
    d_gated = u * wide_scale - gated * spread(inner, spread_ref)
    dz_ref[...] = (d_gated * y * slope).astype(LOW)
    dy = d_gated * silu
    dy_ref[...] = dy
    entering = spread(jnp.exp(cum) * marks[:, 4:5], spread_ref)
    own = tn(bcact_ref[:, LANES:], (dy * entering).astype(LOW))
    decay = spread(jnp.exp(cum[CHUNK - 8 :]) * marks[CHUNK - 8 :, 7:8], spread_ref)[7:8]

    @pl.when(part == 0)
    def _():
        state_ref[...] = own
        decay_ref[...] = jnp.ones_like(decay_ref)
        decay_ref[0:1, :] = decay

    @pl.when(part > 0)
    def _():
        state_ref[...] = state_ref[...] * decay + own
        decay_ref[0:1, :] = decay_ref[0:1, :] * decay

    @pl.when(part == pl.num_programs(0) - 1)
    def _():
        sent_ref[...] = with_decay(state_ref[...], decay_ref[0:1, :])


def scan_back_kernel(
    act_ref, slope_ref, bcact_ref, bcslope_ref, dt_ref, step_ref, cum_ref, marks_ref, docs_ref, dy_ref, entry_ref, first_ref,
    skip_ref, bias_ref, rate_ref, spread_ref, gather_ref, x_ref, xp_ref, bc_ref, bcp_ref, rimx_ref, rimb_ref, tapx_ref, tapb_ref,
    dscan_ref, dskip_ref, dhead_ref, dtap_ref, rim_ref, edge_ref, state_ref, inner_ref, rows_ref, next_ref, nextm_ref,
):
    part = pl.program_id(0)

    @pl.when(part == 0)
    def _():
        state_ref[...] = first_ref[...]
        rows_ref[...] = jnp.zeros_like(rows_ref)
        dskip_ref[...] = jnp.zeros_like(dskip_ref)
        dhead_ref[...] = jnp.zeros_like(dhead_ref)
        dtap_ref[...] = jnp.zeros_like(dtap_ref)
        next_ref[...] = jnp.zeros_like(next_ref)
        nextm_ref[...] = jnp.zeros_like(nextm_ref)

    marks = marks_ref[...]
    cum = cum_ref[...]
    cum_rows = cum.T
    step = step_ref[...]
    b_mat = bcact_ref[:, :LANES]
    c_mat = bcact_ref[:, LANES:]
    act = act_ref[...]
    wide_step = spread(step, spread_ref)
    stepped = act * wide_step
    low_stepped = stepped.astype(LOW)
    dy = dy_ref[...]
    low_dy = dy.astype(LOW)
    row = lax.broadcasted_iota(jnp.int32, (CHUNK, CHUNK), 0)
    col = lax.broadcasted_iota(jnp.int32, (CHUNK, CHUNK), 1)
    allowed = (row <= col) & (marks[:, 6:7] == docs_ref[0:1, :])
    gram = jnp.where(allowed, nt(b_mat, c_mat), 0.0)
    first = lax.broadcasted_iota(jnp.int32, (CHUNK, LANES), 1) < LANES // 2
    lane = lax.broadcasted_iota(jnp.int32, (CHUNK, LANES), 1)
    pairs = act.shape[1] // LANES
    d_gram = jnp.zeros((CHUNK, CHUNK), jnp.float32)
    leaving = jnp.zeros((CHUNK, LANES), jnp.float32)
    for pair in range(pairs):
        cols = slice(pair * LANES, (pair + 1) * LANES)
        values, grads = low_stepped[:, cols], low_dy[:, cols]
        zero = jnp.zeros_like(values)
        d_weights = nt(jnp.concatenate([jnp.where(first, values, zero), jnp.where(first, zero, values)], axis=0), grads)
        parts = []
        for i, head in enumerate((2 * pair, 2 * pair + 1)):
            fade = jnp.exp(jnp.minimum(cum_rows[head : head + 1, :] - cum[:, head : head + 1], 0.0))
            d_weight = d_weights[i * CHUNK : (i + 1) * CHUNK]
            weight = fade * gram
            d_gram = d_gram + d_weight * fade
            moved = d_weight * weight
            rows_ref[head : head + 1, :] = jnp.sum(moved, axis=0, keepdims=True)
            leaving = jnp.where(lane == head, jnp.sum(moved, axis=1, keepdims=True), leaving)
            parts.append(weight.astype(LOW))
        inner_ref[:, cols] = nn(
            jnp.concatenate(parts, axis=1),
            jnp.concatenate([jnp.where(first, grads, zero), jnp.where(first, zero, grads)], axis=0),
        )
    d_state = state_ref[...]
    low_d_state = d_state.astype(LOW)
    entry = entry_ref[0]
    entering = spread(jnp.exp(cum) * marks[:, 4:5], spread_ref)
    tail = spread(jnp.exp(cum[CHUNK - 1 :] - cum) * marks[:, 5:6], spread_ref)
    from_state = nn(b_mat, low_d_state) * tail
    d_stepped = inner_ref[...] + from_state
    out_moved = gathered_fine(stepped * from_state, gather_ref)
    entering_dy = dy * entering
    in_moved = gathered_fine(entering_dy * nn(c_mat, entry), gather_ref)
    low_entering_dy = entering_dy.astype(LOW)
    low_gram = jnp.where(allowed, d_gram, 0.0).astype(LOW)
    d_b = nt((stepped * tail).astype(LOW), low_d_state) + nn(low_gram, c_mat)
    d_c = nt(low_entering_dy, entry) + tn(low_gram, b_mat)
    decay_small = jnp.exp(cum[CHUNK - 8 :]) * marks[CHUNK - 8 :, 7:8]
    decay = spread(decay_small, spread_ref)[7:8]
    overlap = jnp.sum(d_state * entry.astype(jnp.float32), axis=0, keepdims=True)
    d_decay = nn(jnp.concatenate(split_low(jnp.broadcast_to(overlap, (8, overlap.shape[1])), 2), axis=0), gather_ref[...])
    at_end = jnp.sum(out_moved, axis=0, keepdims=True) + (d_decay[0:1] + d_decay[8:9]) * decay_small[7:8]
    d_cum = rows_ref[...].T - leaving + in_moved - out_moved
    d_cum = d_cum + jnp.where(lax.broadcasted_iota(jnp.int32, d_cum.shape, 0) == CHUNK - 1, at_end, 0.0)
    d_log = jnp.dot((row <= col).astype(jnp.float32), d_cum, precision=highest, preferred_element_type=jnp.float32)
    rate = rate_ref[0:1, :]
    d_step = gathered_fine(act * d_stepped, gather_ref) + d_log * rate
    d_dt = d_step * jax.nn.sigmoid(dt_ref[...] + bias_ref[0:1, :])
    d_dt = jnp.where(rate < 0.0, d_dt, 0.0)
    inner = act.shape[1]
    scan = inner + 2 * LANES
    dscan_ref[:, scan:] = d_dt.astype(LOW)
    dhead_ref[0:1, :] += jnp.sum(d_dt, axis=0, keepdims=True)
    dhead_ref[1:2, :] += jnp.sum(d_log * rate * step, axis=0, keepdims=True)
    dskip_ref[0:1, :] += jnp.sum(dy * act, axis=0, keepdims=True)
    taps = 4
    marks_ext = jnp.concatenate([marks, nextm_ref[...]], axis=0)

    def conv_back(d_pre, lanes, raw_ref, prev_ref, edge_raw_ref, tap_ref):
        before = jnp.where(part == pl.num_programs(0) - 1, edge_raw_ref[...], prev_ref[...])
        raw = jnp.concatenate([before, raw_ref[...]], axis=0)
        ext = jnp.concatenate([d_pre, next_ref[:, lanes]], axis=0)
        top = jnp.concatenate([jnp.zeros_like(ext[:8]), d_pre[:8]], axis=0)
        top_marks = jnp.concatenate([marks[:8], marks[:8]], axis=0)
        d_raw, rim = None, None
        for i in range(taps):
            ahead = taps - 1 - i
            tap = tap_ref[i : i + 1, :]
            masked = d_pre * marks[:, i : i + 1]
            dtap_ref[i : i + 1, lanes] += jnp.sum(masked * raw[8 - ahead : 8 - ahead + CHUNK], axis=0, keepdims=True)
            term = (ext * marks_ext[:, i : i + 1])[ahead : ahead + CHUNK] * tap
            d_raw = term if d_raw is None else d_raw + term
            if ahead:
                term = (top * top_marks[:, i : i + 1])[ahead : ahead + 8] * tap
                rim = term if rim is None else rim + term
        next_ref[:, lanes] = d_pre[:8]
        dscan_ref[:, lanes] = d_raw.astype(LOW)
        rim_ref[:, lanes] = rim

        @pl.when(part == 0)
        def _():
            edge_ref[:, lanes] = d_raw[CHUNK - 8 :]

    conv_back(
        (d_stepped * wide_step + dy * skip_ref[0:1, :]) * slope_ref[...].astype(jnp.float32),
        slice(0, inner), x_ref, xp_ref, rimx_ref, tapx_ref,
    )
    conv_back(
        jnp.concatenate([d_b, d_c], axis=1) * bcslope_ref[...].astype(jnp.float32),
        slice(inner, scan), bc_ref, bcp_ref, rimb_ref, tapb_ref,
    )
    nextm_ref[...] = marks[:8]
    state_ref[...] = d_state * decay + tn(c_mat, low_entering_dy)


def head_matrices(inner, heads):
    owner = jnp.arange(inner, dtype=jnp.int32) // (inner // heads)
    gather_m = (owner[:, None] == jnp.arange(LANES, dtype=jnp.int32)[None, :]).astype(LOW)
    return jnp.concatenate([gather_m.T, gather_m.T], axis=0), gather_m


def lanes_row(vector):
    return jnp.pad(vector, (0, LANES - vector.shape[0]))[None, :]


def call(kernel, name, us, parts, ins, outs, scratch, reverse=False):
    def spec(block, how):
        if how == "part":
            how = lambda c: (c,) + (0,) * (len(block) - 1)
        elif how == "whole":
            how = lambda c: (0,) * len(block)
        elif isinstance(how, int):
            column = how
            how = lambda c: (c, column)

        def index(c):
            return how(parts - 1 - c if reverse else c)

        return pl.BlockSpec(block, index)

    return pl.pallas_call(
        kernel,
        grid=(parts,),
        in_specs=[spec(block, how) for _, block, how in ins],
        out_specs=[spec(block, how) for _, block, how in outs],
        scratch_shapes=scratch,
        out_shape=[shape for shape, _, _ in outs],
        compiler_params=pltpu.CompilerParams(vmem_limit_bytes=56 * 2**20),
        cost_estimate=guess(us),
        name=name,
    )(*[array for array, _, _ in ins])


def mamba_local(raw, rim, marks, taps, bias, rate, cols, mats):
    length = raw.shape[0]
    parts = length // CHUNK
    inner, n2, x_at, bc_at, dt_at = cols
    before = CHUNK // 8

    def prev(column):
        return lambda c: (jnp.maximum(c * before - 1, 0), column)

    return call(
        local_kernel,
        "mamba_local",
        11,
        parts,
        [
            (raw, (CHUNK, inner), x_at),
            (raw, (8, inner), prev(x_at)),
            (raw, (CHUNK, n2), bc_at),
            (raw, (8, n2), prev(bc_at)),
            (rim[:, :inner], (8, inner), "whole"),
            (rim[:, inner:], (8, n2), "whole"),
            (raw, (CHUNK, LANES), dt_at),
            (marks, (CHUNK, LANES), "part"),
            (taps[:, :inner], (8, inner), "whole"),
            (taps[:, inner:], (8, n2), "whole"),
            (bias, (1, LANES), "whole"),
            (rate, (1, LANES), "whole"),
            (mats[0], mats[0].shape, "whole"),
        ],
        [
            (shape((length, inner)), (CHUNK, inner), "part"),
            (shape((length, inner), LOW), (CHUNK, inner), "part"),
            (shape((length, n2), LOW), (CHUNK, n2), "part"),
            (shape((length, n2), LOW), (CHUNK, n2), "part"),
            (shape((length, LANES)), (CHUNK, LANES), "part"),
            (shape((length, LANES)), (CHUNK, LANES), "part"),
            (shape((n2 // 2 + EXTRA, inner), LOW), (n2 // 2 + EXTRA, inner), "whole"),
            (shape((n2 // 2, inner)), (n2 // 2, inner), "whole"),
            (shape((8, inner)), (8, inner), "whole"),
        ],
        [],
    )


def mamba_mix(feats, raw, marks, docs, state, skip, gain, mats):
    act, slope, bcact, bcslope, step, cum = feats
    length, inner = act.shape
    parts = length // CHUNK
    n2 = bcact.shape[1]
    return call(
        mix_kernel,
        "mamba_mix",
        11,
        parts,
        [
            (act, (CHUNK, inner), "part"),
            (bcact, (CHUNK, n2), "part"),
            (raw, (CHUNK, inner), 0),
            (step, (CHUNK, LANES), "part"),
            (cum, (CHUNK, LANES), "part"),
            (marks, (CHUNK, LANES), "part"),
            (docs, (8, CHUNK), lambda c: (0, c)),
            (state, state.shape, "whole"),
            (skip, (1, inner), "whole"),
            (gain, (1, inner), "whole"),
            (mats[0], mats[0].shape, "whole"),
            (mats[1], mats[1].shape, "whole"),
        ],
        [
            (shape((length, inner), LOW), (CHUNK, inner), "part"),
            (shape((length, inner)), (CHUNK, inner), "part"),
            (shape((parts, n2 // 2, inner), LOW), (1, n2 // 2, inner), "part"),
        ],
        [pltpu.VMEM((n2 // 2, inner), jnp.float32), pltpu.VMEM((CHUNK, inner), jnp.float32)],
    )


def mamba_gate_back(d_normed, y, raw, feats, marks, gain, mats):
    act, slope, bcact, bcslope, step, cum = feats
    length, inner = act.shape
    parts = length // CHUNK
    n2 = bcact.shape[1]
    return call(
        gate_back_kernel,
        "mamba_gate_back",
        11,
        parts,
        [
            (d_normed, (CHUNK, inner), "part"),
            (y, (CHUNK, inner), "part"),
            (raw, (CHUNK, inner), 0),
            (bcact, (CHUNK, n2), "part"),
            (cum, (CHUNK, LANES), "part"),
            (marks, (CHUNK, LANES), "part"),
            (gain, (1, inner), "whole"),
            (mats[0], mats[0].shape, "whole"),
            (mats[1], mats[1].shape, "whole"),
        ],
        [
            (shape((length, inner), LOW), (CHUNK, inner), "part"),
            (shape((length, inner)), (CHUNK, inner), "part"),
            (shape((n2 // 2 + EXTRA, inner), LOW), (n2 // 2 + EXTRA, inner), "whole"),
            (shape((n2 // 2, inner)), (n2 // 2, inner), "whole"),
            (shape((8, inner)), (8, inner), "whole"),
        ],
        [],
        reverse=True,
    )


def mamba_scan_back(feats, raw, rim, taps, marks, docs, dy, entry, state, skip, bias, rate, cols, mats):
    act, slope, bcact, bcslope, step, cum = feats
    length, inner = act.shape
    parts = length // CHUNK
    n2 = bcact.shape[1]
    x_at, bc_at, dt_at = cols[2:]
    scan = inner + n2

    def prev(column):
        return lambda c: (jnp.maximum(c * (CHUNK // 8) - 1, 0), column)

    return call(
        scan_back_kernel,
        "mamba_scan_back",
        23,
        parts,
        [
            (act, (CHUNK, inner), "part"),
            (slope, (CHUNK, inner), "part"),
            (bcact, (CHUNK, n2), "part"),
            (bcslope, (CHUNK, n2), "part"),
            (raw, (CHUNK, LANES), dt_at),
            (step, (CHUNK, LANES), "part"),
            (cum, (CHUNK, LANES), "part"),
            (marks, (CHUNK, LANES), "part"),
            (docs, (8, CHUNK), lambda c: (0, c)),
            (dy, (CHUNK, inner), "part"),
            (entry, (1, n2 // 2, inner), "part"),
            (state, state.shape, "whole"),
            (skip, (1, inner), "whole"),
            (bias, (1, LANES), "whole"),
            (rate, (1, LANES), "whole"),
            (mats[0], mats[0].shape, "whole"),
            (mats[1], mats[1].shape, "whole"),
            (raw, (CHUNK, inner), x_at),
            (raw, (8, inner), prev(x_at)),
            (raw, (CHUNK, n2), bc_at),
            (raw, (8, n2), prev(bc_at)),
            (rim[:, :inner], (8, inner), "whole"),
            (rim[:, inner:], (8, n2), "whole"),
            (taps[:, :inner], (8, inner), "whole"),
            (taps[:, inner:], (8, n2), "whole"),
        ],
        [
            (shape((length, scan + LANES), LOW), (CHUNK, scan + LANES), "part"),
            (shape((8, inner)), (8, inner), "whole"),
            (shape((8, LANES)), (8, LANES), "whole"),
            (shape((8, scan)), (8, scan), "whole"),
            (shape((8, scan)), (8, scan), "whole"),
            (shape((8, scan)), (8, scan), "whole"),
        ],
        [
            pltpu.VMEM((n2 // 2, inner), jnp.float32),
            pltpu.VMEM((CHUNK, inner), jnp.float32),
            pltpu.VMEM((LANES, CHUNK), jnp.float32),
            pltpu.VMEM((8, scan), jnp.float32),
            pltpu.VMEM((8, LANES), jnp.float32),
        ],
        reverse=True,
    )


def join(total, state, rows, got, ahead):
    whole = pl.BlockSpec(memory_space=pltpu.VMEM)
    return pl.pallas_call(
        join_kernel,
        in_specs=[pl.BlockSpec(memory_space=pltpu.SMEM)] + [whole] * 4,
        out_specs=[whole] * 4,
        out_shape=[shape(total.shape), shape(total.shape), shape(rows.shape), shape(got.shape, LOW)],
        compiler_params=pltpu.CompilerParams(vmem_limit_bytes=32 * 2**20),
        cost_estimate=guess(2),
        name="join",
    )(ahead, total, state, rows, got)


BOTH = 4
ONES = 16


def causal(scores):
    key_row = lax.broadcasted_iota(jnp.int32, scores.shape, 0)
    query = lax.broadcasted_iota(jnp.int32, scores.shape, 1)
    return jnp.where(key_row <= query, scores, FAR)


def attend_kernel(place_ref, q_ref, far_ref, kv_ref, extra_ref, o_ref, qb_ref, keys_ref, values_ref, acc_ref):
    blk = q_ref.shape[2]
    last = place_ref[0]

    @pl.when(pl.program_id(0) == 0)
    def _():
        first = lax.broadcasted_iota(jnp.int32, (blk, LANES), 1) < HEAD_SIZE

        @pl.loop(0, last + 1)
        def _(block):
            rows = pl.ds(pl.multiple_of(block * blk, blk), blk)
            both = kv_ref[rows, :]
            keys_ref[rows, :] = jnp.where(first, both, extra_ref[rows, :])
            values_ref[:ONES, rows] = jnp.ones((ONES, blk), LOW)
            values_ref[ONES:, rows] = both.astype(jnp.float32).T[HEAD_SIZE:].astype(LOW)

    queries = [
        jnp.concatenate([q_ref[i] * jnp.asarray(HEAD_SIZE ** (-0.5), LOW), far_ref[...]], axis=0)
        for i in range(BOTH)
    ]
    acc_ref[...] = jnp.zeros_like(acc_ref)

    def step(block, tops, diagonal):
        rows = pl.ds(pl.multiple_of(block * blk, blk), blk)
        keys, values = keys_ref[rows, :], values_ref[:, rows]
        new_tops = []
        for i in range(BOTH):
            scores = nn(keys, queries[i])
            if diagonal:
                scores = causal(scores)
            new_top = jnp.maximum(tops[i], jnp.max(scores, axis=0, keepdims=True))
            probs = jnp.exp(scores - new_top).astype(LOW)
            acc_ref[i] = acc_ref[i] * jnp.exp(tops[i] - new_top) + nn(values, probs)
            new_tops.append(new_top)
        return tuple(new_tops)

    tops = (jnp.full((1, blk), FAR, jnp.float32),) * BOTH
    tops = lax.fori_loop(0, last, lambda block, tops: step(block, tops, False), tops)
    tops = step(last, tops, True)
    row = lax.broadcasted_iota(jnp.int32, (HEAD_SIZE, blk), 0)
    for i in range(BOTH):
        total = acc_ref[i, 0:1, :]
        o_ref[i] = acc_ref[i, ONES:, :] / total
        extra = far_ref[...].astype(jnp.float32)
        for at, term in enumerate(split_low(-(tops[i] + jnp.log(total)), 3)):
            extra = jnp.where(row == 4 + at, term.astype(jnp.float32), extra)
        qb_ref[i] = jnp.concatenate([queries[i][:HEAD_SIZE], extra.astype(LOW)], axis=0)


def attend_back_kernel(place_ref, qb_ref, dot_ref, o_ref, kv_ref, extra_ref, dq_ref, dkv_ref, keys_ref, rows_ref, values_ref, acc_ref, dqa_ref):
    blk = qb_ref.shape[2]
    last = place_ref[0]
    member = pl.program_id(0)

    @pl.when(member == 0)
    def _():
        acc_ref[...] = jnp.zeros_like(acc_ref)
        lane = lax.broadcasted_iota(jnp.int32, (blk, LANES), 1)
        ones = jnp.where(lane < 3, 1.0, 0.0).astype(LOW)

        @pl.loop(0, last + 1)
        def _(block):
            rows = pl.ds(pl.multiple_of(block * blk, blk), blk)
            both = kv_ref[rows, :]
            keys_ref[rows, :] = jnp.where(lane < HEAD_SIZE, both, extra_ref[rows, :])
            values_ref[rows, :] = jnp.where(lane < HEAD_SIZE, ones, both)
            rows_ref[:, rows] = both.astype(jnp.float32).T[:HEAD_SIZE].astype(LOW)

    row = lax.broadcasted_iota(jnp.int32, (HEAD_SIZE, blk), 0)
    none = jnp.zeros((HEAD_SIZE, blk), jnp.float32)
    queries, d_outs, pairs = [], [], []
    for i in range(BOTH):
        queries.append(qb_ref[i])
        d_out = dot_ref[i].astype(jnp.float32)
        row_dot = jnp.sum(d_out * o_ref[i], axis=0, keepdims=True)
        extra = none
        for at, term in enumerate(split_low(-row_dot, 3)):
            extra = jnp.where(row == at, term.astype(jnp.float32), extra)
        d_outs.append(jnp.concatenate([extra, d_out], axis=0).astype(LOW))
        q_part = jnp.concatenate([qb_ref[i, :HEAD_SIZE, :].astype(jnp.float32), none], axis=0)
        pairs.append(jnp.concatenate([q_part.T, jnp.concatenate([none, d_out], axis=0).T], axis=0).astype(LOW))
    dqa_ref[...] = jnp.zeros_like(dqa_ref)

    def step(block, diagonal):
        rows = pl.ds(pl.multiple_of(block * blk, blk), blk)
        keys, values, key_rows = keys_ref[rows, :], values_ref[rows, :], rows_ref[:, rows]
        total = acc_ref[rows, :]
        for i in range(BOTH):
            logs = nn(keys, queries[i])
            if diagonal:
                logs = causal(logs)
            probs = jnp.exp(logs)
            d_scores = (probs * nn(values, d_outs[i])).astype(LOW)
            total = total + nn(jnp.concatenate([d_scores, probs.astype(LOW)], axis=1), pairs[i])
            dqa_ref[i] += nn(key_rows, d_scores)
        acc_ref[rows, :] = total

    @pl.loop(0, last)
    def _(block):
        step(block, False)

    step(last, True)
    dq_ref[...] = (dqa_ref[...] * HEAD_SIZE ** (-0.5)).astype(LOW)

    @pl.when(member == GROUP // BOTH - 1)
    def _():
        dkv_ref[...] = acc_ref[...].astype(LOW)


def attend_specs(blk, total, group):
    mine = group * (GROUP // BOTH)
    return dict(
        narrow=pl.BlockSpec((BOTH, HEAD_SIZE, blk), lambda r, p: (mine + r, 0, 0)),
        own_narrow=pl.BlockSpec((BOTH, HEAD_SIZE, blk), lambda r, p: (r, 0, 0)),
        own_broad=pl.BlockSpec((BOTH, LANES, blk), lambda r, p: (r, 0, 0)),
        kv=pl.BlockSpec((total, LANES), lambda r, p: (0, group)),
        extra=pl.BlockSpec((total, LANES), lambda r, p: (0, 0)),
        far=pl.BlockSpec((HEAD_SIZE, blk), lambda r, p: (0, 0)),
    )


def attend_masks(doc_here, key_doc, doc_count):
    docs = jnp.arange(HEAD_SIZE, dtype=jnp.int32)
    far = jnp.where((docs[:, None] != doc_here[None, :]) & (docs[:, None] < doc_count), FAR, 0.0).astype(LOW)
    lane = jnp.arange(LANES, dtype=jnp.int32)[None, :] - HEAD_SIZE
    extra = ((key_doc[:, None] == lane) | ((lane >= doc_count) & (lane < doc_count + 3))).astype(LOW)
    return far, extra


def attend(group, q_rows, key_all, masks, place):
    blk = q_rows.shape[2]
    total = key_all.shape[0]
    specs = attend_specs(blk, total, group)
    return pl.pallas_call(
        attend_kernel,
        grid_spec=pltpu.PrefetchScalarGridSpec(
            num_scalar_prefetch=1,
            grid=(GROUP // BOTH,),
            in_specs=[specs["narrow"], specs["far"], specs["kv"], specs["extra"]],
            out_specs=[specs["own_narrow"], specs["own_broad"]],
            scratch_shapes=[
                pltpu.VMEM((total, LANES), LOW),
                pltpu.VMEM((HEAD_SIZE + ONES, total), LOW),
                pltpu.VMEM((BOTH, HEAD_SIZE + ONES, blk), jnp.float32),
            ],
        ),
        out_shape=[shape((GROUP, HEAD_SIZE, blk)), shape((GROUP, LANES, blk), LOW)],
        compiler_params=pltpu.CompilerParams(vmem_limit_bytes=56 * 2**20),
        cost_estimate=guess(17),
        name="attend",
    )(place, q_rows, masks[0], key_all, masks[1])


def attend_back(group, q_back, out, d_rows, key_all, masks, place):
    blk = d_rows.shape[2]
    total = key_all.shape[0]
    specs = attend_specs(blk, total, group)
    return pl.pallas_call(
        attend_back_kernel,
        grid_spec=pltpu.PrefetchScalarGridSpec(
            num_scalar_prefetch=1,
            grid=(GROUP // BOTH,),
            in_specs=[specs["own_broad"], specs["narrow"], specs["own_narrow"], specs["kv"], specs["extra"]],
            out_specs=[specs["own_narrow"], specs["extra"]],
            scratch_shapes=[
                pltpu.VMEM((total, LANES), LOW),
                pltpu.VMEM((HEAD_SIZE, total), LOW),
                pltpu.VMEM((total, LANES), LOW),
                pltpu.VMEM((total, LANES), jnp.float32),
                pltpu.VMEM((BOTH, HEAD_SIZE, blk), jnp.float32),
            ],
        ),
        out_shape=[shape((GROUP, HEAD_SIZE, blk), LOW), shape((total, LANES), LOW)],
        compiler_params=pltpu.CompilerParams(vmem_limit_bytes=60 * 2**20),
        cost_estimate=guess(27),
        name="attend_back",
    )(place, q_back, d_rows, out, key_all, masks[1])


PIECE = 256


def feed_kernel(x_ref, gy_ref, plain_ref, w_ref, out_ref, dx_ref, grad_ref, xt_ref):
    fold = w_ref.shape[1] // 3

    @pl.when(pl.program_id(0) == 0)
    def _():
        out_ref[...] = jnp.zeros_like(out_ref)
        dx_ref[...] = jnp.zeros_like(dx_ref)
        xt_ref[...] = x_ref[...].astype(jnp.float32).T.astype(LOW)

    @pl.loop(0, fold // PIECE)
    def _(piece):
        at = pl.multiple_of(piece * PIECE, PIECE)
        gate_cols = pl.ds(at, PIECE)
        up_cols = pl.ds(pl.multiple_of(fold + at, PIECE), PIECE)
        down_cols = pl.ds(2 * fold, fold)
        w_gate, w_up, w_down = w_ref[:, gate_cols], w_ref[:, up_cols], w_ref[gate_cols, down_cols]
        x, gy = x_ref[...], gy_ref[...]
        gate, up = nn(x, w_gate), nn(x, w_up)
        sigma = jax.nn.sigmoid(gate)
        silu = gate * sigma
        act = silu * up
        d_act = nt(gy, w_down)
        d_gate = (d_act * up * sigma * (1.0 + gate * (1.0 - sigma))).astype(LOW)
        d_up = (d_act * silu).astype(LOW)
        out_ref[...] += nn(act.astype(LOW), w_down)
        dx_ref[...] += nt(d_gate, w_gate) + nt(d_up, w_up)
        x_t = xt_ref[...]
        grad_ref[:, gate_cols] = nn(x_t, d_gate).astype(LOW)
        grad_ref[:, up_cols] = nn(x_t, d_up).astype(LOW)
        grad_ref[gate_cols, down_cols] = nn(act.T.astype(LOW), plain_ref[...]).astype(LOW)


def feed_forward(x, gy, plain, w, folds, fold):
    tokens, width = x.shape
    whole = pl.BlockSpec((tokens, width), lambda j: (0, 0))
    return pl.pallas_call(
        feed_kernel,
        grid=(folds,),
        in_specs=[whole, whole, whole, pl.BlockSpec((width, 3 * fold), lambda j: (0, j))],
        out_specs=[whole, whole, pl.BlockSpec((width, 3 * fold), lambda j: (0, j))],
        out_shape=[
            shape((tokens, width)),
            shape((tokens, width)),
            shape((width, 3 * fold * folds), LOW),
        ],
        scratch_shapes=[pltpu.VMEM((width, tokens), LOW)],
        compiler_params=pltpu.CompilerParams(vmem_limit_bytes=60 * 2**20),
        cost_estimate=guess(35),
        name="feed_forward",
    )(x, gy, plain, w)


def last_grads_kernel(x_ref, scan_ref, query_ref, kv_ref, small_ref, grad_ref):
    x_t = x_ref[...].astype(jnp.float32).T.astype(LOW)
    scan = scan_ref.shape[1]
    query = query_ref.shape[1]
    grad_ref[:, : scan - LANES] = nn(x_t, scan_ref[:, : scan - LANES]).astype(LOW)
    grad_ref[:, scan - LANES : scan] = (nn(x_t, scan_ref[:, scan - LANES :]) + small_ref[...]).astype(LOW)
    grad_ref[:, scan : scan + query] = nn(x_t, query_ref[...]).astype(LOW)
    grad_ref[:, scan + query :] = nn(x_t, kv_ref[...]).astype(LOW)


def last_grads(x, d_scan, d_query, d_kv, small):
    tokens, width = x.shape
    count = d_scan.shape[1] + d_query.shape[1] + d_kv.shape[1]
    return pl.pallas_call(
        last_grads_kernel,
        out_shape=shape((width, count), LOW),
        compiler_params=pltpu.CompilerParams(vmem_limit_bytes=56 * 2**20),
        cost_estimate=guess(8),
        name="last_grads",
    )(x, d_scan, d_query, d_kv, small)


def input_back_kernel(scan_ref, gate_ref, query_ref, kv_ref, w_ref, x_ref, more_ref, gain_ref, dx_ref):
    at, total = 0, None
    for ref in (scan_ref, gate_ref, query_ref, kv_ref):
        term = nt(ref[...], w_ref[:, at : at + ref.shape[1]])
        total = term if total is None else total + term
        at += ref.shape[1]
    x = x_ref[...]
    scale = lax.rsqrt(jnp.mean(x * x, axis=1, keepdims=True) + epsilon)
    u = total * gain_ref[...]
    inner = jnp.mean(u * x, axis=1, keepdims=True) * scale * scale * scale
    dx_ref[...] = (more_ref[...] + u * scale - x * inner).astype(LOW)


def input_back(d_scan, d_gate, d_query, d_kv, w, x, more, gain):
    tokens, width = x.shape
    part = min(2 * CHUNK, tokens)
    rows = lambda array: pl.BlockSpec((part, array.shape[1]), lambda i: (i, 0))
    whole = lambda array: pl.BlockSpec(array.shape, lambda i: (0, 0))
    return pl.pallas_call(
        input_back_kernel,
        grid=(tokens // part,),
        in_specs=[rows(a) for a in (d_scan, d_gate, d_query, d_kv)] + [whole(w), rows(x), rows(more), whole(gain)],
        out_specs=rows(x),
        out_shape=shape((tokens, width), LOW),
        compiler_params=pltpu.CompilerParams(vmem_limit_bytes=56 * 2**20),
        cost_estimate=guess(10),
        name="input_back",
    )(d_scan, d_gate, d_query, d_kv, w, x, more, gain)


def owned_kernel(count_ref, own_ref, a_ref, b_ref, c_ref, gain_ref, gate_ref, x_ref, bc_ref, dt_ref, query_ref, kv_ref, *outs):
    total = own_ref[...].astype(jnp.float32) * count_ref[0].astype(jnp.float32)
    total = total + a_ref[...].astype(jnp.float32) + b_ref[...].astype(jnp.float32) + c_ref[...].astype(jnp.float32)
    at, inner = 0, gate_ref[...]
    for weight_ref, out_ref in zip((x_ref, bc_ref, dt_ref, query_ref, kv_ref), outs):
        part = total[:, at : at + out_ref.shape[1]]
        out_ref[...] = part
        heads = weight_ref.shape[1]
        inner = inner + jnp.sum(weight_ref[...].astype(jnp.float32) * part[:, :heads], axis=1, keepdims=True)
        at += out_ref.shape[1]
    outs[-1][...] = inner / gain_ref[...].astype(jnp.float32)


def owned_last(own, got, counts, gain, gate, weights, sizes):
    rows = own.shape[0]
    arrays = (own, *got, gain, gate, *weights)
    whole = lambda dims: pl.BlockSpec(dims, lambda i: (0, 0))
    return pl.pallas_call(
        owned_kernel,
        grid=(1,),
        in_specs=[pl.BlockSpec(memory_space=pltpu.SMEM)] + [whole(array.shape) for array in arrays],
        out_specs=[whole((rows, size)) for size in sizes] + [whole((rows, 1))],
        out_shape=[shape((rows, size)) for size in sizes] + [shape((rows, 1))],
        compiler_params=pltpu.CompilerParams(vmem_limit_bytes=16 * 2**20),
        cost_estimate=guess(3),
        name="owned_last",
    )(counts, *arrays)


def tap_marks(starts, first, length, taps):
    ext = doc_index(starts, first - (taps - 1) + jnp.arange(length + taps - 1, dtype=jnp.int32))
    return jnp.stack([(ext[i : i + length] == ext[taps - 1 :]).astype(jnp.float32) for i in range(taps)], axis=1)


def marks_of(starts, block_base, length, taps):
    ext = doc_index(starts, block_base - (taps - 1) + jnp.arange(length + taps - 1, dtype=jnp.int32))
    here = ext[taps - 1 :]
    chunks = here.reshape(-1, CHUNK)
    ahead = ext[taps - 2 : taps - 2 + length].reshape(-1, CHUNK)[:, :1]
    last = chunks[:, -1:]
    columns = [ext[i : i + length] == here for i in range(taps)] + [
        (chunks == ahead).reshape(-1),
        (chunks == last).reshape(-1),
        here,
        jnp.broadcast_to(last == ahead, chunks.shape).reshape(-1),
    ]
    marks = jnp.stack([column.astype(jnp.float32) for column in columns], axis=1)
    marks = jnp.pad(marks, ((0, 0), (0, LANES - len(columns))))
    return marks, jnp.broadcast_to(here.astype(jnp.float32)[None], (8, length)), here


def per_device(
    hidden_in,
    cotangent,
    doc_starts,
    gain_in,
    mamba_gate_w,
    mamba_in_w,
    mamba_bc_w,
    mamba_dt_w,
    dt_bias,
    a_log,
    d_skip,
    conv_x,
    conv_bc,
    mamba_gain,
    attn_q_w,
    attention_key_value_weight,
    mamba_out_w,
    attn_out_w,
    gain_ffn,
    ffn_gate_w,
    ffn_up_w,
    ffn_down_w,
):
    devices = lax.axis_size("head") * lax.axis_size("wide")
    wide_id = lax.axis_index("wide")
    micro_count = hidden_in.shape[0]
    block_tok = hidden_in.shape[2] * lax.axis_size("head")
    taps = conv_x.shape[0]
    heads = dt_bias.shape[0]
    rows, inner = mamba_gate_w.shape
    width = rows * devices
    bc_cols = mamba_bc_w.shape[1]
    query_cols = attn_q_w.shape[1]
    kv_cols = attention_key_value_weight.shape[1]
    hidden = ffn_gate_w.shape[1]
    out_rows = mamba_out_w.shape[0]
    attn_rows = attn_out_w.shape[0]
    chan = conv_x.shape[1]
    chan_bc = conv_bc.shape[1]

    scan_cols = inner + bc_cols
    first_cols = scan_cols + LANES

    heads_dev, wide_dev = lax.axis_size("head"), lax.axis_size("wide")
    folds = hidden // width
    feature = jnp.arange(width, dtype=jnp.int32)
    inside = (feature // rows) % wide_dev * heads_dev + feature // (rows * wide_dev)
    order = (inside[:, None] * rows + (feature % rows)[:, None] == feature[None, :]).astype(LOW)

    def mixed(array):
        return nn(array.reshape(-1, width), order).astype(LOW).reshape(array.shape)

    def plain(array):
        return nt(array.reshape(-1, width), order).astype(LOW).reshape(array.shape)

    def by_place(array):
        return array.reshape((heads_dev, wide_dev) + array.shape[1:]).swapaxes(0, 1).reshape(array.shape)

    def by_owner(array):
        return array.reshape((wide_dev, heads_dev) + array.shape[1:]).swapaxes(0, 1).reshape(array.shape)

    def folded(weight):
        return weight.reshape(rows, heads_dev, wide_dev, folds, rows).transpose(0, 3, 2, 1, 4).reshape(rows, folds, width)

    def unfolded(parts):
        unit = jnp.arange(hidden, dtype=jnp.int32)
        owner, fold, row = unit // (folds * rows), unit // rows % folds, unit % rows
        at = (owner % wide_dev * heads_dev + owner // wide_dev) * rows + row
        total = 0.0
        for i, part in enumerate(parts):
            one_hot = ((feature[:, None] == at[None, :]) & (fold == i)[None, :]).astype(LOW)
            total = total + nn(jnp.concatenate(split_low(part, 3), axis=0), one_hot)
        high, middle, low = split_at(total, (rows,) * 3, 0)
        return high + (middle + low)

    small = packed([gain_in, gain_ffn, mamba_gain, conv_x, conv_bc], rows)
    small_cols = small.shape[1]
    pad = jnp.zeros((rows, LANES - heads - small_cols), LOW)
    in_shard = jnp.concatenate(
        [mamba_in_w, mamba_bc_w, mamba_dt_w, small, pad, mamba_gate_w, attn_q_w, attention_key_value_weight], axis=1
    )
    to_width = mixed(jnp.concatenate([ffn_down_w, mamba_out_w, attn_out_w], axis=0)).reshape(-1, rows, width)
    gate_folds, up_folds = folded(ffn_gate_w), folded(ffn_up_w)
    ffn_shard = []
    for i in range(folds):
        ffn_shard += [gate_folds[:, i], up_folds[:, i], to_width[i]]
    ffn_shard = jnp.concatenate(ffn_shard, axis=1)
    out_shard = jnp.concatenate([to_width[i] for i in range(folds, to_width.shape[0])], axis=1)
    x_pieces = mixed(hidden_in[:, 0])

    micro = jnp.minimum(lax.axis_index("head"), micro_count - 1)
    starts = pick(doc_starts, micro)
    block_base = wide_id * block_tok
    marks, docs_row, doc_here = marks_of(starts, block_base, block_tok, taps)
    key_doc = doc_index(starts, jnp.arange(block_tok * lax.axis_size("wide"), dtype=jnp.int32))
    masks = attend_masks(doc_here, key_doc, doc_starts.shape[1])
    mats = head_matrices(inner, heads)
    bias_row = lanes_row(dt_bias)
    rate_row = lanes_row(-jnp.exp(a_log))
    skip_row = jnp.repeat(d_skip, inner // heads)[None]
    in_rows = HeadRows(in_shard, micro_count)
    prepared = (marks, docs_row, masks, mats, bias_row, rate_row, skip_row, ffn_shard, out_shard, x_pieces)
    in_rows.got, prepared = tied(in_rows.got, prepared)
    marks, docs_row, masks, mats, bias_row, rate_row, skip_row, ffn_shard, out_shard, x_pieces = prepared
    in_rows, out_shard = tied(in_rows.end(), out_shard)
    w_in = gather_wide(in_rows)
    out_rows_all, x_pieces = tied(HeadRows(out_shard, micro_count).end(), x_pieces)
    x_low, ffn_shard = tied(ToBlocks(x_pieces).end(), ffn_shard)
    ffn_rows = HeadRows(ffn_shard, micro_count)
    w_in, out_rows_all = tied(w_in, out_rows_all)
    w_out = gather_wide(out_rows_all)
    x_tokens = x_low.astype(jnp.float32)

    small_at = scan_cols + heads
    w_scan, w_gate, w_qkv = split_at(w_in, (first_cols, inner, query_cols + kv_cols), 1)
    small_all = w_scan[:, small_at : small_at + small_cols].reshape(devices, -1).astype(jnp.float32)
    g_in, g_ffn, g_mamba, c_x, c_bc = split_at(
        small_all, (rows, rows, chan, taps * chan, taps * chan_bc), 1
    )
    gain_in_all = g_in.reshape(-1)
    gain_ffn_all = g_ffn.reshape(-1)
    g_mamba, c_x, c_bc = by_owner(g_mamba), by_owner(c_x), by_owner(c_bc)
    gain_mamba_row = g_mamba.reshape(1, -1)
    taps_all = jnp.concatenate(
        [
            c_x.reshape(devices, taps, chan).transpose(1, 0, 2).reshape(taps, -1),
            c_bc.reshape(devices, taps, chan_bc).transpose(1, 0, 2).reshape(taps, -1),
        ],
        axis=1,
    )
    cols = (inner, bc_cols, 0, inner // bc_cols, scan_cols // LANES)
    place = jnp.reshape(wide_id, (1,)).astype(jnp.int32)


    block_in = rms_scale(x_tokens, gain_in_all).astype(LOW)
    raw_qkv, block_in = tied(nn(block_in, w_qkv).astype(LOW), block_in)
    keys = Gathered(raw_qkv[:, query_cols:])
    keys.begin()
    keys.got, raw_scan, block_in = tied(keys.got, nn(block_in, w_scan), block_in)
    keys.end()
    rim = shifted(raw_scan[block_tok - 8 :, :scan_cols], "wide", 1)
    keys.begin()
    rim, raw_gate = tied(rim, nn(block_in, w_gate))
    rim = jnp.where(jnp.arange(8)[:, None] > 8 - taps, rim, 0.0)
    taps_ext = jnp.pad(taps_all, ((0, 8 - taps), (0, 0)))
    *feats, sent, total, decay_rows = mamba_local(raw_scan, rim, marks, taps_ext, bias_row, rate_row, cols, mats)
    keys.got, ffn_rows.got, sent = tied(keys.got, ffn_rows.got, sent)
    ffn_rows, w_out = tied(ffn_rows.end(), w_out)
    w_ffn = gather_wide(ffn_rows)
    keys.end()
    forward = Carried(sent, total, decay_rows, False)
    forward.begin()
    key_all = keys.rest()
    forward.end()
    q_rows = raw_qkv[:, :query_cols].T.reshape(QUERY_HEADS, HEAD_SIZE, block_tok)
    gy = ToBlocks(cotangent[:, 0])
    forward.begin()
    out_0, q_back_0 = attend(0, q_rows, key_all, masks, place)
    forward.got, gy.got, out_0, q_rows = tied(forward.got, gy.got, out_0, q_rows)
    forward.end()
    forward.sent, q_rows = tied(forward.sent, q_rows)
    forward.begin()
    out_1, q_back_1 = attend(1, q_rows, key_all, masks, place)
    forward.got, out_1 = tied(forward.got, out_1)
    state_in = forward.last()
    attn_low = jnp.concatenate([out_0, out_1], axis=0).reshape(query_cols, block_tok).astype(LOW)
    mamba_low, y_low, entry = mamba_mix(feats, raw_gate, marks, docs_row, state_in, skip_row, gain_mamba_row, mats)
    gy_plain = gy.end()
    d_out_low = mixed(gy_plain)
    out_both = jnp.concatenate(
        [w_out[:, i : i + width].reshape(devices, rows, width) for i in range(0, w_out.shape[1], width)], axis=1
    )
    out_both = by_owner(out_both)
    w_mamba_out = out_both[:, :out_rows].reshape(-1, width)
    w_attn_out = out_both[:, out_rows:].reshape(-1, width)

    resid = x_tokens + nn(mamba_low, w_mamba_out) + tn(attn_low, w_attn_out)
    normed_ffn, pull_ffn = jax.vjp(lambda values: rms_scale(values, gain_ffn_all), resid)
    ffn_in = normed_ffn.astype(LOW)
    fed, d_ffn_in, grad_ffn = feed_forward(ffn_in, d_out_low, gy_plain, w_ffn, folds, width)
    part_ffn = sum_wide(grad_ffn)
    out_low = (resid + fed).astype(LOW)
    (d_resid_norm,) = pull_ffn(d_ffn_in)
    d_resid = d_out_low.astype(jnp.float32) + d_resid_norm

    d_mix = d_resid.astype(LOW)
    d_gate_z, dy_low, sent_back, total, decay_rows = mamba_gate_back(
        nt(d_mix, w_mamba_out), y_low, raw_gate, feats, marks, gain_mamba_row, mats
    )
    backward = Carried(sent_back, total, decay_rows, True)
    backward.begin()
    d_attn = nt(w_attn_out, d_mix).astype(LOW).reshape(QUERY_HEADS, HEAD_SIZE, block_tok)
    backward.got, d_attn = tied(backward.got, d_attn)
    backward.end()
    backward.sent, d_attn = tied(backward.sent, d_attn)
    backward.begin()
    d_query_0, d_kv_0 = attend_back(0, q_back_0, out_0, d_attn, key_all, masks, place)
    backward.got, d_query_0, d_kv_0, d_attn = tied(backward.got, d_query_0, d_kv_0, d_attn)
    backward.end()
    backward.sent, d_attn, d_kv_0 = tied(backward.sent, d_attn, d_kv_0)
    backward.begin()
    core_0 = CoreSum(d_kv_0)
    d_query_1, d_kv_1 = attend_back(1, q_back_1, out_1, d_attn, key_all, masks, place)
    backward.got, core_0.got, d_query_1, d_kv_1 = tied(backward.got, core_0.got, d_query_1, d_kv_1)
    d_state = backward.last()
    d_state, d_kv_1, d_mix = tied(d_state, d_kv_1, d_mix)
    core_1 = CoreSum(d_kv_1)
    d_query = jnp.concatenate([d_query_0, d_query_1], axis=0).reshape(query_cols, block_tok).T
    d_mix_plain = plain(d_mix)
    grad_out = jnp.concatenate(
        [
            tn(mamba_low, d_mix_plain).astype(LOW).reshape(devices, out_rows, width),
            nn(attn_low, d_mix_plain).astype(LOW).reshape(devices, attn_rows, width),
        ],
        axis=1,
    ).reshape(devices, -1, rows, width)
    grad_out = by_place(grad_out)
    grad_gate = tn(block_in, d_gate_z).astype(LOW)
    early = jnp.concatenate(
        [grad_out[:, i].reshape(width, width) for i in range(grad_out.shape[1])] + [grad_gate], axis=1
    )
    core_1.got, early = tied(core_1.got, early)
    chip_sum = ChipSum(jnp.concatenate([core_0.end(), core_1.end()], axis=2))
    early, part_ffn = tied(early, part_ffn)
    part_early = sum_wide(early)
    own_ffn = HeadSum(part_ffn, micro_count)
    d_scan, grad_skip, grad_head, grad_taps, rim_back, edge = mamba_scan_back(
        feats, raw_scan, rim, taps_ext, marks, docs_row, dy_low, entry, d_state,
        skip_row, bias_row, rate_row, cols, mats,
    )
    chip_sum.got, own_ffn.got, d_scan, edge, rim_back, grad_taps, grad_head, grad_skip, d_query, out_low = tied(
        chip_sum.got, own_ffn.got, d_scan, edge, rim_back, grad_taps, grad_head, grad_skip, d_query, out_low
    )
    rim_came = shifted(rim_back, "wide", -1)
    out_back = FromBlocks(out_low, micro_count)
    d_kv = chip_sum.end()
    own_ffn = own_ffn.end()
    d_scan = lax.dynamic_update_slice(d_scan, (edge + rim_came).astype(LOW), (block_tok - 8, 0))
    grad_small = jnp.concatenate(
        [
            by_place(grad_taps[:taps, :inner].reshape(taps, devices, chan).transpose(1, 0, 2).reshape(devices, -1)),
            by_place(grad_taps[:taps, inner:].reshape(taps, devices, chan_bc).transpose(1, 0, 2).reshape(devices, -1)),
        ],
        axis=1,
    )
    grad_small = jnp.pad(grad_small, ((0, 0), (0, rows * small_cols - grad_small.shape[1])))
    grad_small = jnp.pad(
        grad_small.reshape(width, small_cols), ((0, 0), (heads, LANES - heads - small_cols))
    )
    late = last_grads(block_in, d_scan, d_query, d_kv, grad_small)

    head_sums = jnp.concatenate(
        [grad_head[:2, :heads].reshape(-1), jnp.sum(grad_skip[0].reshape(heads, -1), axis=1)]
    )
    out_back.got, late, part_early, d_scan, own_ffn, head_sums = tied(
        out_back.got, late, part_early, d_scan, own_ffn, head_sums
    )
    part_late = sum_wide(late)
    totals = EverySum(head_sums)
    totals.begin()
    totals.got, part_early, d_scan = tied(totals.got, part_early, d_scan)
    totals.end()
    own_early = HeadSum(part_early, micro_count)
    totals.begin()
    grad_x = input_back(d_scan, d_gate_z, d_query, d_kv, w_in, x_tokens, d_resid, gain_in_all[None])
    own_early.got, own_early.own, totals.got, grad_x = tied(own_early.got, own_early.own, totals.got, grad_x)
    totals.end()
    x_plain, own_ffn = tied(plain(grad_x), own_ffn)
    x_back = FromBlocks(x_plain, micro_count)
    totals.begin()
    g_ffn = split_at(own_ffn, (width,) * (3 * folds), 1)
    g_gate_w, g_up_w = unfolded(g_ffn[0::3]), unfolded(g_ffn[1::3])
    totals.got, g_gate_w, g_up_w = tied(totals.got, g_gate_w, g_up_w)
    totals.end()
    totals.begin()
    *g_out, g_gate = own_early.end((width,) * ((out_rows + attn_rows) // rows) + (inner,))
    out_done = plain(out_back.end())
    x_back.got, g_out, g_gate, out_done, part_late, totals.got, g_gate_w, g_up_w = tied(
        x_back.got, g_out, g_gate, out_done, part_late, totals.got, g_gate_w, g_up_w
    )
    totals.end()
    own_late = HeadSum(part_late, micro_count)
    summed = totals.rest()
    results = x_back.end()
    own_late.got, results = tied(own_late.got, results)
    per_head = summed[: 3 * heads].reshape(3, heads)
    gate_sum = jnp.sum(mamba_gate_w.astype(jnp.float32) * g_gate, axis=1, keepdims=True)
    summing = (lax.axis_index("head") < micro_count).astype(jnp.int32).reshape(1)
    g_x, g_bc, g_tail, g_q, g_kv, o_gain_in = owned_last(
        own_late.own,
        own_late.got,
        summing,
        gain_in[:, None],
        gate_sum,
        (mamba_in_w, mamba_bc_w, mamba_dt_w, attn_q_w, attention_key_value_weight),
        (inner, bc_cols, LANES, query_cols, kv_cols),
    )
    g_dt, g_small, _ = split_at(g_tail, (heads, small_cols, LANES - heads - small_cols), 1)
    o_conv_x, o_conv_bc, _ = split_at(
        g_small.reshape(-1), (taps * chan, taps * chan_bc, rows * small_cols - taps * (chan + chan_bc)), 0
    )
    g_mamba_out, g_attn_out = split_at(jnp.concatenate(g_out, axis=0), (out_rows, attn_rows), 0)
    def gain_grad(gain, pairs):
        total = 0.0
        for weight, grad in pairs:
            total = total + jnp.sum(weight.astype(jnp.float32) * grad, axis=1)
        return total / gain.astype(jnp.float32)

    o_gain_ffn = gain_grad(gain_ffn, ((ffn_gate_w, g_gate_w), (ffn_up_w, g_up_w)))
    o_gain_m = gain_grad(mamba_gain, ((mamba_out_w, g_mamba_out),))
    return (
        out_done[:, None],
        results[:, None],
        o_gain_in[:, 0],
        g_gate,
        g_x,
        g_bc,
        g_dt,
        per_head[0],
        per_head[1],
        per_head[2],
        o_conv_x.reshape(taps, chan),
        o_conv_bc.reshape(taps, chan_bc),
        o_gain_m,
        g_q,
        g_kv,
        g_mamba_out,
        g_attn_out,
        o_gain_ffn,
        g_gate_w,
        g_up_w,
        jnp.concatenate(g_ffn[2::3], axis=0),
    )


def solution(mesh):
    tokens = P(None, "wide", "head", None)
    matrix = P(ALL, None)
    vector = P(ALL)
    taps = P(None, ALL)
    in_specs = (
        (tokens, tokens, P(), vector)
        + (matrix,) * 4
        + (P(),) * 3
        + (taps, taps, vector)
        + (matrix,) * 4
        + (vector,)
        + (matrix,) * 3
    )
    out_specs = (
        (tokens, tokens, vector)
        + (matrix,) * 4
        + (P(),) * 3
        + (taps, taps, vector)
        + (matrix,) * 4
        + (vector,)
        + (matrix,) * 3
    )
    return jax.shard_map(
        per_device, mesh=mesh, in_specs=in_specs, out_specs=out_specs, check_vma=False
    )
```

```python
from functools import partial

import jax
import jax.numpy as jnp
from jax import lax
from jax.experimental import pallas as pl
from jax.experimental.pallas import tpu as pltpu
from jax.sharding import PartitionSpec as P

QUERY_HEADS = 8
KEY_VALUE_HEADS = 2
HEAD_SIZE = 64
GROUP = QUERY_HEADS // KEY_VALUE_HEADS
LANES = 128
LOW = jnp.bfloat16
FAR = -1e30
ALL = ("head", "wide")

epsilon = 1e-05
highest = lax.Precision.HIGHEST


def nn(left, right):
    return jnp.dot(left, right, preferred_element_type=jnp.float32)


def nt(left, right):
    return lax.dot_general(left, right, (((1,), (1,)), ((), ())), preferred_element_type=jnp.float32)


def tn(left, right):
    return lax.dot_general(left, right, (((0,), (0,)), ((), ())), preferred_element_type=jnp.float32)


def split_low(value, parts):
    terms = []
    for _ in range(parts):
        term = value.astype(LOW)
        terms.append(term)
        value = value - term.astype(jnp.float32)
    return terms


def shape(dims, kind=jnp.float32):
    return jax.ShapeDtypeStruct(dims, kind)


def shifted(value, axis, steps):
    count = lax.axis_size(axis)
    initial, last = (max(0, -steps), min(count, count - steps))
    return lax.ppermute(value, axis, [(source, source + steps) for source in range(initial, last)])


def swapped(value, axis, bit):
    count = lax.axis_size(axis)
    return lax.ppermute(value, axis, [(i, i ^ bit) for i in range(count)])


def pick(array, index, axis=0):
    return lax.dynamic_index_in_dim(array, index, axis, False)


def guess(us):
    return pl.CostEstimate(flops=int(us * 1e9), bytes_accessed=int(us * 3e6), transcendentals=0)


def tied(*values):
    return lax.optimization_barrier(values)


def sent_on(pieces, sources, receivers):
    count = lax.axis_size("head")
    place = lax.axis_index("head")
    got = []
    for step in range(1, count):
        pairs = [(i, (i + step) % count) for i in range(count)]
        pairs = [(i, k) for i, k in pairs if i < sources and k < receivers]
        got.append(lax.ppermute(pieces((place + step) % count), "head", pairs))
    return got


def put_together(own, got):
    place = lax.axis_index("head")
    count = len(got) + 1
    whole = lax.dynamic_update_index_in_dim(jnp.zeros((count,) + own.shape, own.dtype), own, place, 0)
    for step, array in enumerate(got, 1):
        whole = lax.dynamic_update_index_in_dim(whole, array, (place - step) % count, 0)
    return whole


class HeadRows:
    def __init__(self, own, receivers):
        self.own = own
        self.got = sent_on(lambda target: own, lax.axis_size("head"), receivers)

    def end(self):
        return put_together(self.own, self.got).reshape(-1, self.own.shape[1])


class ToBlocks:
    def __init__(self, pieces):
        micro_count = pieces.shape[0]
        place = lax.axis_index("head")

        def of(target):
            return pick(pieces, jnp.minimum(target, micro_count - 1))

        self.own = jnp.where(place < micro_count, of(place), jnp.zeros_like(pieces[0]))
        self.got = sent_on(of, lax.axis_size("head"), micro_count)

    def end(self):
        return put_together(self.own, self.got).reshape(-1, self.own.shape[1])


class FromBlocks:
    def __init__(self, block, micro_count):
        count = lax.axis_size("head")
        parts = block.reshape(count, block.shape[0] // count, block.shape[1])
        self.micro_count = micro_count
        self.own = pick(parts, lax.axis_index("head"))
        self.got = sent_on(lambda target: pick(parts, target), micro_count, count)

    def end(self):
        return put_together(self.own, self.got)[: self.micro_count]


class HeadSum:
    def __init__(self, part, sources, block=None):
        count = lax.axis_size("head")
        place = lax.axis_index("head")
        array = part.reshape(count, -1, part.shape[1])
        self.width = array.shape[2]
        self.sources = sources
        if block is not None:
            self.block_shape = (block.shape[0] // count, block.shape[1])
            array = jnp.concatenate([array, block.reshape(count, array.shape[1], -1)], axis=2)
        self.own = pick(array, place)
        self.got = sent_on(lambda target: pick(array, target), sources, count)

    def end(self, sizes=None):
        place = lax.axis_index("head")
        at, out = 0, []
        for size in sizes or (self.width,):
            cut = [array[:, at : at + size].astype(jnp.float32) for array in [self.own] + self.got]
            total = jnp.where(place < self.sources, cut[0], 0.0)
            for term in cut[1:]:
                total = total + term
            out.append(total)
            at += size
        return out if sizes else out[0]

    def end_block(self):
        own, got = self.own[:, self.width :], [array[:, self.width :] for array in self.got]
        whole = put_together(own, got)
        return whole.reshape((whole.shape[0],) + self.block_shape)[: self.sources]


def wide_bits():
    bits = []
    while 1 << (len(bits) + 1) <= lax.axis_size("wide"):
        bits.append(1 << len(bits))
    return bits


class EverySum:
    def __init__(self, value):
        self.value = value
        self.left = [("wide", bit) for bit in wide_bits()]
        bit = 1
        while bit < lax.axis_size("head"):
            self.left.append(("head", bit))
            bit *= 2

    def begin(self):
        self.got = swapped(self.value, *self.left.pop(0))

    def end(self):
        self.value = self.value + self.got

    def rest(self):
        while self.left:
            self.begin()
            self.end()
        return self.value


class Gathered:
    def __init__(self, own):
        bits = wide_bits()
        half = own.shape[1] // 2
        self.parts = [own[:, :half], own[:, half:]]
        self.left = [bits[1:], bits[:0:-1]]
        self.done = [[], []]

    def begin(self):
        self.got = [swapped(array, "wide", left[0]) for array, left in zip(self.parts, self.left)]

    def end(self):
        place = lax.axis_index("wide")
        for i, got in enumerate(self.got):
            bit = self.left[i].pop(0)
            mine = (place // bit) % 2
            array = self.parts[i]
            self.parts[i] = jnp.where(mine == 0, jnp.stack([array, got]), jnp.stack([got, array]))
            self.done[i].insert(0, bit)

    def rest(self):
        while self.left[0]:
            self.begin()
            self.end()
        arrays = []
        for array, done in zip(self.parts, self.done):
            ranks = [done.index(bit) for bit in sorted(done, reverse=True)]
            arrays.append(array.transpose(ranks + [len(done), len(done) + 1]))
        both = jnp.concatenate(arrays, axis=-1)
        got = swapped(both, "wide", 1)
        mine = lax.axis_index("wide") % 2
        stacked = jnp.where(mine == 0, jnp.stack([both, got], axis=-3), jnp.stack([got, both], axis=-3))
        return stacked.reshape(-1, both.shape[-1])


class CoreSum:
    def __init__(self, part):
        count = lax.axis_size("wide")
        mine = lax.axis_index("wide") % 2
        part = part.reshape(count // 2, 2, -1, part.shape[1])
        self.own = pick(part, mine, 1)
        self.got = swapped(pick(part, 1 - mine, 1), "wide", 1)

    def end(self):
        return (self.own.astype(jnp.float32) + self.got.astype(jnp.float32)).astype(self.own.dtype)


class ChipSum:
    def __init__(self, array):
        chip = lax.axis_index("wide") // 2
        self.own = pick(array, chip)
        self.got = [swapped(pick(array, chip ^ other), "wide", 2 * other) for other in range(1, array.shape[0])]

    def end(self):
        total = self.own.astype(jnp.float32)
        for array in self.got:
            total = total + array.astype(jnp.float32)
        return total.astype(self.own.dtype)


def sum_wide(array):
    return lax.psum_scatter(array, "wide", scatter_dimension=0, tiled=True)


def gather_wide(array):
    return lax.all_gather(array, "wide", axis=0, tiled=True)


class Carried:
    def __init__(self, sent, total, rows, backward):
        self.sent, self.total, self.rows = sent, total, rows
        self.state = jnp.zeros_like(total)
        self.backward = backward
        self.left = wide_bits()

    def begin(self):
        self.got = swapped(self.sent, "wide", self.left[0])

    def end(self):
        bit = self.left.pop(0)
        mine = (lax.axis_index("wide") // bit) % 2
        ahead = 1 - mine if self.backward else mine
        self.total, self.state, self.rows, self.sent = join(
            self.total, self.state, self.rows, self.got, jnp.reshape(ahead, (1,)).astype(jnp.int32)
        )

    def last(self):
        self.end()
        while self.left:
            self.begin()
            self.end()
        return self.state


def rms_scale(values, scales):
    return values * lax.rsqrt(jnp.mean(values * values, axis=-1, keepdims=True) + epsilon) * scales


def doc_index(starts, positions):
    passed = (starts[None, :] <= positions[:, None]).astype(jnp.int32)
    return jnp.sum(passed, axis=1) - 1


def split_at(array, sizes, axis):
    out, at = [], 0
    for size in sizes:
        out.append(lax.slice_in_dim(array, at, at + size, axis=axis))
        at += size
    return out


def packed(parts, rows):
    flat = jnp.concatenate([part.reshape(-1) for part in parts])
    columns = -(-flat.shape[0] // rows)
    return jnp.pad(flat, (0, rows * columns - flat.shape[0])).reshape(rows, columns)


CHUNK = 128
EXTRA = 16


def spread(value, spread_ref):
    return nn(jnp.concatenate(split_low(value, 2), axis=1), spread_ref[...])


def gathered(value, gather_ref):
    return nn(value.astype(LOW), gather_ref[...])


def gathered_fine(value, gather_ref):
    high, rest = split_low(value, 2)
    return nn(high, gather_ref[...]) + nn(rest, gather_ref[...])


def with_decay(state, decay):
    terms = split_low(decay, 3) + [jnp.zeros((EXTRA - 3, decay.shape[1]), LOW)]
    return jnp.concatenate([state.astype(LOW)] + terms, axis=0)


def silu_parts(value):
    sigma = jax.nn.sigmoid(value)
    return value * sigma, sigma * (1.0 + value * (1.0 - sigma))


def local_kernel(
    x_ref, xp_ref, bc_ref, bcp_ref, rimx_ref, rimb_ref, dt_ref, marks_ref, tapx_ref, tapb_ref, bias_ref, rate_ref, spread_ref,
    act_ref, slope_ref, bcact_ref, bcslope_ref, step_ref, cum_ref, sent_ref, state_ref, decay_ref,
):
    part = pl.program_id(0)
    marks = marks_ref[...]

    def conv(raw_ref, prev_ref, rim_ref, tap_ref):
        before = jnp.where(part == 0, rim_ref[...], prev_ref[...])
        both = jnp.concatenate([before, raw_ref[...]], axis=0)
        taps = 4
        total = None
        for i in range(taps):
            term = both[8 - taps + 1 + i : 8 - taps + 1 + i + CHUNK] * tap_ref[i : i + 1, :] * marks[:, i : i + 1]
            total = term if total is None else total + term
        return silu_parts(total)

    act, slope = conv(x_ref, xp_ref, rimx_ref, tapx_ref)
    act_ref[...] = act
    slope_ref[...] = slope.astype(LOW)
    bc, bc_slope = conv(bc_ref, bcp_ref, rimb_ref, tapb_ref)
    bcact_ref[...] = bc.astype(LOW)
    bcslope_ref[...] = bc_slope.astype(LOW)
    lane = lax.broadcasted_iota(jnp.int32, (CHUNK, LANES), 1)
    value = dt_ref[...] + bias_ref[0:1, :]
    softplus = jnp.maximum(value, 0.0) + jnp.log1p(jnp.exp(-jnp.abs(value)))
    step = jnp.where(rate_ref[0:1, :] < 0.0, softplus, 0.0)
    row = lax.broadcasted_iota(jnp.int32, (CHUNK, CHUNK), 0)
    col = lax.broadcasted_iota(jnp.int32, (CHUNK, CHUNK), 1)
    cum = jnp.dot((col <= row).astype(jnp.float32), step * rate_ref[0:1, :], precision=highest, preferred_element_type=jnp.float32)
    step_ref[...] = step
    cum_ref[...] = cum
    tail = jnp.exp(cum[CHUNK - 1 :] - cum) * marks[:, 5:6] * step
    weighted = (act * spread(tail, spread_ref)).astype(LOW)
    decay = spread(jnp.exp(cum[CHUNK - 8 :]) * marks[CHUNK - 8 :, 7:8], spread_ref)[7:8]
    own = tn(bc[:, :LANES].astype(LOW), weighted)

    @pl.when(part == 0)
    def _():
        state_ref[...] = own
        decay_ref[...] = jnp.ones_like(decay_ref)
        decay_ref[0:1, :] = decay

    @pl.when(part > 0)
    def _():
        state_ref[...] = state_ref[...] * decay + own
        decay_ref[0:1, :] = decay_ref[0:1, :] * decay

    @pl.when(part == pl.num_programs(0) - 1)
    def _():
        sent_ref[...] = with_decay(state_ref[...], decay_ref[0:1, :])


def join_kernel(ahead_ref, total_ref, state_ref, rows_ref, got_ref, total_out, state_out, rows_out, sent_out):
    size = total_ref.shape[0]
    got = got_ref[:size, :].astype(jnp.float32)
    extra = got_ref[size:, :].astype(jnp.float32)
    got_decay = extra[0:1] + extra[1:2] + extra[2:3]
    decay, sweep = rows_ref[0:1, :], rows_ref[1:2, :]
    rows_out[...] = jnp.ones_like(rows_out)
    rows_out[0:1, :] = decay * got_decay

    @pl.when(ahead_ref[0] == 1)
    def _():
        state_out[...] = state_ref[...] + sweep * got
        rows_out[1:2, :] = sweep * got_decay
        total_out[...] = total_ref[...] + decay * got

    @pl.when(ahead_ref[0] == 0)
    def _():
        state_out[...] = state_ref[...]
        rows_out[1:2, :] = sweep
        total_out[...] = got + got_decay * total_ref[...]

    sent_out[...] = with_decay(total_out[...], decay * got_decay)


def mix_kernel(
    act_ref, bcact_ref, z_ref, step_ref, cum_ref, marks_ref, docs_ref, first_ref, skip_ref, gain_ref, spread_ref, gather_ref,
    ym_ref, y_ref, entry_ref, state_ref, inner_ref,
):
    part = pl.program_id(0)

    @pl.when(part == 0)
    def _():
        state_ref[...] = first_ref[...]

    marks = marks_ref[...]
    cum = cum_ref[...]
    cum_rows = cum.T
    step = step_ref[...]
    b_mat = bcact_ref[:, :LANES]
    c_mat = bcact_ref[:, LANES:]
    act = act_ref[...]
    stepped = act * spread(step, spread_ref)
    low_stepped = stepped.astype(LOW)
    row = lax.broadcasted_iota(jnp.int32, (CHUNK, CHUNK), 0)
    col = lax.broadcasted_iota(jnp.int32, (CHUNK, CHUNK), 1)
    allowed = (row >= col) & (marks[:, 6:7] == docs_ref[0:1, :])
    gram = jnp.where(allowed, nt(c_mat, b_mat), 0.0)
    first = lax.broadcasted_iota(jnp.int32, (CHUNK, LANES), 1) < LANES // 2
    pairs = act.shape[1] // LANES
    for pair in range(pairs):
        parts = []
        for head in (2 * pair, 2 * pair + 1):
            gaps = jnp.minimum(cum[:, head : head + 1] - cum_rows[head : head + 1, :], 0.0)
            parts.append((jnp.exp(gaps) * gram).astype(LOW))
        values = low_stepped[:, pair * LANES : (pair + 1) * LANES]
        zero = jnp.zeros_like(values)
        inner_ref[:, pair * LANES : (pair + 1) * LANES] = nn(
            jnp.concatenate(parts, axis=1),
            jnp.concatenate([jnp.where(first, values, zero), jnp.where(first, zero, values)], axis=0),
        )
    state = state_ref[...]
    low_state = state.astype(LOW)
    entry_ref[0] = low_state
    entering = spread(jnp.exp(cum) * marks[:, 4:5], spread_ref)
    y = inner_ref[...] + nn(c_mat, low_state) * entering + skip_ref[0:1, :] * act
    y_ref[...] = y
    gated = y * silu_parts(z_ref[...])[0]
    scale = lax.rsqrt(gathered(gated * gated, gather_ref) * (2.0 / LANES) + epsilon)
    ym_ref[...] = (gated * spread(scale, spread_ref) * gain_ref[0:1, :]).astype(LOW)
    tail = jnp.exp(cum[CHUNK - 1 :] - cum) * marks[:, 5:6]
    weighted = (stepped * spread(tail, spread_ref)).astype(LOW)
    decay = spread(jnp.exp(cum[CHUNK - 8 :]) * marks[CHUNK - 8 :, 7:8], spread_ref)[7:8]
    state_ref[...] = state * decay + tn(b_mat, weighted)


def gate_back_kernel(
    dym_ref, y_ref, z_ref, bcact_ref, cum_ref, marks_ref, gain_ref, spread_ref, gather_ref,
    dz_ref, dy_ref, sent_ref, state_ref, decay_ref,
):
    part = pl.program_id(0)
    marks = marks_ref[...]
    cum = cum_ref[...]
    y = y_ref[...]
    silu, slope = silu_parts(z_ref[...])
    gated = y * silu
    scale = lax.rsqrt(gathered(gated * gated, gather_ref) * (2.0 / LANES) + epsilon)
    wide_scale = spread(scale, spread_ref)
    d_normed = dym_ref[...]
    u = d_normed * gain_ref[0:1, :]
    inner = gathered(u * gated, gather_ref) * (2.0 / LANES) * scale * scale * scale
    d_gated = u * wide_scale - gated * spread(inner, spread_ref)
    dz_ref[...] = (d_gated * y * slope).astype(LOW)
    dy = d_gated * silu
    dy_ref[...] = dy
    entering = spread(jnp.exp(cum) * marks[:, 4:5], spread_ref)
    own = tn(bcact_ref[:, LANES:], (dy * entering).astype(LOW))
    decay = spread(jnp.exp(cum[CHUNK - 8 :]) * marks[CHUNK - 8 :, 7:8], spread_ref)[7:8]

    @pl.when(part == 0)
    def _():
        state_ref[...] = own
        decay_ref[...] = jnp.ones_like(decay_ref)
        decay_ref[0:1, :] = decay

    @pl.when(part > 0)
    def _():
        state_ref[...] = state_ref[...] * decay + own
        decay_ref[0:1, :] = decay_ref[0:1, :] * decay

    @pl.when(part == pl.num_programs(0) - 1)
    def _():
        sent_ref[...] = with_decay(state_ref[...], decay_ref[0:1, :])


def scan_back_kernel(
    act_ref, slope_ref, bcact_ref, bcslope_ref, dt_ref, step_ref, cum_ref, marks_ref, docs_ref, dy_ref, entry_ref, first_ref,
    skip_ref, bias_ref, rate_ref, spread_ref, gather_ref, x_ref, xp_ref, bc_ref, bcp_ref, rimx_ref, rimb_ref, tapx_ref, tapb_ref,
    dscan_ref, dskip_ref, dhead_ref, dtap_ref, rim_ref, edge_ref, state_ref, inner_ref, rows_ref, next_ref, nextm_ref,
):
    part = pl.program_id(0)

    @pl.when(part == 0)
    def _():
        state_ref[...] = first_ref[...]
        rows_ref[...] = jnp.zeros_like(rows_ref)
        dskip_ref[...] = jnp.zeros_like(dskip_ref)
        dhead_ref[...] = jnp.zeros_like(dhead_ref)
        dtap_ref[...] = jnp.zeros_like(dtap_ref)
        next_ref[...] = jnp.zeros_like(next_ref)
        nextm_ref[...] = jnp.zeros_like(nextm_ref)

    marks = marks_ref[...]
    cum = cum_ref[...]
    cum_rows = cum.T
    step = step_ref[...]
    b_mat = bcact_ref[:, :LANES]
    c_mat = bcact_ref[:, LANES:]
    act = act_ref[...]
    wide_step = spread(step, spread_ref)
    stepped = act * wide_step
    low_stepped = stepped.astype(LOW)
    dy = dy_ref[...]
    low_dy = dy.astype(LOW)
    row = lax.broadcasted_iota(jnp.int32, (CHUNK, CHUNK), 0)
    col = lax.broadcasted_iota(jnp.int32, (CHUNK, CHUNK), 1)
    allowed = (row <= col) & (marks[:, 6:7] == docs_ref[0:1, :])
    gram = jnp.where(allowed, nt(b_mat, c_mat), 0.0)
    first = lax.broadcasted_iota(jnp.int32, (CHUNK, LANES), 1) < LANES // 2
    lane = lax.broadcasted_iota(jnp.int32, (CHUNK, LANES), 1)
    pairs = act.shape[1] // LANES
    d_gram = jnp.zeros((CHUNK, CHUNK), jnp.float32)
    leaving = jnp.zeros((CHUNK, LANES), jnp.float32)
    for pair in range(pairs):
        cols = slice(pair * LANES, (pair + 1) * LANES)
        values, grads = low_stepped[:, cols], low_dy[:, cols]
        zero = jnp.zeros_like(values)
        d_weights = nt(jnp.concatenate([jnp.where(first, values, zero), jnp.where(first, zero, values)], axis=0), grads)
        parts = []
        for i, head in enumerate((2 * pair, 2 * pair + 1)):
            fade = jnp.exp(jnp.minimum(cum_rows[head : head + 1, :] - cum[:, head : head + 1], 0.0))
            d_weight = d_weights[i * CHUNK : (i + 1) * CHUNK]
            weight = fade * gram
            d_gram = d_gram + d_weight * fade
            moved = d_weight * weight
            rows_ref[head : head + 1, :] = jnp.sum(moved, axis=0, keepdims=True)
            leaving = jnp.where(lane == head, jnp.sum(moved, axis=1, keepdims=True), leaving)
            parts.append(weight.astype(LOW))
        inner_ref[:, cols] = nn(
            jnp.concatenate(parts, axis=1),
            jnp.concatenate([jnp.where(first, grads, zero), jnp.where(first, zero, grads)], axis=0),
        )
    d_state = state_ref[...]
    low_d_state = d_state.astype(LOW)
    entry = entry_ref[0]
    entering = spread(jnp.exp(cum) * marks[:, 4:5], spread_ref)
    tail = spread(jnp.exp(cum[CHUNK - 1 :] - cum) * marks[:, 5:6], spread_ref)
    from_state = nn(b_mat, low_d_state) * tail
    d_stepped = inner_ref[...] + from_state
    out_moved = gathered_fine(stepped * from_state, gather_ref)
    entering_dy = dy * entering
    in_moved = gathered_fine(entering_dy * nn(c_mat, entry), gather_ref)
    low_entering_dy = entering_dy.astype(LOW)
    low_gram = jnp.where(allowed, d_gram, 0.0).astype(LOW)
    d_b = nt((stepped * tail).astype(LOW), low_d_state) + nn(low_gram, c_mat)
    d_c = nt(low_entering_dy, entry) + tn(low_gram, b_mat)
    decay_small = jnp.exp(cum[CHUNK - 8 :]) * marks[CHUNK - 8 :, 7:8]
    decay = spread(decay_small, spread_ref)[7:8]
    overlap = jnp.sum(d_state * entry.astype(jnp.float32), axis=0, keepdims=True)
    d_decay = nn(jnp.concatenate(split_low(jnp.broadcast_to(overlap, (8, overlap.shape[1])), 2), axis=0), gather_ref[...])
    at_end = jnp.sum(out_moved, axis=0, keepdims=True) + (d_decay[0:1] + d_decay[8:9]) * decay_small[7:8]
    d_cum = rows_ref[...].T - leaving + in_moved - out_moved
    d_cum = d_cum + jnp.where(lax.broadcasted_iota(jnp.int32, d_cum.shape, 0) == CHUNK - 1, at_end, 0.0)
    d_log = jnp.dot((row <= col).astype(jnp.float32), d_cum, precision=highest, preferred_element_type=jnp.float32)
    rate = rate_ref[0:1, :]
    d_step = gathered_fine(act * d_stepped, gather_ref) + d_log * rate
    d_dt = d_step * jax.nn.sigmoid(dt_ref[...] + bias_ref[0:1, :])
    d_dt = jnp.where(rate < 0.0, d_dt, 0.0)
    inner = act.shape[1]
    scan = inner + 2 * LANES
    dscan_ref[:, scan:] = d_dt.astype(LOW)
    dhead_ref[0:1, :] += jnp.sum(d_dt, axis=0, keepdims=True)
    dhead_ref[1:2, :] += jnp.sum(d_log * rate * step, axis=0, keepdims=True)
    dskip_ref[0:1, :] += jnp.sum(dy * act, axis=0, keepdims=True)
    taps = 4
    marks_ext = jnp.concatenate([marks, nextm_ref[...]], axis=0)

    def conv_back(d_pre, lanes, raw_ref, prev_ref, edge_raw_ref, tap_ref):
        before = jnp.where(part == pl.num_programs(0) - 1, edge_raw_ref[...], prev_ref[...])
        raw = jnp.concatenate([before, raw_ref[...]], axis=0)
        ext = jnp.concatenate([d_pre, next_ref[:, lanes]], axis=0)
        top = jnp.concatenate([jnp.zeros_like(ext[:8]), d_pre[:8]], axis=0)
        top_marks = jnp.concatenate([marks[:8], marks[:8]], axis=0)
        d_raw, rim = None, None
        for i in range(taps):
            ahead = taps - 1 - i
            tap = tap_ref[i : i + 1, :]
            masked = d_pre * marks[:, i : i + 1]
            dtap_ref[i : i + 1, lanes] += jnp.sum(masked * raw[8 - ahead : 8 - ahead + CHUNK], axis=0, keepdims=True)
            term = (ext * marks_ext[:, i : i + 1])[ahead : ahead + CHUNK] * tap
            d_raw = term if d_raw is None else d_raw + term
            if ahead:
                term = (top * top_marks[:, i : i + 1])[ahead : ahead + 8] * tap
                rim = term if rim is None else rim + term
        next_ref[:, lanes] = d_pre[:8]
        dscan_ref[:, lanes] = d_raw.astype(LOW)
        rim_ref[:, lanes] = rim

        @pl.when(part == 0)
        def _():
            edge_ref[:, lanes] = d_raw[CHUNK - 8 :]

    conv_back(
        (d_stepped * wide_step + dy * skip_ref[0:1, :]) * slope_ref[...].astype(jnp.float32),
        slice(0, inner), x_ref, xp_ref, rimx_ref, tapx_ref,
    )
    conv_back(
        jnp.concatenate([d_b, d_c], axis=1) * bcslope_ref[...].astype(jnp.float32),
        slice(inner, scan), bc_ref, bcp_ref, rimb_ref, tapb_ref,
    )
    nextm_ref[...] = marks[:8]
    state_ref[...] = d_state * decay + tn(c_mat, low_entering_dy)


def head_matrices(inner, heads):
    owner = jnp.arange(inner, dtype=jnp.int32) // (inner // heads)
    gather_m = (owner[:, None] == jnp.arange(LANES, dtype=jnp.int32)[None, :]).astype(LOW)
    return jnp.concatenate([gather_m.T, gather_m.T], axis=0), gather_m


def lanes_row(vector):
    return jnp.pad(vector, (0, LANES - vector.shape[0]))[None, :]


def call(kernel, name, us, parts, ins, outs, scratch, reverse=False):
    def spec(block, how):
        if how == "part":
            how = lambda c: (c,) + (0,) * (len(block) - 1)
        elif how == "whole":
            how = lambda c: (0,) * len(block)
        elif isinstance(how, int):
            column = how
            how = lambda c: (c, column)

        def index(c):
            return how(parts - 1 - c if reverse else c)

        return pl.BlockSpec(block, index)

    return pl.pallas_call(
        kernel,
        grid=(parts,),
        in_specs=[spec(block, how) for _, block, how in ins],
        out_specs=[spec(block, how) for _, block, how in outs],
        scratch_shapes=scratch,
        out_shape=[shape for shape, _, _ in outs],
        compiler_params=pltpu.CompilerParams(vmem_limit_bytes=56 * 2**20),
        cost_estimate=guess(us),
        name=name,
    )(*[array for array, _, _ in ins])


def mamba_local(raw, rim, marks, taps, bias, rate, cols, mats):
    length = raw.shape[0]
    parts = length // CHUNK
    inner, n2, x_at, bc_at, dt_at = cols
    before = CHUNK // 8

    def prev(column):
        return lambda c: (jnp.maximum(c * before - 1, 0), column)

    return call(
        local_kernel,
        "mamba_local",
        11,
        parts,
        [
            (raw, (CHUNK, inner), x_at),
            (raw, (8, inner), prev(x_at)),
            (raw, (CHUNK, n2), bc_at),
            (raw, (8, n2), prev(bc_at)),
            (rim[:, :inner], (8, inner), "whole"),
            (rim[:, inner:], (8, n2), "whole"),
            (raw, (CHUNK, LANES), dt_at),
            (marks, (CHUNK, LANES), "part"),
            (taps[:, :inner], (8, inner), "whole"),
            (taps[:, inner:], (8, n2), "whole"),
            (bias, (1, LANES), "whole"),
            (rate, (1, LANES), "whole"),
            (mats[0], mats[0].shape, "whole"),
        ],
        [
            (shape((length, inner)), (CHUNK, inner), "part"),
            (shape((length, inner), LOW), (CHUNK, inner), "part"),
            (shape((length, n2), LOW), (CHUNK, n2), "part"),
            (shape((length, n2), LOW), (CHUNK, n2), "part"),
            (shape((length, LANES)), (CHUNK, LANES), "part"),
            (shape((length, LANES)), (CHUNK, LANES), "part"),
            (shape((n2 // 2 + EXTRA, inner), LOW), (n2 // 2 + EXTRA, inner), "whole"),
            (shape((n2 // 2, inner)), (n2 // 2, inner), "whole"),
            (shape((8, inner)), (8, inner), "whole"),
        ],
        [],
    )


def mamba_mix(feats, raw, marks, docs, state, skip, gain, mats):
    act, slope, bcact, bcslope, step, cum = feats
    length, inner = act.shape
    parts = length // CHUNK
    n2 = bcact.shape[1]
    return call(
        mix_kernel,
        "mamba_mix",
        11,
        parts,
        [
            (act, (CHUNK, inner), "part"),
            (bcact, (CHUNK, n2), "part"),
            (raw, (CHUNK, inner), 0),
            (step, (CHUNK, LANES), "part"),
            (cum, (CHUNK, LANES), "part"),
            (marks, (CHUNK, LANES), "part"),
            (docs, (8, CHUNK), lambda c: (0, c)),
            (state, state.shape, "whole"),
            (skip, (1, inner), "whole"),
            (gain, (1, inner), "whole"),
            (mats[0], mats[0].shape, "whole"),
            (mats[1], mats[1].shape, "whole"),
        ],
        [
            (shape((length, inner), LOW), (CHUNK, inner), "part"),
            (shape((length, inner)), (CHUNK, inner), "part"),
            (shape((parts, n2 // 2, inner), LOW), (1, n2 // 2, inner), "part"),
        ],
        [pltpu.VMEM((n2 // 2, inner), jnp.float32), pltpu.VMEM((CHUNK, inner), jnp.float32)],
    )


def mamba_gate_back(d_normed, y, raw, feats, marks, gain, mats):
    act, slope, bcact, bcslope, step, cum = feats
    length, inner = act.shape
    parts = length // CHUNK
    n2 = bcact.shape[1]
    return call(
        gate_back_kernel,
        "mamba_gate_back",
        11,
        parts,
        [
            (d_normed, (CHUNK, inner), "part"),
            (y, (CHUNK, inner), "part"),
            (raw, (CHUNK, inner), 0),
            (bcact, (CHUNK, n2), "part"),
            (cum, (CHUNK, LANES), "part"),
            (marks, (CHUNK, LANES), "part"),
            (gain, (1, inner), "whole"),
            (mats[0], mats[0].shape, "whole"),
            (mats[1], mats[1].shape, "whole"),
        ],
        [
            (shape((length, inner), LOW), (CHUNK, inner), "part"),
            (shape((length, inner)), (CHUNK, inner), "part"),
            (shape((n2 // 2 + EXTRA, inner), LOW), (n2 // 2 + EXTRA, inner), "whole"),
            (shape((n2 // 2, inner)), (n2 // 2, inner), "whole"),
            (shape((8, inner)), (8, inner), "whole"),
        ],
        [],
        reverse=True,
    )


def mamba_scan_back(feats, raw, rim, taps, marks, docs, dy, entry, state, skip, bias, rate, cols, mats):
    act, slope, bcact, bcslope, step, cum = feats
    length, inner = act.shape
    parts = length // CHUNK
    n2 = bcact.shape[1]
    x_at, bc_at, dt_at = cols[2:]
    scan = inner + n2

    def prev(column):
        return lambda c: (jnp.maximum(c * (CHUNK // 8) - 1, 0), column)

    return call(
        scan_back_kernel,
        "mamba_scan_back",
        23,
        parts,
        [
            (act, (CHUNK, inner), "part"),
            (slope, (CHUNK, inner), "part"),
            (bcact, (CHUNK, n2), "part"),
            (bcslope, (CHUNK, n2), "part"),
            (raw, (CHUNK, LANES), dt_at),
            (step, (CHUNK, LANES), "part"),
            (cum, (CHUNK, LANES), "part"),
            (marks, (CHUNK, LANES), "part"),
            (docs, (8, CHUNK), lambda c: (0, c)),
            (dy, (CHUNK, inner), "part"),
            (entry, (1, n2 // 2, inner), "part"),
            (state, state.shape, "whole"),
            (skip, (1, inner), "whole"),
            (bias, (1, LANES), "whole"),
            (rate, (1, LANES), "whole"),
            (mats[0], mats[0].shape, "whole"),
            (mats[1], mats[1].shape, "whole"),
            (raw, (CHUNK, inner), x_at),
            (raw, (8, inner), prev(x_at)),
            (raw, (CHUNK, n2), bc_at),
            (raw, (8, n2), prev(bc_at)),
            (rim[:, :inner], (8, inner), "whole"),
            (rim[:, inner:], (8, n2), "whole"),
            (taps[:, :inner], (8, inner), "whole"),
            (taps[:, inner:], (8, n2), "whole"),
        ],
        [
            (shape((length, scan + LANES), LOW), (CHUNK, scan + LANES), "part"),
            (shape((8, inner)), (8, inner), "whole"),
            (shape((8, LANES)), (8, LANES), "whole"),
            (shape((8, scan)), (8, scan), "whole"),
            (shape((8, scan)), (8, scan), "whole"),
            (shape((8, scan)), (8, scan), "whole"),
        ],
        [
            pltpu.VMEM((n2 // 2, inner), jnp.float32),
            pltpu.VMEM((CHUNK, inner), jnp.float32),
            pltpu.VMEM((LANES, CHUNK), jnp.float32),
            pltpu.VMEM((8, scan), jnp.float32),
            pltpu.VMEM((8, LANES), jnp.float32),
        ],
        reverse=True,
    )


def join(total, state, rows, got, ahead):
    whole = pl.BlockSpec(memory_space=pltpu.VMEM)
    return pl.pallas_call(
        join_kernel,
        in_specs=[pl.BlockSpec(memory_space=pltpu.SMEM)] + [whole] * 4,
        out_specs=[whole] * 4,
        out_shape=[shape(total.shape), shape(total.shape), shape(rows.shape), shape(got.shape, LOW)],
        compiler_params=pltpu.CompilerParams(vmem_limit_bytes=32 * 2**20),
        cost_estimate=guess(2),
        name="join",
    )(ahead, total, state, rows, got)


BOTH = 4
ONES = 16


def causal(scores):
    key_row = lax.broadcasted_iota(jnp.int32, scores.shape, 0)
    query = lax.broadcasted_iota(jnp.int32, scores.shape, 1)
    return jnp.where(key_row <= query, scores, FAR)


def attend_kernel(place_ref, q_ref, far_ref, kv_ref, extra_ref, o_ref, qb_ref, keys_ref, values_ref, acc_ref):
    blk = q_ref.shape[2]
    last = place_ref[0]

    @pl.when(pl.program_id(0) == 0)
    def _():
        first = lax.broadcasted_iota(jnp.int32, (blk, LANES), 1) < HEAD_SIZE

        @pl.loop(0, last + 1)
        def _(block):
            rows = pl.ds(pl.multiple_of(block * blk, blk), blk)
            both = kv_ref[rows, :]
            keys_ref[rows, :] = jnp.where(first, both, extra_ref[rows, :])
            values_ref[:ONES, rows] = jnp.ones((ONES, blk), LOW)
            values_ref[ONES:, rows] = both.astype(jnp.float32).T[HEAD_SIZE:].astype(LOW)

    queries = [
        jnp.concatenate([q_ref[i] * jnp.asarray(HEAD_SIZE ** (-0.5), LOW), far_ref[...]], axis=0)
        for i in range(BOTH)
    ]
    acc_ref[...] = jnp.zeros_like(acc_ref)

    def step(block, tops, diagonal):
        rows = pl.ds(pl.multiple_of(block * blk, blk), blk)
        keys, values = keys_ref[rows, :], values_ref[:, rows]
        new_tops = []
        for i in range(BOTH):
            scores = nn(keys, queries[i])
            if diagonal:
                scores = causal(scores)
            new_top = jnp.maximum(tops[i], jnp.max(scores, axis=0, keepdims=True))
            probs = jnp.exp(scores - new_top).astype(LOW)
            acc_ref[i] = acc_ref[i] * jnp.exp(tops[i] - new_top) + nn(values, probs)
            new_tops.append(new_top)
        return tuple(new_tops)

    tops = (jnp.full((1, blk), FAR, jnp.float32),) * BOTH
    tops = lax.fori_loop(0, last, lambda block, tops: step(block, tops, False), tops)
    tops = step(last, tops, True)
    row = lax.broadcasted_iota(jnp.int32, (HEAD_SIZE, blk), 0)
    for i in range(BOTH):
        total = acc_ref[i, 0:1, :]
        o_ref[i] = acc_ref[i, ONES:, :] / total
        extra = far_ref[...].astype(jnp.float32)
        for at, term in enumerate(split_low(-(tops[i] + jnp.log(total)), 3)):
            extra = jnp.where(row == 4 + at, term.astype(jnp.float32), extra)
        qb_ref[i] = jnp.concatenate([queries[i][:HEAD_SIZE], extra.astype(LOW)], axis=0)


def attend_back_kernel(place_ref, qb_ref, dot_ref, o_ref, kv_ref, extra_ref, dq_ref, dkv_ref, keys_ref, rows_ref, values_ref, acc_ref, dqa_ref):
    blk = qb_ref.shape[2]
    last = place_ref[0]
    member = pl.program_id(0)

    @pl.when(member == 0)
    def _():
        acc_ref[...] = jnp.zeros_like(acc_ref)
        lane = lax.broadcasted_iota(jnp.int32, (blk, LANES), 1)
        ones = jnp.where(lane < 3, 1.0, 0.0).astype(LOW)

        @pl.loop(0, last + 1)
        def _(block):
            rows = pl.ds(pl.multiple_of(block * blk, blk), blk)
            both = kv_ref[rows, :]
            keys_ref[rows, :] = jnp.where(lane < HEAD_SIZE, both, extra_ref[rows, :])
            values_ref[rows, :] = jnp.where(lane < HEAD_SIZE, ones, both)
            rows_ref[:, rows] = both.astype(jnp.float32).T[:HEAD_SIZE].astype(LOW)

    row = lax.broadcasted_iota(jnp.int32, (HEAD_SIZE, blk), 0)
    none = jnp.zeros((HEAD_SIZE, blk), jnp.float32)
    queries, d_outs, pairs = [], [], []
    for i in range(BOTH):
        queries.append(qb_ref[i])
        d_out = dot_ref[i].astype(jnp.float32)
        row_dot = jnp.sum(d_out * o_ref[i], axis=0, keepdims=True)
        extra = none
        for at, term in enumerate(split_low(-row_dot, 3)):
            extra = jnp.where(row == at, term.astype(jnp.float32), extra)
        d_outs.append(jnp.concatenate([extra, d_out], axis=0).astype(LOW))
        q_part = jnp.concatenate([qb_ref[i, :HEAD_SIZE, :].astype(jnp.float32), none], axis=0)
        pairs.append(jnp.concatenate([q_part.T, jnp.concatenate([none, d_out], axis=0).T], axis=0).astype(LOW))
    dqa_ref[...] = jnp.zeros_like(dqa_ref)

    def step(block, diagonal):
        rows = pl.ds(pl.multiple_of(block * blk, blk), blk)
        keys, values, key_rows = keys_ref[rows, :], values_ref[rows, :], rows_ref[:, rows]
        total = acc_ref[rows, :]
        for i in range(BOTH):
            logs = nn(keys, queries[i])
            if diagonal:
                logs = causal(logs)
            probs = jnp.exp(logs)
            d_scores = (probs * nn(values, d_outs[i])).astype(LOW)
            total = total + nn(jnp.concatenate([d_scores, probs.astype(LOW)], axis=1), pairs[i])
            dqa_ref[i] += nn(key_rows, d_scores)
        acc_ref[rows, :] = total

    @pl.loop(0, last)
    def _(block):
        step(block, False)

    step(last, True)
    dq_ref[...] = (dqa_ref[...] * HEAD_SIZE ** (-0.5)).astype(LOW)

    @pl.when(member == GROUP // BOTH - 1)
    def _():
        dkv_ref[...] = acc_ref[...].astype(LOW)


def attend_specs(blk, total, group):
    mine = group * (GROUP // BOTH)
    return dict(
        narrow=pl.BlockSpec((BOTH, HEAD_SIZE, blk), lambda r, p: (mine + r, 0, 0)),
        own_narrow=pl.BlockSpec((BOTH, HEAD_SIZE, blk), lambda r, p: (r, 0, 0)),
        own_broad=pl.BlockSpec((BOTH, LANES, blk), lambda r, p: (r, 0, 0)),
        kv=pl.BlockSpec((total, LANES), lambda r, p: (0, group)),
        extra=pl.BlockSpec((total, LANES), lambda r, p: (0, 0)),
        far=pl.BlockSpec((HEAD_SIZE, blk), lambda r, p: (0, 0)),
    )


def attend_masks(doc_here, key_doc, doc_count):
    docs = jnp.arange(HEAD_SIZE, dtype=jnp.int32)
    far = jnp.where((docs[:, None] != doc_here[None, :]) & (docs[:, None] < doc_count), FAR, 0.0).astype(LOW)
    lane = jnp.arange(LANES, dtype=jnp.int32)[None, :] - HEAD_SIZE
    extra = ((key_doc[:, None] == lane) | ((lane >= doc_count) & (lane < doc_count + 3))).astype(LOW)
    return far, extra


def attend(group, q_rows, key_all, masks, place):
    blk = q_rows.shape[2]
    total = key_all.shape[0]
    specs = attend_specs(blk, total, group)
    return pl.pallas_call(
        attend_kernel,
        grid_spec=pltpu.PrefetchScalarGridSpec(
            num_scalar_prefetch=1,
            grid=(GROUP // BOTH,),
            in_specs=[specs["narrow"], specs["far"], specs["kv"], specs["extra"]],
            out_specs=[specs["own_narrow"], specs["own_broad"]],
            scratch_shapes=[
                pltpu.VMEM((total, LANES), LOW),
                pltpu.VMEM((HEAD_SIZE + ONES, total), LOW),
                pltpu.VMEM((BOTH, HEAD_SIZE + ONES, blk), jnp.float32),
            ],
        ),
        out_shape=[shape((GROUP, HEAD_SIZE, blk)), shape((GROUP, LANES, blk), LOW)],
        compiler_params=pltpu.CompilerParams(vmem_limit_bytes=56 * 2**20),
        cost_estimate=guess(17),
        name="attend",
    )(place, q_rows, masks[0], key_all, masks[1])


def attend_back(group, q_back, out, d_rows, key_all, masks, place):
    blk = d_rows.shape[2]
    total = key_all.shape[0]
    specs = attend_specs(blk, total, group)
    return pl.pallas_call(
        attend_back_kernel,
        grid_spec=pltpu.PrefetchScalarGridSpec(
            num_scalar_prefetch=1,
            grid=(GROUP // BOTH,),
            in_specs=[specs["own_broad"], specs["narrow"], specs["own_narrow"], specs["kv"], specs["extra"]],
            out_specs=[specs["own_narrow"], specs["extra"]],
            scratch_shapes=[
                pltpu.VMEM((total, LANES), LOW),
                pltpu.VMEM((HEAD_SIZE, total), LOW),
                pltpu.VMEM((total, LANES), LOW),
                pltpu.VMEM((total, LANES), jnp.float32),
                pltpu.VMEM((BOTH, HEAD_SIZE, blk), jnp.float32),
            ],
        ),
        out_shape=[shape((GROUP, HEAD_SIZE, blk), LOW), shape((total, LANES), LOW)],
        compiler_params=pltpu.CompilerParams(vmem_limit_bytes=60 * 2**20),
        cost_estimate=guess(27),
        name="attend_back",
    )(place, q_back, d_rows, out, key_all, masks[1])


PIECE = 256


def feed_kernel(x_ref, gy_ref, plain_ref, w_ref, out_ref, dx_ref, grad_ref, xt_ref):
    fold = w_ref.shape[1] // 3

    @pl.when(pl.program_id(0) == 0)
    def _():
        out_ref[...] = jnp.zeros_like(out_ref)
        dx_ref[...] = jnp.zeros_like(dx_ref)
        xt_ref[...] = x_ref[...].astype(jnp.float32).T.astype(LOW)

    @pl.loop(0, fold // PIECE)
    def _(piece):
        at = pl.multiple_of(piece * PIECE, PIECE)
        gate_cols = pl.ds(at, PIECE)
        up_cols = pl.ds(pl.multiple_of(fold + at, PIECE), PIECE)
        down_cols = pl.ds(2 * fold, fold)
        w_gate, w_up, w_down = w_ref[:, gate_cols], w_ref[:, up_cols], w_ref[gate_cols, down_cols]
        x, gy = x_ref[...], gy_ref[...]
        gate, up = nn(x, w_gate), nn(x, w_up)
        sigma = jax.nn.sigmoid(gate)
        silu = gate * sigma
        act = silu * up
        d_act = nt(gy, w_down)
        d_gate = (d_act * up * sigma * (1.0 + gate * (1.0 - sigma))).astype(LOW)
        d_up = (d_act * silu).astype(LOW)
        out_ref[...] += nn(act.astype(LOW), w_down)
        dx_ref[...] += nt(d_gate, w_gate) + nt(d_up, w_up)
        x_t = xt_ref[...]
        grad_ref[:, gate_cols] = nn(x_t, d_gate).astype(LOW)
        grad_ref[:, up_cols] = nn(x_t, d_up).astype(LOW)
        grad_ref[gate_cols, down_cols] = nn(act.T.astype(LOW), plain_ref[...]).astype(LOW)


def feed_forward(x, gy, plain, w, folds, fold):
    tokens, width = x.shape
    whole = pl.BlockSpec((tokens, width), lambda j: (0, 0))
    return pl.pallas_call(
        feed_kernel,
        grid=(folds,),
        in_specs=[whole, whole, whole, pl.BlockSpec((width, 3 * fold), lambda j: (0, j))],
        out_specs=[whole, whole, pl.BlockSpec((width, 3 * fold), lambda j: (0, j))],
        out_shape=[
            shape((tokens, width)),
            shape((tokens, width)),
            shape((width, 3 * fold * folds), LOW),
        ],
        scratch_shapes=[pltpu.VMEM((width, tokens), LOW)],
        compiler_params=pltpu.CompilerParams(vmem_limit_bytes=60 * 2**20),
        cost_estimate=guess(35),
        name="feed_forward",
    )(x, gy, plain, w)


def last_grads_kernel(x_ref, scan_ref, query_ref, kv_ref, small_ref, grad_ref):
    x_t = x_ref[...].astype(jnp.float32).T.astype(LOW)
    scan = scan_ref.shape[1]
    query = query_ref.shape[1]
    grad_ref[:, : scan - LANES] = nn(x_t, scan_ref[:, : scan - LANES]).astype(LOW)
    grad_ref[:, scan - LANES : scan] = (nn(x_t, scan_ref[:, scan - LANES :]) + small_ref[...]).astype(LOW)
    grad_ref[:, scan : scan + query] = nn(x_t, query_ref[...]).astype(LOW)
    grad_ref[:, scan + query :] = nn(x_t, kv_ref[...]).astype(LOW)


def last_grads(x, d_scan, d_query, d_kv, small):
    tokens, width = x.shape
    count = d_scan.shape[1] + d_query.shape[1] + d_kv.shape[1]
    return pl.pallas_call(
        last_grads_kernel,
        out_shape=shape((width, count), LOW),
        compiler_params=pltpu.CompilerParams(vmem_limit_bytes=56 * 2**20),
        cost_estimate=guess(8),
        name="last_grads",
    )(x, d_scan, d_query, d_kv, small)


def input_back_kernel(scan_ref, gate_ref, query_ref, kv_ref, w_ref, x_ref, more_ref, gain_ref, dx_ref):
    at, total = 0, None
    for ref in (scan_ref, gate_ref, query_ref, kv_ref):
        term = nt(ref[...], w_ref[:, at : at + ref.shape[1]])
        total = term if total is None else total + term
        at += ref.shape[1]
    x = x_ref[...]
    scale = lax.rsqrt(jnp.mean(x * x, axis=1, keepdims=True) + epsilon)
    u = total * gain_ref[...]
    inner = jnp.mean(u * x, axis=1, keepdims=True) * scale * scale * scale
    dx_ref[...] = (more_ref[...] + u * scale - x * inner).astype(LOW)


def input_back(d_scan, d_gate, d_query, d_kv, w, x, more, gain):
    tokens, width = x.shape
    part = min(2 * CHUNK, tokens)
    rows = lambda array: pl.BlockSpec((part, array.shape[1]), lambda i: (i, 0))
    whole = lambda array: pl.BlockSpec(array.shape, lambda i: (0, 0))
    return pl.pallas_call(
        input_back_kernel,
        grid=(tokens // part,),
        in_specs=[rows(a) for a in (d_scan, d_gate, d_query, d_kv)] + [whole(w), rows(x), rows(more), whole(gain)],
        out_specs=rows(x),
        out_shape=shape((tokens, width), LOW),
        compiler_params=pltpu.CompilerParams(vmem_limit_bytes=56 * 2**20),
        cost_estimate=guess(10),
        name="input_back",
    )(d_scan, d_gate, d_query, d_kv, w, x, more, gain)


def owned_kernel(count_ref, own_ref, a_ref, b_ref, c_ref, gain_ref, gate_ref, x_ref, bc_ref, dt_ref, query_ref, kv_ref, *outs):
    total = own_ref[...].astype(jnp.float32) * count_ref[0].astype(jnp.float32)
    total = total + a_ref[...].astype(jnp.float32) + b_ref[...].astype(jnp.float32) + c_ref[...].astype(jnp.float32)
    at, inner = 0, gate_ref[...]
    for weight_ref, out_ref in zip((x_ref, bc_ref, dt_ref, query_ref, kv_ref), outs):
        part = total[:, at : at + out_ref.shape[1]]
        out_ref[...] = part
        heads = weight_ref.shape[1]
        inner = inner + jnp.sum(weight_ref[...].astype(jnp.float32) * part[:, :heads], axis=1, keepdims=True)
        at += out_ref.shape[1]
    outs[-1][...] = inner / gain_ref[...].astype(jnp.float32)


def owned_last(own, got, counts, gain, gate, weights, sizes):
    rows = own.shape[0]
    arrays = (own, *got, gain, gate, *weights)
    whole = lambda dims: pl.BlockSpec(dims, lambda i: (0, 0))
    return pl.pallas_call(
        owned_kernel,
        grid=(1,),
        in_specs=[pl.BlockSpec(memory_space=pltpu.SMEM)] + [whole(array.shape) for array in arrays],
        out_specs=[whole((rows, size)) for size in sizes] + [whole((rows, 1))],
        out_shape=[shape((rows, size)) for size in sizes] + [shape((rows, 1))],
        compiler_params=pltpu.CompilerParams(vmem_limit_bytes=16 * 2**20),
        cost_estimate=guess(3),
        name="owned_last",
    )(counts, *arrays)


def tap_marks(starts, first, length, taps):
    ext = doc_index(starts, first - (taps - 1) + jnp.arange(length + taps - 1, dtype=jnp.int32))
    return jnp.stack([(ext[i : i + length] == ext[taps - 1 :]).astype(jnp.float32) for i in range(taps)], axis=1)


def marks_of(starts, block_base, length, taps):
    ext = doc_index(starts, block_base - (taps - 1) + jnp.arange(length + taps - 1, dtype=jnp.int32))
    here = ext[taps - 1 :]
    chunks = here.reshape(-1, CHUNK)
    ahead = ext[taps - 2 : taps - 2 + length].reshape(-1, CHUNK)[:, :1]
    last = chunks[:, -1:]
    columns = [ext[i : i + length] == here for i in range(taps)] + [
        (chunks == ahead).reshape(-1),
        (chunks == last).reshape(-1),
        here,
        jnp.broadcast_to(last == ahead, chunks.shape).reshape(-1),
    ]
    marks = jnp.stack([column.astype(jnp.float32) for column in columns], axis=1)
    marks = jnp.pad(marks, ((0, 0), (0, LANES - len(columns))))
    return marks, jnp.broadcast_to(here.astype(jnp.float32)[None], (8, length)), here


def per_device(
    hidden_in,
    cotangent,
    doc_starts,
    gain_in,
    mamba_gate_w,
    mamba_in_w,
    mamba_bc_w,
    mamba_dt_w,
    dt_bias,
    a_log,
    d_skip,
    conv_x,
    conv_bc,
    mamba_gain,
    attn_q_w,
    attention_key_value_weight,
    mamba_out_w,
    attn_out_w,
    gain_ffn,
    ffn_gate_w,
    ffn_up_w,
    ffn_down_w,
):
    devices = lax.axis_size("head") * lax.axis_size("wide")
    wide_id = lax.axis_index("wide")
    micro_count = hidden_in.shape[0]
    block_tok = hidden_in.shape[2] * lax.axis_size("head")
    taps = conv_x.shape[0]
    heads = dt_bias.shape[0]
    rows, inner = mamba_gate_w.shape
    width = rows * devices
    bc_cols = mamba_bc_w.shape[1]
    query_cols = attn_q_w.shape[1]
    kv_cols = attention_key_value_weight.shape[1]
    hidden = ffn_gate_w.shape[1]
    out_rows = mamba_out_w.shape[0]
    attn_rows = attn_out_w.shape[0]
    chan = conv_x.shape[1]
    chan_bc = conv_bc.shape[1]

    scan_cols = inner + bc_cols
    first_cols = scan_cols + LANES

    heads_dev, wide_dev = lax.axis_size("head"), lax.axis_size("wide")
    folds = hidden // width
    feature = jnp.arange(width, dtype=jnp.int32)
    inside = (feature // rows) % wide_dev * heads_dev + feature // (rows * wide_dev)
    order = (inside[:, None] * rows + (feature % rows)[:, None] == feature[None, :]).astype(LOW)

    def mixed(array):
        return nn(array.reshape(-1, width), order).astype(LOW).reshape(array.shape)

    def plain(array):
        return nt(array.reshape(-1, width), order).astype(LOW).reshape(array.shape)

    def by_place(array):
        return array.reshape((heads_dev, wide_dev) + array.shape[1:]).swapaxes(0, 1).reshape(array.shape)

    def by_owner(array):
        return array.reshape((wide_dev, heads_dev) + array.shape[1:]).swapaxes(0, 1).reshape(array.shape)

    def folded(weight):
        return weight.reshape(rows, heads_dev, wide_dev, folds, rows).transpose(0, 3, 2, 1, 4).reshape(rows, folds, width)

    def unfolded(parts):
        unit = jnp.arange(hidden, dtype=jnp.int32)
        owner, fold, row = unit // (folds * rows), unit // rows % folds, unit % rows
        at = (owner % wide_dev * heads_dev + owner // wide_dev) * rows + row
        total = 0.0
        for i, part in enumerate(parts):
            one_hot = ((feature[:, None] == at[None, :]) & (fold == i)[None, :]).astype(LOW)
            total = total + nn(jnp.concatenate(split_low(part, 3), axis=0), one_hot)
        high, middle, low = split_at(total, (rows,) * 3, 0)
        return high + (middle + low)

    small = packed([gain_in, gain_ffn, mamba_gain, conv_x, conv_bc], rows)
    small_cols = small.shape[1]
    pad = jnp.zeros((rows, LANES - heads - small_cols), LOW)
    in_shard = jnp.concatenate(
        [mamba_in_w, mamba_bc_w, mamba_dt_w, small, pad, mamba_gate_w, attn_q_w, attention_key_value_weight], axis=1
    )
    to_width = mixed(jnp.concatenate([ffn_down_w, mamba_out_w, attn_out_w], axis=0)).reshape(-1, rows, width)
    gate_folds, up_folds = folded(ffn_gate_w), folded(ffn_up_w)
    ffn_shard = []
    for i in range(folds):
        ffn_shard += [gate_folds[:, i], up_folds[:, i], to_width[i]]
    ffn_shard = jnp.concatenate(ffn_shard, axis=1)
    out_shard = jnp.concatenate([to_width[i] for i in range(folds, to_width.shape[0])], axis=1)
    x_pieces = mixed(hidden_in[:, 0])

    micro = jnp.minimum(lax.axis_index("head"), micro_count - 1)
    starts = pick(doc_starts, micro)
    block_base = wide_id * block_tok
    marks, docs_row, doc_here = marks_of(starts, block_base, block_tok, taps)
    key_doc = doc_index(starts, jnp.arange(block_tok * lax.axis_size("wide"), dtype=jnp.int32))
    masks = attend_masks(doc_here, key_doc, doc_starts.shape[1])
    mats = head_matrices(inner, heads)
    bias_row = lanes_row(dt_bias)
    rate_row = lanes_row(-jnp.exp(a_log))
    skip_row = jnp.repeat(d_skip, inner // heads)[None]
    in_rows = HeadRows(in_shard, micro_count)
    prepared = (marks, docs_row, masks, mats, bias_row, rate_row, skip_row, ffn_shard, out_shard, x_pieces)
    in_rows.got, prepared = tied(in_rows.got, prepared)
    marks, docs_row, masks, mats, bias_row, rate_row, skip_row, ffn_shard, out_shard, x_pieces = prepared
    in_rows, out_shard = tied(in_rows.end(), out_shard)
    w_in = gather_wide(in_rows)
    out_rows_all, x_pieces = tied(HeadRows(out_shard, micro_count).end(), x_pieces)
    x_low, ffn_shard = tied(ToBlocks(x_pieces).end(), ffn_shard)
    ffn_rows = HeadRows(ffn_shard, micro_count)
    w_in, out_rows_all = tied(w_in, out_rows_all)
    w_out = gather_wide(out_rows_all)
    x_tokens = x_low.astype(jnp.float32)

    small_at = scan_cols + heads
    w_scan, w_gate, w_qkv = split_at(w_in, (first_cols, inner, query_cols + kv_cols), 1)
    small_all = w_scan[:, small_at : small_at + small_cols].reshape(devices, -1).astype(jnp.float32)
    g_in, g_ffn, g_mamba, c_x, c_bc = split_at(
        small_all, (rows, rows, chan, taps * chan, taps * chan_bc), 1
    )
    gain_in_all = g_in.reshape(-1)
    gain_ffn_all = g_ffn.reshape(-1)
    g_mamba, c_x, c_bc = by_owner(g_mamba), by_owner(c_x), by_owner(c_bc)
    gain_mamba_row = g_mamba.reshape(1, -1)
    taps_all = jnp.concatenate(
        [
            c_x.reshape(devices, taps, chan).transpose(1, 0, 2).reshape(taps, -1),
            c_bc.reshape(devices, taps, chan_bc).transpose(1, 0, 2).reshape(taps, -1),
        ],
        axis=1,
    )
    cols = (inner, bc_cols, 0, inner // bc_cols, scan_cols // LANES)
    place = jnp.reshape(wide_id, (1,)).astype(jnp.int32)


    block_in = rms_scale(x_tokens, gain_in_all).astype(LOW)
    raw_qkv, block_in = tied(nn(block_in, w_qkv).astype(LOW), block_in)
    keys = Gathered(raw_qkv[:, query_cols:])
    keys.begin()
    keys.got, raw_scan, block_in = tied(keys.got, nn(block_in, w_scan), block_in)
    keys.end()
    rim = shifted(raw_scan[block_tok - 8 :, :scan_cols], "wide", 1)
    keys.begin()
    rim, raw_gate = tied(rim, nn(block_in, w_gate))
    rim = jnp.where(jnp.arange(8)[:, None] > 8 - taps, rim, 0.0)
    taps_ext = jnp.pad(taps_all, ((0, 8 - taps), (0, 0)))
    *feats, sent, total, decay_rows = mamba_local(raw_scan, rim, marks, taps_ext, bias_row, rate_row, cols, mats)
    keys.got, ffn_rows.got, sent = tied(keys.got, ffn_rows.got, sent)
    ffn_rows, w_out = tied(ffn_rows.end(), w_out)
    w_ffn = gather_wide(ffn_rows)
    keys.end()
    forward = Carried(sent, total, decay_rows, False)
    forward.begin()
    key_all = keys.rest()
    forward.end()
    q_rows = raw_qkv[:, :query_cols].T.reshape(QUERY_HEADS, HEAD_SIZE, block_tok)
    gy = ToBlocks(cotangent[:, 0])
    forward.begin()
    out_0, q_back_0 = attend(0, q_rows, key_all, masks, place)
    forward.got, gy.got, out_0, q_rows = tied(forward.got, gy.got, out_0, q_rows)
    forward.end()
    forward.sent, q_rows = tied(forward.sent, q_rows)
    forward.begin()
    out_1, q_back_1 = attend(1, q_rows, key_all, masks, place)
    forward.got, out_1 = tied(forward.got, out_1)
    state_in = forward.last()
    attn_low = jnp.concatenate([out_0, out_1], axis=0).reshape(query_cols, block_tok).astype(LOW)
    mamba_low, y_low, entry = mamba_mix(feats, raw_gate, marks, docs_row, state_in, skip_row, gain_mamba_row, mats)
    gy_plain = gy.end()
    d_out_low = mixed(gy_plain)
    out_both = jnp.concatenate(
        [w_out[:, i : i + width].reshape(devices, rows, width) for i in range(0, w_out.shape[1], width)], axis=1
    )
    out_both = by_owner(out_both)
    w_mamba_out = out_both[:, :out_rows].reshape(-1, width)
    w_attn_out = out_both[:, out_rows:].reshape(-1, width)

    resid = x_tokens + nn(mamba_low, w_mamba_out) + tn(attn_low, w_attn_out)
    normed_ffn, pull_ffn = jax.vjp(lambda values: rms_scale(values, gain_ffn_all), resid)
    ffn_in = normed_ffn.astype(LOW)
    fed, d_ffn_in, grad_ffn = feed_forward(ffn_in, d_out_low, gy_plain, w_ffn, folds, width)
    part_ffn = sum_wide(grad_ffn)
    out_low = (resid + fed).astype(LOW)
    (d_resid_norm,) = pull_ffn(d_ffn_in)
    d_resid = d_out_low.astype(jnp.float32) + d_resid_norm

    d_mix = d_resid.astype(LOW)
    d_gate_z, dy_low, sent_back, total, decay_rows = mamba_gate_back(
        nt(d_mix, w_mamba_out), y_low, raw_gate, feats, marks, gain_mamba_row, mats
    )
    backward = Carried(sent_back, total, decay_rows, True)
    backward.begin()
    d_attn = nt(w_attn_out, d_mix).astype(LOW).reshape(QUERY_HEADS, HEAD_SIZE, block_tok)
    backward.got, d_attn = tied(backward.got, d_attn)
    backward.end()
    backward.sent, d_attn = tied(backward.sent, d_attn)
    backward.begin()
    d_query_0, d_kv_0 = attend_back(0, q_back_0, out_0, d_attn, key_all, masks, place)
    backward.got, d_query_0, d_kv_0, d_attn = tied(backward.got, d_query_0, d_kv_0, d_attn)
    backward.end()
    backward.sent, d_attn, d_kv_0 = tied(backward.sent, d_attn, d_kv_0)
    backward.begin()
    core_0 = CoreSum(d_kv_0)
    d_query_1, d_kv_1 = attend_back(1, q_back_1, out_1, d_attn, key_all, masks, place)
    backward.got, core_0.got, d_query_1, d_kv_1 = tied(backward.got, core_0.got, d_query_1, d_kv_1)
    d_state = backward.last()
    d_state, d_kv_1, d_mix = tied(d_state, d_kv_1, d_mix)
    core_1 = CoreSum(d_kv_1)
    d_query = jnp.concatenate([d_query_0, d_query_1], axis=0).reshape(query_cols, block_tok).T
    d_mix_plain = plain(d_mix)
    grad_out = jnp.concatenate(
        [
            tn(mamba_low, d_mix_plain).astype(LOW).reshape(devices, out_rows, width),
            nn(attn_low, d_mix_plain).astype(LOW).reshape(devices, attn_rows, width),
        ],
        axis=1,
    ).reshape(devices, -1, rows, width)
    grad_out = by_place(grad_out)
    grad_gate = tn(block_in, d_gate_z).astype(LOW)
    early = jnp.concatenate(
        [grad_out[:, i].reshape(width, width) for i in range(grad_out.shape[1])] + [grad_gate], axis=1
    )
    core_1.got, early = tied(core_1.got, early)
    chip_sum = ChipSum(jnp.concatenate([core_0.end(), core_1.end()], axis=2))
    early, part_ffn = tied(early, part_ffn)
    part_early = sum_wide(early)
    own_ffn = HeadSum(part_ffn, micro_count)
    d_scan, grad_skip, grad_head, grad_taps, rim_back, edge = mamba_scan_back(
        feats, raw_scan, rim, taps_ext, marks, docs_row, dy_low, entry, d_state,
        skip_row, bias_row, rate_row, cols, mats,
    )
    chip_sum.got, own_ffn.got, d_scan, edge, rim_back, grad_taps, grad_head, grad_skip, d_query, out_low = tied(
        chip_sum.got, own_ffn.got, d_scan, edge, rim_back, grad_taps, grad_head, grad_skip, d_query, out_low
    )
    rim_came = shifted(rim_back, "wide", -1)
    out_back = FromBlocks(out_low, micro_count)
    d_kv = chip_sum.end()
    d_scan = lax.dynamic_update_slice(d_scan, (edge + rim_came).astype(LOW), (block_tok - 8, 0))
    grad_small = jnp.concatenate(
        [
            by_place(grad_taps[:taps, :inner].reshape(taps, devices, chan).transpose(1, 0, 2).reshape(devices, -1)),
            by_place(grad_taps[:taps, inner:].reshape(taps, devices, chan_bc).transpose(1, 0, 2).reshape(devices, -1)),
        ],
        axis=1,
    )
    grad_small = jnp.pad(grad_small, ((0, 0), (0, rows * small_cols - grad_small.shape[1])))
    grad_small = jnp.pad(
        grad_small.reshape(width, small_cols), ((0, 0), (heads, LANES - heads - small_cols))
    )
    late = last_grads(block_in, d_scan, d_query, d_kv, grad_small)

    out_back.got, late, part_early, d_scan, grad_head, grad_skip, own_ffn.got, own_ffn.own = tied(
        out_back.got, late, part_early, d_scan, grad_head, grad_skip, own_ffn.got, own_ffn.own
    )
    part_late = sum_wide(late)
    head_sums = jnp.concatenate(
        [grad_head[:2, :heads].reshape(-1), jnp.sum(grad_skip[0].reshape(heads, -1), axis=1)]
    )
    totals = EverySum(head_sums)
    totals.begin()
    totals.got, part_early, d_scan = tied(totals.got, part_early, d_scan)
    totals.end()
    own_early = HeadSum(part_early, micro_count)
    totals.begin()
    grad_x = input_back(d_scan, d_gate_z, d_query, d_kv, w_in, x_tokens, d_resid, gain_in_all[None])
    own_early.got, own_early.own, totals.got, grad_x = tied(own_early.got, own_early.own, totals.got, grad_x)
    totals.end()
    x_plain, own_ffn.got, own_ffn.own = tied(plain(grad_x), own_ffn.got, own_ffn.own)
    own_ffn = own_ffn.end()
    x_back = FromBlocks(x_plain, micro_count)
    totals.begin()
    g_ffn = split_at(own_ffn, (width,) * (3 * folds), 1)
    g_gate_w, g_up_w = unfolded(g_ffn[0::3]), unfolded(g_ffn[1::3])
    totals.got, g_gate_w, g_up_w = tied(totals.got, g_gate_w, g_up_w)
    totals.end()
    totals.begin()
    *g_out, g_gate = own_early.end((width,) * ((out_rows + attn_rows) // rows) + (inner,))
    out_done = plain(out_back.end())
    x_back.got, g_out, g_gate, out_done, part_late, totals.got, g_gate_w, g_up_w = tied(
        x_back.got, g_out, g_gate, out_done, part_late, totals.got, g_gate_w, g_up_w
    )
    totals.end()
    own_late = HeadSum(part_late, micro_count)
    summed = totals.rest()
    results = x_back.end()
    own_late.got, results = tied(own_late.got, results)
    per_head = summed[: 3 * heads].reshape(3, heads)
    gate_sum = jnp.sum(mamba_gate_w.astype(jnp.float32) * g_gate, axis=1, keepdims=True)
    summing = (lax.axis_index("head") < micro_count).astype(jnp.int32).reshape(1)
    g_x, g_bc, g_tail, g_q, g_kv, o_gain_in = owned_last(
        own_late.own,
        own_late.got,
        summing,
        gain_in[:, None],
        gate_sum,
        (mamba_in_w, mamba_bc_w, mamba_dt_w, attn_q_w, attention_key_value_weight),
        (inner, bc_cols, LANES, query_cols, kv_cols),
    )
    g_dt, g_small, _ = split_at(g_tail, (heads, small_cols, LANES - heads - small_cols), 1)
    o_conv_x, o_conv_bc, _ = split_at(
        g_small.reshape(-1), (taps * chan, taps * chan_bc, rows * small_cols - taps * (chan + chan_bc)), 0
    )
    g_mamba_out, g_attn_out = split_at(jnp.concatenate(g_out, axis=0), (out_rows, attn_rows), 0)
    def gain_grad(gain, pairs):
        total = 0.0
        for weight, grad in pairs:
            total = total + jnp.sum(weight.astype(jnp.float32) * grad, axis=1)
        return total / gain.astype(jnp.float32)

    o_gain_ffn = gain_grad(gain_ffn, ((ffn_gate_w, g_gate_w), (ffn_up_w, g_up_w)))
    o_gain_m = gain_grad(mamba_gain, ((mamba_out_w, g_mamba_out),))
    return (
        out_done[:, None],
        results[:, None],
        o_gain_in[:, 0],
        g_gate,
        g_x,
        g_bc,
        g_dt,
        per_head[0],
        per_head[1],
        per_head[2],
        o_conv_x.reshape(taps, chan),
        o_conv_bc.reshape(taps, chan_bc),
        o_gain_m,
        g_q,
        g_kv,
        g_mamba_out,
        g_attn_out,
        o_gain_ffn,
        g_gate_w,
        g_up_w,
        jnp.concatenate(g_ffn[2::3], axis=0),
    )


def solution(mesh):
    tokens = P(None, "wide", "head", None)
    matrix = P(ALL, None)
    vector = P(ALL)
    taps = P(None, ALL)
    in_specs = (
        (tokens, tokens, P(), vector)
        + (matrix,) * 4
        + (P(),) * 3
        + (taps, taps, vector)
        + (matrix,) * 4
        + (vector,)
        + (matrix,) * 3
    )
    out_specs = (
        (tokens, tokens, vector)
        + (matrix,) * 4
        + (P(),) * 3
        + (taps, taps, vector)
        + (matrix,) * 4
        + (vector,)
        + (matrix,) * 3
    )
    return jax.shard_map(
        per_device, mesh=mesh, in_specs=in_specs, out_specs=out_specs, check_vma=False
    )
```

```python
from functools import partial

import jax
import jax.numpy as jnp
from jax import lax
from jax.experimental import pallas as pl
from jax.experimental.pallas import tpu as pltpu
from jax.sharding import PartitionSpec as P

QUERY_HEADS = 8
KEY_VALUE_HEADS = 2
HEAD_SIZE = 64
GROUP = QUERY_HEADS // KEY_VALUE_HEADS
LANES = 128
LOW = jnp.bfloat16
FAR = -1e30
ALL = ("head", "wide")

epsilon = 1e-05
highest = lax.Precision.HIGHEST


def nn(left, right):
    return jnp.dot(left, right, preferred_element_type=jnp.float32)


def nt(left, right):
    return lax.dot_general(left, right, (((1,), (1,)), ((), ())), preferred_element_type=jnp.float32)


def tn(left, right):
    return lax.dot_general(left, right, (((0,), (0,)), ((), ())), preferred_element_type=jnp.float32)


def split_low(value, parts):
    terms = []
    for _ in range(parts):
        term = value.astype(LOW)
        terms.append(term)
        value = value - term.astype(jnp.float32)
    return terms


def shape(dims, kind=jnp.float32):
    return jax.ShapeDtypeStruct(dims, kind)


def shifted(value, axis, steps):
    count = lax.axis_size(axis)
    initial, last = (max(0, -steps), min(count, count - steps))
    return lax.ppermute(value, axis, [(source, source + steps) for source in range(initial, last)])


def swapped(value, axis, bit):
    count = lax.axis_size(axis)
    return lax.ppermute(value, axis, [(i, i ^ bit) for i in range(count)])


def pick(array, index, axis=0):
    return lax.dynamic_index_in_dim(array, index, axis, False)


def guess(us):
    return pl.CostEstimate(flops=int(us * 1e9), bytes_accessed=int(us * 3e6), transcendentals=0)


def tied(*values):
    return lax.optimization_barrier(values)


def sent_on(pieces, sources, receivers):
    count = lax.axis_size("head")
    place = lax.axis_index("head")
    got = []
    for step in range(1, count):
        pairs = [(i, (i + step) % count) for i in range(count)]
        pairs = [(i, k) for i, k in pairs if i < sources and k < receivers]
        got.append(lax.ppermute(pieces((place + step) % count), "head", pairs))
    return got


def put_together(own, got):
    place = lax.axis_index("head")
    count = len(got) + 1
    whole = lax.dynamic_update_index_in_dim(jnp.zeros((count,) + own.shape, own.dtype), own, place, 0)
    for step, array in enumerate(got, 1):
        whole = lax.dynamic_update_index_in_dim(whole, array, (place - step) % count, 0)
    return whole


class HeadRows:
    def __init__(self, own, receivers):
        self.own = own
        self.got = sent_on(lambda target: own, lax.axis_size("head"), receivers)

    def end(self):
        return put_together(self.own, self.got).reshape(-1, self.own.shape[1])


class ToBlocks:
    def __init__(self, pieces):
        micro_count = pieces.shape[0]
        place = lax.axis_index("head")

        def of(target):
            return pick(pieces, jnp.minimum(target, micro_count - 1))

        self.own = jnp.where(place < micro_count, of(place), jnp.zeros_like(pieces[0]))
        self.got = sent_on(of, lax.axis_size("head"), micro_count)

    def end(self):
        return put_together(self.own, self.got).reshape(-1, self.own.shape[1])


class FromBlocks:
    def __init__(self, block, micro_count):
        count = lax.axis_size("head")
        parts = block.reshape(count, block.shape[0] // count, block.shape[1])
        self.micro_count = micro_count
        self.own = pick(parts, lax.axis_index("head"))
        self.got = sent_on(lambda target: pick(parts, target), micro_count, count)

    def end(self):
        return put_together(self.own, self.got)[: self.micro_count]


class HeadSum:
    def __init__(self, part, sources, block=None):
        count = lax.axis_size("head")
        place = lax.axis_index("head")
        array = part.reshape(count, -1, part.shape[1])
        self.width = array.shape[2]
        self.sources = sources
        if block is not None:
            self.block_shape = (block.shape[0] // count, block.shape[1])
            array = jnp.concatenate([array, block.reshape(count, array.shape[1], -1)], axis=2)
        self.own = pick(array, place)
        self.got = sent_on(lambda target: pick(array, target), sources, count)

    def end(self, sizes=None):
        place = lax.axis_index("head")
        at, out = 0, []
        for size in sizes or (self.width,):
            cut = [array[:, at : at + size].astype(jnp.float32) for array in [self.own] + self.got]
            total = jnp.where(place < self.sources, cut[0], 0.0)
            for term in cut[1:]:
                total = total + term
            out.append(total)
            at += size
        return out if sizes else out[0]

    def end_block(self):
        own, got = self.own[:, self.width :], [array[:, self.width :] for array in self.got]
        whole = put_together(own, got)
        return whole.reshape((whole.shape[0],) + self.block_shape)[: self.sources]


def wide_bits():
    bits = []
    while 1 << (len(bits) + 1) <= lax.axis_size("wide"):
        bits.append(1 << len(bits))
    return bits


class EverySum:
    def __init__(self, value):
        self.value = value
        self.left = [("wide", bit) for bit in wide_bits()]
        bit = 1
        while bit < lax.axis_size("head"):
            self.left.append(("head", bit))
            bit *= 2

    def begin(self):
        self.got = swapped(self.value, *self.left.pop(0))

    def end(self):
        self.value = self.value + self.got

    def rest(self):
        while self.left:
            self.begin()
            self.end()
        return self.value


class Gathered:
    def __init__(self, own):
        bits = wide_bits()
        half = own.shape[1] // 2
        self.parts = [own[:, :half], own[:, half:]]
        self.left = [bits[1:], bits[:0:-1]]
        self.done = [[], []]

    def begin(self):
        self.got = [swapped(array, "wide", left[0]) for array, left in zip(self.parts, self.left)]

    def end(self):
        place = lax.axis_index("wide")
        for i, got in enumerate(self.got):
            bit = self.left[i].pop(0)
            mine = (place // bit) % 2
            array = self.parts[i]
            self.parts[i] = jnp.where(mine == 0, jnp.stack([array, got]), jnp.stack([got, array]))
            self.done[i].insert(0, bit)

    def rest(self):
        while self.left[0]:
            self.begin()
            self.end()
        arrays = []
        for array, done in zip(self.parts, self.done):
            ranks = [done.index(bit) for bit in sorted(done, reverse=True)]
            arrays.append(array.transpose(ranks + [len(done), len(done) + 1]))
        both = jnp.concatenate(arrays, axis=-1)
        got = swapped(both, "wide", 1)
        mine = lax.axis_index("wide") % 2
        stacked = jnp.where(mine == 0, jnp.stack([both, got], axis=-3), jnp.stack([got, both], axis=-3))
        return stacked.reshape(-1, both.shape[-1])


class CoreSum:
    def __init__(self, part):
        count = lax.axis_size("wide")
        mine = lax.axis_index("wide") % 2
        part = part.reshape(count // 2, 2, -1, part.shape[1])
        self.own = pick(part, mine, 1)
        self.got = swapped(pick(part, 1 - mine, 1), "wide", 1)

    def end(self):
        return (self.own.astype(jnp.float32) + self.got.astype(jnp.float32)).astype(self.own.dtype)


class ChipSum:
    def __init__(self, array):
        chip = lax.axis_index("wide") // 2
        self.own = pick(array, chip)
        self.got = [swapped(pick(array, chip ^ other), "wide", 2 * other) for other in range(1, array.shape[0])]

    def end(self):
        total = self.own.astype(jnp.float32)
        for array in self.got:
            total = total + array.astype(jnp.float32)
        return total.astype(self.own.dtype)


def sum_wide(array):
    return lax.psum_scatter(array, "wide", scatter_dimension=0, tiled=True)


def gather_wide(array):
    return lax.all_gather(array, "wide", axis=0, tiled=True)


class Carried:
    def __init__(self, sent, total, rows, backward):
        self.sent, self.total, self.rows = sent, total, rows
        self.state = jnp.zeros_like(total)
        self.backward = backward
        self.left = wide_bits()

    def begin(self):
        self.got = swapped(self.sent, "wide", self.left[0])

    def end(self):
        bit = self.left.pop(0)
        mine = (lax.axis_index("wide") // bit) % 2
        ahead = 1 - mine if self.backward else mine
        self.total, self.state, self.rows, self.sent = join(
            self.total, self.state, self.rows, self.got, jnp.reshape(ahead, (1,)).astype(jnp.int32)
        )

    def last(self):
        self.end()
        while self.left:
            self.begin()
            self.end()
        return self.state


def rms_scale(values, scales):
    return values * lax.rsqrt(jnp.mean(values * values, axis=-1, keepdims=True) + epsilon) * scales


def doc_index(starts, positions):
    passed = (starts[None, :] <= positions[:, None]).astype(jnp.int32)
    return jnp.sum(passed, axis=1) - 1


def split_at(array, sizes, axis):
    out, at = [], 0
    for size in sizes:
        out.append(lax.slice_in_dim(array, at, at + size, axis=axis))
        at += size
    return out


def packed(parts, rows):
    flat = jnp.concatenate([part.reshape(-1) for part in parts])
    columns = -(-flat.shape[0] // rows)
    return jnp.pad(flat, (0, rows * columns - flat.shape[0])).reshape(rows, columns)


CHUNK = 128
EXTRA = 16


def spread(value, spread_ref):
    return nn(jnp.concatenate(split_low(value, 2), axis=1), spread_ref[...])


def gathered(value, gather_ref):
    return nn(value.astype(LOW), gather_ref[...])


def gathered_fine(value, gather_ref):
    high, rest = split_low(value, 2)
    return nn(high, gather_ref[...]) + nn(rest, gather_ref[...])


def with_decay(state, decay):
    terms = split_low(decay, 3) + [jnp.zeros((EXTRA - 3, decay.shape[1]), LOW)]
    return jnp.concatenate([state.astype(LOW)] + terms, axis=0)


def silu_parts(value):
    sigma = jax.nn.sigmoid(value)
    return value * sigma, sigma * (1.0 + value * (1.0 - sigma))


def local_kernel(
    x_ref, xp_ref, bc_ref, bcp_ref, rimx_ref, rimb_ref, dt_ref, marks_ref, tapx_ref, tapb_ref, bias_ref, rate_ref, spread_ref,
    act_ref, slope_ref, bcact_ref, bcslope_ref, step_ref, cum_ref, sent_ref, state_ref, decay_ref,
):
    part = pl.program_id(0)
    marks = marks_ref[...]

    def conv(raw_ref, prev_ref, rim_ref, tap_ref):
        before = jnp.where(part == 0, rim_ref[...], prev_ref[...])
        both = jnp.concatenate([before, raw_ref[...]], axis=0)
        taps = 4
        total = None
        for i in range(taps):
            term = both[8 - taps + 1 + i : 8 - taps + 1 + i + CHUNK] * tap_ref[i : i + 1, :] * marks[:, i : i + 1]
            total = term if total is None else total + term
        return silu_parts(total)

    act, slope = conv(x_ref, xp_ref, rimx_ref, tapx_ref)
    act_ref[...] = act
    slope_ref[...] = slope.astype(LOW)
    bc, bc_slope = conv(bc_ref, bcp_ref, rimb_ref, tapb_ref)
    bcact_ref[...] = bc.astype(LOW)
    bcslope_ref[...] = bc_slope.astype(LOW)
    lane = lax.broadcasted_iota(jnp.int32, (CHUNK, LANES), 1)
    value = dt_ref[...] + bias_ref[0:1, :]
    softplus = jnp.maximum(value, 0.0) + jnp.log1p(jnp.exp(-jnp.abs(value)))
    step = jnp.where(rate_ref[0:1, :] < 0.0, softplus, 0.0)
    row = lax.broadcasted_iota(jnp.int32, (CHUNK, CHUNK), 0)
    col = lax.broadcasted_iota(jnp.int32, (CHUNK, CHUNK), 1)
    cum = jnp.dot((col <= row).astype(jnp.float32), step * rate_ref[0:1, :], precision=highest, preferred_element_type=jnp.float32)
    step_ref[...] = step
    cum_ref[...] = cum
    tail = jnp.exp(cum[CHUNK - 1 :] - cum) * marks[:, 5:6] * step
    weighted = (act * spread(tail, spread_ref)).astype(LOW)
    decay = spread(jnp.exp(cum[CHUNK - 8 :]) * marks[CHUNK - 8 :, 7:8], spread_ref)[7:8]
    own = tn(bc[:, :LANES].astype(LOW), weighted)

    @pl.when(part == 0)
    def _():
        state_ref[...] = own
        decay_ref[...] = jnp.ones_like(decay_ref)
        decay_ref[0:1, :] = decay

    @pl.when(part > 0)
    def _():
        state_ref[...] = state_ref[...] * decay + own
        decay_ref[0:1, :] = decay_ref[0:1, :] * decay

    @pl.when(part == pl.num_programs(0) - 1)
    def _():
        sent_ref[...] = with_decay(state_ref[...], decay_ref[0:1, :])


def join_kernel(ahead_ref, total_ref, state_ref, rows_ref, got_ref, total_out, state_out, rows_out, sent_out):
    size = total_ref.shape[0]
    got = got_ref[:size, :].astype(jnp.float32)
    extra = got_ref[size:, :].astype(jnp.float32)
    got_decay = extra[0:1] + extra[1:2] + extra[2:3]
    decay, sweep = rows_ref[0:1, :], rows_ref[1:2, :]
    rows_out[...] = jnp.ones_like(rows_out)
    rows_out[0:1, :] = decay * got_decay

    @pl.when(ahead_ref[0] == 1)
    def _():
        state_out[...] = state_ref[...] + sweep * got
        rows_out[1:2, :] = sweep * got_decay
        total_out[...] = total_ref[...] + decay * got

    @pl.when(ahead_ref[0] == 0)
    def _():
        state_out[...] = state_ref[...]
        rows_out[1:2, :] = sweep
        total_out[...] = got + got_decay * total_ref[...]

    sent_out[...] = with_decay(total_out[...], decay * got_decay)


def mix_kernel(
    act_ref, bcact_ref, z_ref, step_ref, cum_ref, marks_ref, docs_ref, first_ref, skip_ref, gain_ref, spread_ref, gather_ref,
    ym_ref, y_ref, entry_ref, state_ref, inner_ref,
):
    part = pl.program_id(0)

    @pl.when(part == 0)
    def _():
        state_ref[...] = first_ref[...]

    marks = marks_ref[...]
    cum = cum_ref[...]
    cum_rows = cum.T
    step = step_ref[...]
    b_mat = bcact_ref[:, :LANES]
    c_mat = bcact_ref[:, LANES:]
    act = act_ref[...]
    stepped = act * spread(step, spread_ref)
    low_stepped = stepped.astype(LOW)
    row = lax.broadcasted_iota(jnp.int32, (CHUNK, CHUNK), 0)
    col = lax.broadcasted_iota(jnp.int32, (CHUNK, CHUNK), 1)
    allowed = (row >= col) & (marks[:, 6:7] == docs_ref[0:1, :])
    gram = jnp.where(allowed, nt(c_mat, b_mat), 0.0)
    first = lax.broadcasted_iota(jnp.int32, (CHUNK, LANES), 1) < LANES // 2
    pairs = act.shape[1] // LANES
    for pair in range(pairs):
        parts = []
        for head in (2 * pair, 2 * pair + 1):
            gaps = jnp.minimum(cum[:, head : head + 1] - cum_rows[head : head + 1, :], 0.0)
            parts.append((jnp.exp(gaps) * gram).astype(LOW))
        values = low_stepped[:, pair * LANES : (pair + 1) * LANES]
        zero = jnp.zeros_like(values)
        inner_ref[:, pair * LANES : (pair + 1) * LANES] = nn(
            jnp.concatenate(parts, axis=1),
            jnp.concatenate([jnp.where(first, values, zero), jnp.where(first, zero, values)], axis=0),
        )
    state = state_ref[...]
    low_state = state.astype(LOW)
    entry_ref[0] = low_state
    entering = spread(jnp.exp(cum) * marks[:, 4:5], spread_ref)
    y = inner_ref[...] + nn(c_mat, low_state) * entering + skip_ref[0:1, :] * act
    y_ref[...] = y
    gated = y * silu_parts(z_ref[...])[0]
    scale = lax.rsqrt(gathered(gated * gated, gather_ref) * (2.0 / LANES) + epsilon)
    ym_ref[...] = (gated * spread(scale, spread_ref) * gain_ref[0:1, :]).astype(LOW)
    tail = jnp.exp(cum[CHUNK - 1 :] - cum) * marks[:, 5:6]
    weighted = (stepped * spread(tail, spread_ref)).astype(LOW)
    decay = spread(jnp.exp(cum[CHUNK - 8 :]) * marks[CHUNK - 8 :, 7:8], spread_ref)[7:8]
    state_ref[...] = state * decay + tn(b_mat, weighted)


def gate_back_kernel(
    dym_ref, y_ref, z_ref, bcact_ref, cum_ref, marks_ref, gain_ref, spread_ref, gather_ref,
    dz_ref, dy_ref, sent_ref, state_ref, decay_ref,
):
    part = pl.program_id(0)
    marks = marks_ref[...]
    cum = cum_ref[...]
    y = y_ref[...]
    silu, slope = silu_parts(z_ref[...])
    gated = y * silu
    scale = lax.rsqrt(gathered(gated * gated, gather_ref) * (2.0 / LANES) + epsilon)
    wide_scale = spread(scale, spread_ref)
    d_normed = dym_ref[...]
    u = d_normed * gain_ref[0:1, :]
    inner = gathered(u * gated, gather_ref) * (2.0 / LANES) * scale * scale * scale
    d_gated = u * wide_scale - gated * spread(inner, spread_ref)
    dz_ref[...] = (d_gated * y * slope).astype(LOW)
    dy = d_gated * silu
    dy_ref[...] = dy
    entering = spread(jnp.exp(cum) * marks[:, 4:5], spread_ref)
    own = tn(bcact_ref[:, LANES:], (dy * entering).astype(LOW))
    decay = spread(jnp.exp(cum[CHUNK - 8 :]) * marks[CHUNK - 8 :, 7:8], spread_ref)[7:8]

    @pl.when(part == 0)
    def _():
        state_ref[...] = own
        decay_ref[...] = jnp.ones_like(decay_ref)
        decay_ref[0:1, :] = decay

    @pl.when(part > 0)
    def _():
        state_ref[...] = state_ref[...] * decay + own
        decay_ref[0:1, :] = decay_ref[0:1, :] * decay

    @pl.when(part == pl.num_programs(0) - 1)
    def _():
        sent_ref[...] = with_decay(state_ref[...], decay_ref[0:1, :])


def scan_back_kernel(
    act_ref, slope_ref, bcact_ref, bcslope_ref, dt_ref, step_ref, cum_ref, marks_ref, docs_ref, dy_ref, entry_ref, first_ref,
    skip_ref, bias_ref, rate_ref, spread_ref, gather_ref, x_ref, xp_ref, bc_ref, bcp_ref, rimx_ref, rimb_ref, tapx_ref, tapb_ref,
    dscan_ref, dskip_ref, dhead_ref, dtap_ref, rim_ref, edge_ref, state_ref, inner_ref, rows_ref, next_ref, nextm_ref,
):
    part = pl.program_id(0)

    @pl.when(part == 0)
    def _():
        state_ref[...] = first_ref[...]
        rows_ref[...] = jnp.zeros_like(rows_ref)
        dskip_ref[...] = jnp.zeros_like(dskip_ref)
        dhead_ref[...] = jnp.zeros_like(dhead_ref)
        dtap_ref[...] = jnp.zeros_like(dtap_ref)
        next_ref[...] = jnp.zeros_like(next_ref)
        nextm_ref[...] = jnp.zeros_like(nextm_ref)

    marks = marks_ref[...]
    cum = cum_ref[...]
    cum_rows = cum.T
    step = step_ref[...]
    b_mat = bcact_ref[:, :LANES]
    c_mat = bcact_ref[:, LANES:]
    act = act_ref[...]
    wide_step = spread(step, spread_ref)
    stepped = act * wide_step
    low_stepped = stepped.astype(LOW)
    dy = dy_ref[...]
    low_dy = dy.astype(LOW)
    row = lax.broadcasted_iota(jnp.int32, (CHUNK, CHUNK), 0)
    col = lax.broadcasted_iota(jnp.int32, (CHUNK, CHUNK), 1)
    allowed = (row <= col) & (marks[:, 6:7] == docs_ref[0:1, :])
    gram = jnp.where(allowed, nt(b_mat, c_mat), 0.0)
    first = lax.broadcasted_iota(jnp.int32, (CHUNK, LANES), 1) < LANES // 2
    lane = lax.broadcasted_iota(jnp.int32, (CHUNK, LANES), 1)
    pairs = act.shape[1] // LANES
    d_gram = jnp.zeros((CHUNK, CHUNK), jnp.float32)
    leaving = jnp.zeros((CHUNK, LANES), jnp.float32)
    for pair in range(pairs):
        cols = slice(pair * LANES, (pair + 1) * LANES)
        values, grads = low_stepped[:, cols], low_dy[:, cols]
        zero = jnp.zeros_like(values)
        d_weights = nt(jnp.concatenate([jnp.where(first, values, zero), jnp.where(first, zero, values)], axis=0), grads)
        parts = []
        for i, head in enumerate((2 * pair, 2 * pair + 1)):
            fade = jnp.exp(jnp.minimum(cum_rows[head : head + 1, :] - cum[:, head : head + 1], 0.0))
            d_weight = d_weights[i * CHUNK : (i + 1) * CHUNK]
            weight = fade * gram
            d_gram = d_gram + d_weight * fade
            moved = d_weight * weight
            rows_ref[head : head + 1, :] = jnp.sum(moved, axis=0, keepdims=True)
            leaving = jnp.where(lane == head, jnp.sum(moved, axis=1, keepdims=True), leaving)
            parts.append(weight.astype(LOW))
        inner_ref[:, cols] = nn(
            jnp.concatenate(parts, axis=1),
            jnp.concatenate([jnp.where(first, grads, zero), jnp.where(first, zero, grads)], axis=0),
        )
    d_state = state_ref[...]
    low_d_state = d_state.astype(LOW)
    entry = entry_ref[0]
    entering = spread(jnp.exp(cum) * marks[:, 4:5], spread_ref)
    tail = spread(jnp.exp(cum[CHUNK - 1 :] - cum) * marks[:, 5:6], spread_ref)
    from_state = nn(b_mat, low_d_state) * tail
    d_stepped = inner_ref[...] + from_state
    out_moved = gathered_fine(stepped * from_state, gather_ref)
    entering_dy = dy * entering
    in_moved = gathered_fine(entering_dy * nn(c_mat, entry), gather_ref)
    low_entering_dy = entering_dy.astype(LOW)
    low_gram = jnp.where(allowed, d_gram, 0.0).astype(LOW)
    d_b = nt((stepped * tail).astype(LOW), low_d_state) + nn(low_gram, c_mat)
    d_c = nt(low_entering_dy, entry) + tn(low_gram, b_mat)
    decay_small = jnp.exp(cum[CHUNK - 8 :]) * marks[CHUNK - 8 :, 7:8]
    decay = spread(decay_small, spread_ref)[7:8]
    overlap = jnp.sum(d_state * entry.astype(jnp.float32), axis=0, keepdims=True)
    d_decay = nn(jnp.concatenate(split_low(jnp.broadcast_to(overlap, (8, overlap.shape[1])), 2), axis=0), gather_ref[...])
    at_end = jnp.sum(out_moved, axis=0, keepdims=True) + (d_decay[0:1] + d_decay[8:9]) * decay_small[7:8]
    d_cum = rows_ref[...].T - leaving + in_moved - out_moved
    d_cum = d_cum + jnp.where(lax.broadcasted_iota(jnp.int32, d_cum.shape, 0) == CHUNK - 1, at_end, 0.0)
    d_log = jnp.dot((row <= col).astype(jnp.float32), d_cum, precision=highest, preferred_element_type=jnp.float32)
    rate = rate_ref[0:1, :]
    d_step = gathered_fine(act * d_stepped, gather_ref) + d_log * rate
    d_dt = d_step * jax.nn.sigmoid(dt_ref[...] + bias_ref[0:1, :])
    d_dt = jnp.where(rate < 0.0, d_dt, 0.0)
    inner = act.shape[1]
    scan = inner + 2 * LANES
    dscan_ref[:, scan:] = d_dt.astype(LOW)
    dhead_ref[0:1, :] += jnp.sum(d_dt, axis=0, keepdims=True)
    dhead_ref[1:2, :] += jnp.sum(d_log * rate * step, axis=0, keepdims=True)
    dskip_ref[0:1, :] += jnp.sum(dy * act, axis=0, keepdims=True)
    taps = 4
    marks_ext = jnp.concatenate([marks, nextm_ref[...]], axis=0)

    def conv_back(d_pre, lanes, raw_ref, prev_ref, edge_raw_ref, tap_ref):
        before = jnp.where(part == pl.num_programs(0) - 1, edge_raw_ref[...], prev_ref[...])
        raw = jnp.concatenate([before, raw_ref[...]], axis=0)
        ext = jnp.concatenate([d_pre, next_ref[:, lanes]], axis=0)
        top = jnp.concatenate([jnp.zeros_like(ext[:8]), d_pre[:8]], axis=0)
        top_marks = jnp.concatenate([marks[:8], marks[:8]], axis=0)
        d_raw, rim = None, None
        for i in range(taps):
            ahead = taps - 1 - i
            tap = tap_ref[i : i + 1, :]
            masked = d_pre * marks[:, i : i + 1]
            dtap_ref[i : i + 1, lanes] += jnp.sum(masked * raw[8 - ahead : 8 - ahead + CHUNK], axis=0, keepdims=True)
            term = (ext * marks_ext[:, i : i + 1])[ahead : ahead + CHUNK] * tap
            d_raw = term if d_raw is None else d_raw + term
            if ahead:
                term = (top * top_marks[:, i : i + 1])[ahead : ahead + 8] * tap
                rim = term if rim is None else rim + term
        next_ref[:, lanes] = d_pre[:8]
        dscan_ref[:, lanes] = d_raw.astype(LOW)
        rim_ref[:, lanes] = rim

        @pl.when(part == 0)
        def _():
            edge_ref[:, lanes] = d_raw[CHUNK - 8 :]

    conv_back(
        (d_stepped * wide_step + dy * skip_ref[0:1, :]) * slope_ref[...].astype(jnp.float32),
        slice(0, inner), x_ref, xp_ref, rimx_ref, tapx_ref,
    )
    conv_back(
        jnp.concatenate([d_b, d_c], axis=1) * bcslope_ref[...].astype(jnp.float32),
        slice(inner, scan), bc_ref, bcp_ref, rimb_ref, tapb_ref,
    )
    nextm_ref[...] = marks[:8]
    state_ref[...] = d_state * decay + tn(c_mat, low_entering_dy)


def head_matrices(inner, heads):
    owner = jnp.arange(inner, dtype=jnp.int32) // (inner // heads)
    gather_m = (owner[:, None] == jnp.arange(LANES, dtype=jnp.int32)[None, :]).astype(LOW)
    return jnp.concatenate([gather_m.T, gather_m.T], axis=0), gather_m


def lanes_row(vector):
    return jnp.pad(vector, (0, LANES - vector.shape[0]))[None, :]


def call(kernel, name, us, parts, ins, outs, scratch, reverse=False):
    def spec(block, how):
        if how == "part":
            how = lambda c: (c,) + (0,) * (len(block) - 1)
        elif how == "whole":
            how = lambda c: (0,) * len(block)
        elif isinstance(how, int):
            column = how
            how = lambda c: (c, column)

        def index(c):
            return how(parts - 1 - c if reverse else c)

        return pl.BlockSpec(block, index)

    return pl.pallas_call(
        kernel,
        grid=(parts,),
        in_specs=[spec(block, how) for _, block, how in ins],
        out_specs=[spec(block, how) for _, block, how in outs],
        scratch_shapes=scratch,
        out_shape=[shape for shape, _, _ in outs],
        compiler_params=pltpu.CompilerParams(vmem_limit_bytes=56 * 2**20),
        cost_estimate=guess(us),
        name=name,
    )(*[array for array, _, _ in ins])


def mamba_local(raw, rim, marks, taps, bias, rate, cols, mats):
    length = raw.shape[0]
    parts = length // CHUNK
    inner, n2, x_at, bc_at, dt_at = cols
    before = CHUNK // 8

    def prev(column):
        return lambda c: (jnp.maximum(c * before - 1, 0), column)

    return call(
        local_kernel,
        "mamba_local",
        11,
        parts,
        [
            (raw, (CHUNK, inner), x_at),
            (raw, (8, inner), prev(x_at)),
            (raw, (CHUNK, n2), bc_at),
            (raw, (8, n2), prev(bc_at)),
            (rim[:, :inner], (8, inner), "whole"),
            (rim[:, inner:], (8, n2), "whole"),
            (raw, (CHUNK, LANES), dt_at),
            (marks, (CHUNK, LANES), "part"),
            (taps[:, :inner], (8, inner), "whole"),
            (taps[:, inner:], (8, n2), "whole"),
            (bias, (1, LANES), "whole"),
            (rate, (1, LANES), "whole"),
            (mats[0], mats[0].shape, "whole"),
        ],
        [
            (shape((length, inner)), (CHUNK, inner), "part"),
            (shape((length, inner), LOW), (CHUNK, inner), "part"),
            (shape((length, n2), LOW), (CHUNK, n2), "part"),
            (shape((length, n2), LOW), (CHUNK, n2), "part"),
            (shape((length, LANES)), (CHUNK, LANES), "part"),
            (shape((length, LANES)), (CHUNK, LANES), "part"),
            (shape((n2 // 2 + EXTRA, inner), LOW), (n2 // 2 + EXTRA, inner), "whole"),
            (shape((n2 // 2, inner)), (n2 // 2, inner), "whole"),
            (shape((8, inner)), (8, inner), "whole"),
        ],
        [],
    )


def mamba_mix(feats, raw, marks, docs, state, skip, gain, mats):
    act, slope, bcact, bcslope, step, cum = feats
    length, inner = act.shape
    parts = length // CHUNK
    n2 = bcact.shape[1]
    return call(
        mix_kernel,
        "mamba_mix",
        11,
        parts,
        [
            (act, (CHUNK, inner), "part"),
            (bcact, (CHUNK, n2), "part"),
            (raw, (CHUNK, inner), 0),
            (step, (CHUNK, LANES), "part"),
            (cum, (CHUNK, LANES), "part"),
            (marks, (CHUNK, LANES), "part"),
            (docs, (8, CHUNK), lambda c: (0, c)),
            (state, state.shape, "whole"),
            (skip, (1, inner), "whole"),
            (gain, (1, inner), "whole"),
            (mats[0], mats[0].shape, "whole"),
            (mats[1], mats[1].shape, "whole"),
        ],
        [
            (shape((length, inner), LOW), (CHUNK, inner), "part"),
            (shape((length, inner)), (CHUNK, inner), "part"),
            (shape((parts, n2 // 2, inner), LOW), (1, n2 // 2, inner), "part"),
        ],
        [pltpu.VMEM((n2 // 2, inner), jnp.float32), pltpu.VMEM((CHUNK, inner), jnp.float32)],
    )


def mamba_gate_back(d_normed, y, raw, feats, marks, gain, mats):
    act, slope, bcact, bcslope, step, cum = feats
    length, inner = act.shape
    parts = length // CHUNK
    n2 = bcact.shape[1]
    return call(
        gate_back_kernel,
        "mamba_gate_back",
        11,
        parts,
        [
            (d_normed, (CHUNK, inner), "part"),
            (y, (CHUNK, inner), "part"),
            (raw, (CHUNK, inner), 0),
            (bcact, (CHUNK, n2), "part"),
            (cum, (CHUNK, LANES), "part"),
            (marks, (CHUNK, LANES), "part"),
            (gain, (1, inner), "whole"),
            (mats[0], mats[0].shape, "whole"),
            (mats[1], mats[1].shape, "whole"),
        ],
        [
            (shape((length, inner), LOW), (CHUNK, inner), "part"),
            (shape((length, inner)), (CHUNK, inner), "part"),
            (shape((n2 // 2 + EXTRA, inner), LOW), (n2 // 2 + EXTRA, inner), "whole"),
            (shape((n2 // 2, inner)), (n2 // 2, inner), "whole"),
            (shape((8, inner)), (8, inner), "whole"),
        ],
        [],
        reverse=True,
    )


def mamba_scan_back(feats, raw, rim, taps, marks, docs, dy, entry, state, skip, bias, rate, cols, mats):
    act, slope, bcact, bcslope, step, cum = feats
    length, inner = act.shape
    parts = length // CHUNK
    n2 = bcact.shape[1]
    x_at, bc_at, dt_at = cols[2:]
    scan = inner + n2

    def prev(column):
        return lambda c: (jnp.maximum(c * (CHUNK // 8) - 1, 0), column)

    return call(
        scan_back_kernel,
        "mamba_scan_back",
        23,
        parts,
        [
            (act, (CHUNK, inner), "part"),
            (slope, (CHUNK, inner), "part"),
            (bcact, (CHUNK, n2), "part"),
            (bcslope, (CHUNK, n2), "part"),
            (raw, (CHUNK, LANES), dt_at),
            (step, (CHUNK, LANES), "part"),
            (cum, (CHUNK, LANES), "part"),
            (marks, (CHUNK, LANES), "part"),
            (docs, (8, CHUNK), lambda c: (0, c)),
            (dy, (CHUNK, inner), "part"),
            (entry, (1, n2 // 2, inner), "part"),
            (state, state.shape, "whole"),
            (skip, (1, inner), "whole"),
            (bias, (1, LANES), "whole"),
            (rate, (1, LANES), "whole"),
            (mats[0], mats[0].shape, "whole"),
            (mats[1], mats[1].shape, "whole"),
            (raw, (CHUNK, inner), x_at),
            (raw, (8, inner), prev(x_at)),
            (raw, (CHUNK, n2), bc_at),
            (raw, (8, n2), prev(bc_at)),
            (rim[:, :inner], (8, inner), "whole"),
            (rim[:, inner:], (8, n2), "whole"),
            (taps[:, :inner], (8, inner), "whole"),
            (taps[:, inner:], (8, n2), "whole"),
        ],
        [
            (shape((length, scan + LANES), LOW), (CHUNK, scan + LANES), "part"),
            (shape((8, inner)), (8, inner), "whole"),
            (shape((8, LANES)), (8, LANES), "whole"),
            (shape((8, scan)), (8, scan), "whole"),
            (shape((8, scan)), (8, scan), "whole"),
            (shape((8, scan)), (8, scan), "whole"),
        ],
        [
            pltpu.VMEM((n2 // 2, inner), jnp.float32),
            pltpu.VMEM((CHUNK, inner), jnp.float32),
            pltpu.VMEM((LANES, CHUNK), jnp.float32),
            pltpu.VMEM((8, scan), jnp.float32),
            pltpu.VMEM((8, LANES), jnp.float32),
        ],
        reverse=True,
    )


def join(total, state, rows, got, ahead):
    whole = pl.BlockSpec(memory_space=pltpu.VMEM)
    return pl.pallas_call(
        join_kernel,
        in_specs=[pl.BlockSpec(memory_space=pltpu.SMEM)] + [whole] * 4,
        out_specs=[whole] * 4,
        out_shape=[shape(total.shape), shape(total.shape), shape(rows.shape), shape(got.shape, LOW)],
        compiler_params=pltpu.CompilerParams(vmem_limit_bytes=32 * 2**20),
        cost_estimate=guess(2),
        name="join",
    )(ahead, total, state, rows, got)


BOTH = 4
ONES = 16


def causal(scores):
    key_row = lax.broadcasted_iota(jnp.int32, scores.shape, 0)
    query = lax.broadcasted_iota(jnp.int32, scores.shape, 1)
    return jnp.where(key_row <= query, scores, FAR)


def attend_kernel(place_ref, q_ref, far_ref, kv_ref, extra_ref, o_ref, qb_ref, keys_ref, values_ref, acc_ref):
    blk = q_ref.shape[2]
    last = place_ref[0]

    @pl.when(pl.program_id(0) == 0)
    def _():
        first = lax.broadcasted_iota(jnp.int32, (blk, LANES), 1) < HEAD_SIZE

        @pl.loop(0, last + 1)
        def _(block):
            rows = pl.ds(pl.multiple_of(block * blk, blk), blk)
            both = kv_ref[rows, :]
            keys_ref[rows, :] = jnp.where(first, both, extra_ref[rows, :])
            values_ref[:ONES, rows] = jnp.ones((ONES, blk), LOW)
            values_ref[ONES:, rows] = both.astype(jnp.float32).T[HEAD_SIZE:].astype(LOW)

    queries = [
        jnp.concatenate([q_ref[i] * jnp.asarray(HEAD_SIZE ** (-0.5), LOW), far_ref[...]], axis=0)
        for i in range(BOTH)
    ]
    acc_ref[...] = jnp.zeros_like(acc_ref)

    def step(block, tops, diagonal):
        rows = pl.ds(pl.multiple_of(block * blk, blk), blk)
        keys, values = keys_ref[rows, :], values_ref[:, rows]
        new_tops = []
        for i in range(BOTH):
            scores = nn(keys, queries[i])
            if diagonal:
                scores = causal(scores)
            new_top = jnp.maximum(tops[i], jnp.max(scores, axis=0, keepdims=True))
            probs = jnp.exp(scores - new_top).astype(LOW)
            acc_ref[i] = acc_ref[i] * jnp.exp(tops[i] - new_top) + nn(values, probs)
            new_tops.append(new_top)
        return tuple(new_tops)

    tops = (jnp.full((1, blk), FAR, jnp.float32),) * BOTH
    tops = lax.fori_loop(0, last, lambda block, tops: step(block, tops, False), tops)
    tops = step(last, tops, True)
    row = lax.broadcasted_iota(jnp.int32, (HEAD_SIZE, blk), 0)
    for i in range(BOTH):
        total = acc_ref[i, 0:1, :]
        o_ref[i] = acc_ref[i, ONES:, :] / total
        extra = far_ref[...].astype(jnp.float32)
        for at, term in enumerate(split_low(-(tops[i] + jnp.log(total)), 3)):
            extra = jnp.where(row == 4 + at, term.astype(jnp.float32), extra)
        qb_ref[i] = jnp.concatenate([queries[i][:HEAD_SIZE], extra.astype(LOW)], axis=0)


def attend_back_kernel(place_ref, qb_ref, dot_ref, o_ref, kv_ref, extra_ref, dq_ref, dkv_ref, keys_ref, rows_ref, values_ref, acc_ref, dqa_ref):
    blk = qb_ref.shape[2]
    last = place_ref[0]
    member = pl.program_id(0)

    @pl.when(member == 0)
    def _():
        acc_ref[...] = jnp.zeros_like(acc_ref)
        lane = lax.broadcasted_iota(jnp.int32, (blk, LANES), 1)
        ones = jnp.where(lane < 3, 1.0, 0.0).astype(LOW)

        @pl.loop(0, last + 1)
        def _(block):
            rows = pl.ds(pl.multiple_of(block * blk, blk), blk)
            both = kv_ref[rows, :]
            keys_ref[rows, :] = jnp.where(lane < HEAD_SIZE, both, extra_ref[rows, :])
            values_ref[rows, :] = jnp.where(lane < HEAD_SIZE, ones, both)
            rows_ref[:, rows] = both.astype(jnp.float32).T[:HEAD_SIZE].astype(LOW)

    row = lax.broadcasted_iota(jnp.int32, (HEAD_SIZE, blk), 0)
    none = jnp.zeros((HEAD_SIZE, blk), jnp.float32)
    queries, d_outs, pairs = [], [], []
    for i in range(BOTH):
        queries.append(qb_ref[i])
        d_out = dot_ref[i].astype(jnp.float32)
        row_dot = jnp.sum(d_out * o_ref[i], axis=0, keepdims=True)
        extra = none
        for at, term in enumerate(split_low(-row_dot, 3)):
            extra = jnp.where(row == at, term.astype(jnp.float32), extra)
        d_outs.append(jnp.concatenate([extra, d_out], axis=0).astype(LOW))
        q_part = jnp.concatenate([qb_ref[i, :HEAD_SIZE, :].astype(jnp.float32), none], axis=0)
        pairs.append(jnp.concatenate([q_part.T, jnp.concatenate([none, d_out], axis=0).T], axis=0).astype(LOW))
    dqa_ref[...] = jnp.zeros_like(dqa_ref)

    def step(block, diagonal):
        rows = pl.ds(pl.multiple_of(block * blk, blk), blk)
        keys, values, key_rows = keys_ref[rows, :], values_ref[rows, :], rows_ref[:, rows]
        total = acc_ref[rows, :]
        for i in range(BOTH):
            logs = nn(keys, queries[i])
            if diagonal:
                logs = causal(logs)
            probs = jnp.exp(logs)
            d_scores = (probs * nn(values, d_outs[i])).astype(LOW)
            total = total + nn(jnp.concatenate([d_scores, probs.astype(LOW)], axis=1), pairs[i])
            dqa_ref[i] += nn(key_rows, d_scores)
        acc_ref[rows, :] = total

    @pl.loop(0, last)
    def _(block):
        step(block, False)

    step(last, True)
    dq_ref[...] = (dqa_ref[...] * HEAD_SIZE ** (-0.5)).astype(LOW)

    @pl.when(member == GROUP // BOTH - 1)
    def _():
        dkv_ref[...] = acc_ref[...].astype(LOW)


def attend_specs(blk, total, group):
    mine = group * (GROUP // BOTH)
    return dict(
        narrow=pl.BlockSpec((BOTH, HEAD_SIZE, blk), lambda r, p: (mine + r, 0, 0)),
        own_narrow=pl.BlockSpec((BOTH, HEAD_SIZE, blk), lambda r, p: (r, 0, 0)),
        own_broad=pl.BlockSpec((BOTH, LANES, blk), lambda r, p: (r, 0, 0)),
        kv=pl.BlockSpec((total, LANES), lambda r, p: (0, group)),
        extra=pl.BlockSpec((total, LANES), lambda r, p: (0, 0)),
        far=pl.BlockSpec((HEAD_SIZE, blk), lambda r, p: (0, 0)),
    )


def attend_masks(doc_here, key_doc, doc_count):
    docs = jnp.arange(HEAD_SIZE, dtype=jnp.int32)
    far = jnp.where((docs[:, None] != doc_here[None, :]) & (docs[:, None] < doc_count), FAR, 0.0).astype(LOW)
    lane = jnp.arange(LANES, dtype=jnp.int32)[None, :] - HEAD_SIZE
    extra = ((key_doc[:, None] == lane) | ((lane >= doc_count) & (lane < doc_count + 3))).astype(LOW)
    return far, extra


def attend(group, q_rows, key_all, masks, place):
    blk = q_rows.shape[2]
    total = key_all.shape[0]
    specs = attend_specs(blk, total, group)
    return pl.pallas_call(
        attend_kernel,
        grid_spec=pltpu.PrefetchScalarGridSpec(
            num_scalar_prefetch=1,
            grid=(GROUP // BOTH,),
            in_specs=[specs["narrow"], specs["far"], specs["kv"], specs["extra"]],
            out_specs=[specs["own_narrow"], specs["own_broad"]],
            scratch_shapes=[
                pltpu.VMEM((total, LANES), LOW),
                pltpu.VMEM((HEAD_SIZE + ONES, total), LOW),
                pltpu.VMEM((BOTH, HEAD_SIZE + ONES, blk), jnp.float32),
            ],
        ),
        out_shape=[shape((GROUP, HEAD_SIZE, blk)), shape((GROUP, LANES, blk), LOW)],
        compiler_params=pltpu.CompilerParams(vmem_limit_bytes=56 * 2**20),
        cost_estimate=guess(17),
        name="attend",
    )(place, q_rows, masks[0], key_all, masks[1])


def attend_back(group, q_back, out, d_rows, key_all, masks, place):
    blk = d_rows.shape[2]
    total = key_all.shape[0]
    specs = attend_specs(blk, total, group)
    return pl.pallas_call(
        attend_back_kernel,
        grid_spec=pltpu.PrefetchScalarGridSpec(
            num_scalar_prefetch=1,
            grid=(GROUP // BOTH,),
            in_specs=[specs["own_broad"], specs["narrow"], specs["own_narrow"], specs["kv"], specs["extra"]],
            out_specs=[specs["own_narrow"], specs["extra"]],
            scratch_shapes=[
                pltpu.VMEM((total, LANES), LOW),
                pltpu.VMEM((HEAD_SIZE, total), LOW),
                pltpu.VMEM((total, LANES), LOW),
                pltpu.VMEM((total, LANES), jnp.float32),
                pltpu.VMEM((BOTH, HEAD_SIZE, blk), jnp.float32),
            ],
        ),
        out_shape=[shape((GROUP, HEAD_SIZE, blk), LOW), shape((total, LANES), LOW)],
        compiler_params=pltpu.CompilerParams(vmem_limit_bytes=16 * 2**20 + 2816 * total),
        cost_estimate=guess(27),
        name="attend_back",
    )(place, q_back, d_rows, out, key_all, masks[1])


PIECE = 256


def feed_kernel(x_ref, gy_ref, plain_ref, w_ref, out_ref, dx_ref, grad_ref, xt_ref):
    fold = w_ref.shape[1] // 3

    @pl.when(pl.program_id(0) == 0)
    def _():
        out_ref[...] = jnp.zeros_like(out_ref)
        dx_ref[...] = jnp.zeros_like(dx_ref)
        xt_ref[...] = x_ref[...].astype(jnp.float32).T.astype(LOW)

    @pl.loop(0, fold // PIECE)
    def _(piece):
        at = pl.multiple_of(piece * PIECE, PIECE)
        gate_cols = pl.ds(at, PIECE)
        up_cols = pl.ds(pl.multiple_of(fold + at, PIECE), PIECE)
        down_cols = pl.ds(2 * fold, fold)
        w_gate, w_up, w_down = w_ref[:, gate_cols], w_ref[:, up_cols], w_ref[gate_cols, down_cols]
        x, gy = x_ref[...], gy_ref[...]
        gate, up = nn(x, w_gate), nn(x, w_up)
        sigma = jax.nn.sigmoid(gate)
        silu = gate * sigma
        act = silu * up
        d_act = nt(gy, w_down)
        d_gate = (d_act * up * sigma * (1.0 + gate * (1.0 - sigma))).astype(LOW)
        d_up = (d_act * silu).astype(LOW)
        out_ref[...] += nn(act.astype(LOW), w_down)
        dx_ref[...] += nt(d_gate, w_gate) + nt(d_up, w_up)
        x_t = xt_ref[...]
        grad_ref[:, gate_cols] = nn(x_t, d_gate).astype(LOW)
        grad_ref[:, up_cols] = nn(x_t, d_up).astype(LOW)
        grad_ref[gate_cols, down_cols] = nn(act.T.astype(LOW), plain_ref[...]).astype(LOW)


def feed_forward(x, gy, plain, w, folds, fold):
    tokens, width = x.shape
    whole = pl.BlockSpec((tokens, width), lambda j: (0, 0))
    return pl.pallas_call(
        feed_kernel,
        grid=(folds,),
        in_specs=[whole, whole, whole, pl.BlockSpec((width, 3 * fold), lambda j: (0, j))],
        out_specs=[whole, whole, pl.BlockSpec((width, 3 * fold), lambda j: (0, j))],
        out_shape=[
            shape((tokens, width)),
            shape((tokens, width)),
            shape((width, 3 * fold * folds), LOW),
        ],
        scratch_shapes=[pltpu.VMEM((width, tokens), LOW)],
        compiler_params=pltpu.CompilerParams(vmem_limit_bytes=60 * 2**20),
        cost_estimate=guess(35),
        name="feed_forward",
    )(x, gy, plain, w)


def last_grads_kernel(x_ref, scan_ref, query_ref, kv_ref, small_ref, grad_ref):
    x_t = x_ref[...].astype(jnp.float32).T.astype(LOW)
    scan = scan_ref.shape[1]
    query = query_ref.shape[1]
    grad_ref[:, : scan - LANES] = nn(x_t, scan_ref[:, : scan - LANES]).astype(LOW)
    grad_ref[:, scan - LANES : scan] = (nn(x_t, scan_ref[:, scan - LANES :]) + small_ref[...]).astype(LOW)
    grad_ref[:, scan : scan + query] = nn(x_t, query_ref[...]).astype(LOW)
    grad_ref[:, scan + query :] = nn(x_t, kv_ref[...]).astype(LOW)


def last_grads(x, d_scan, d_query, d_kv, small):
    tokens, width = x.shape
    count = d_scan.shape[1] + d_query.shape[1] + d_kv.shape[1]
    return pl.pallas_call(
        last_grads_kernel,
        out_shape=shape((width, count), LOW),
        compiler_params=pltpu.CompilerParams(vmem_limit_bytes=56 * 2**20),
        cost_estimate=guess(8),
        name="last_grads",
    )(x, d_scan, d_query, d_kv, small)


def input_back_kernel(scan_ref, gate_ref, query_ref, kv_ref, w_ref, x_ref, more_ref, gain_ref, dx_ref):
    at, total = 0, None
    for ref in (scan_ref, gate_ref, query_ref, kv_ref):
        term = nt(ref[...], w_ref[:, at : at + ref.shape[1]])
        total = term if total is None else total + term
        at += ref.shape[1]
    x = x_ref[...]
    scale = lax.rsqrt(jnp.mean(x * x, axis=1, keepdims=True) + epsilon)
    u = total * gain_ref[...]
    inner = jnp.mean(u * x, axis=1, keepdims=True) * scale * scale * scale
    dx_ref[...] = (more_ref[...] + u * scale - x * inner).astype(LOW)


def input_back(d_scan, d_gate, d_query, d_kv, w, x, more, gain):
    tokens, width = x.shape
    part = min(2 * CHUNK, tokens)
    rows = lambda array: pl.BlockSpec((part, array.shape[1]), lambda i: (i, 0))
    whole = lambda array: pl.BlockSpec(array.shape, lambda i: (0, 0))
    return pl.pallas_call(
        input_back_kernel,
        grid=(tokens // part,),
        in_specs=[rows(a) for a in (d_scan, d_gate, d_query, d_kv)] + [whole(w), rows(x), rows(more), whole(gain)],
        out_specs=rows(x),
        out_shape=shape((tokens, width), LOW),
        compiler_params=pltpu.CompilerParams(vmem_limit_bytes=56 * 2**20),
        cost_estimate=guess(10),
        name="input_back",
    )(d_scan, d_gate, d_query, d_kv, w, x, more, gain)


def owned_kernel(count_ref, own_ref, a_ref, b_ref, c_ref, gain_ref, gate_ref, x_ref, bc_ref, dt_ref, query_ref, kv_ref, *outs):
    total = own_ref[...].astype(jnp.float32) * count_ref[0].astype(jnp.float32)
    total = total + a_ref[...].astype(jnp.float32) + b_ref[...].astype(jnp.float32) + c_ref[...].astype(jnp.float32)
    at, inner = 0, gate_ref[...]
    for weight_ref, out_ref in zip((x_ref, bc_ref, dt_ref, query_ref, kv_ref), outs):
        part = total[:, at : at + out_ref.shape[1]]
        out_ref[...] = part
        heads = weight_ref.shape[1]
        inner = inner + jnp.sum(weight_ref[...].astype(jnp.float32) * part[:, :heads], axis=1, keepdims=True)
        at += out_ref.shape[1]
    outs[-1][...] = inner / gain_ref[...].astype(jnp.float32)


def owned_last(own, got, counts, gain, gate, weights, sizes):
    rows = own.shape[0]
    arrays = (own, *got, gain, gate, *weights)
    whole = lambda dims: pl.BlockSpec(dims, lambda i: (0, 0))
    return pl.pallas_call(
        owned_kernel,
        grid=(1,),
        in_specs=[pl.BlockSpec(memory_space=pltpu.SMEM)] + [whole(array.shape) for array in arrays],
        out_specs=[whole((rows, size)) for size in sizes] + [whole((rows, 1))],
        out_shape=[shape((rows, size)) for size in sizes] + [shape((rows, 1))],
        compiler_params=pltpu.CompilerParams(vmem_limit_bytes=16 * 2**20),
        cost_estimate=guess(3),
        name="owned_last",
    )(counts, *arrays)


def tap_marks(starts, first, length, taps):
    ext = doc_index(starts, first - (taps - 1) + jnp.arange(length + taps - 1, dtype=jnp.int32))
    return jnp.stack([(ext[i : i + length] == ext[taps - 1 :]).astype(jnp.float32) for i in range(taps)], axis=1)


def marks_of(starts, block_base, length, taps):
    ext = doc_index(starts, block_base - (taps - 1) + jnp.arange(length + taps - 1, dtype=jnp.int32))
    here = ext[taps - 1 :]
    chunks = here.reshape(-1, CHUNK)
    ahead = ext[taps - 2 : taps - 2 + length].reshape(-1, CHUNK)[:, :1]
    last = chunks[:, -1:]
    columns = [ext[i : i + length] == here for i in range(taps)] + [
        (chunks == ahead).reshape(-1),
        (chunks == last).reshape(-1),
        here,
        jnp.broadcast_to(last == ahead, chunks.shape).reshape(-1),
    ]
    marks = jnp.stack([column.astype(jnp.float32) for column in columns], axis=1)
    marks = jnp.pad(marks, ((0, 0), (0, LANES - len(columns))))
    return marks, jnp.broadcast_to(here.astype(jnp.float32)[None], (8, length)), here


def per_device(
    hidden_in,
    cotangent,
    doc_starts,
    gain_in,
    mamba_gate_w,
    mamba_in_w,
    mamba_bc_w,
    mamba_dt_w,
    dt_bias,
    a_log,
    d_skip,
    conv_x,
    conv_bc,
    mamba_gain,
    attn_q_w,
    attention_key_value_weight,
    mamba_out_w,
    attn_out_w,
    gain_ffn,
    ffn_gate_w,
    ffn_up_w,
    ffn_down_w,
):
    devices = lax.axis_size("head") * lax.axis_size("wide")
    wide_id = lax.axis_index("wide")
    micro_count = hidden_in.shape[0]
    block_tok = hidden_in.shape[2] * lax.axis_size("head")
    taps = conv_x.shape[0]
    heads = dt_bias.shape[0]
    rows, inner = mamba_gate_w.shape
    width = rows * devices
    bc_cols = mamba_bc_w.shape[1]
    query_cols = attn_q_w.shape[1]
    kv_cols = attention_key_value_weight.shape[1]
    hidden = ffn_gate_w.shape[1]
    out_rows = mamba_out_w.shape[0]
    attn_rows = attn_out_w.shape[0]
    chan = conv_x.shape[1]
    chan_bc = conv_bc.shape[1]

    scan_cols = inner + bc_cols
    first_cols = scan_cols + LANES

    heads_dev, wide_dev = lax.axis_size("head"), lax.axis_size("wide")
    folds = hidden // width
    feature = jnp.arange(width, dtype=jnp.int32)
    inside = (feature // rows) % wide_dev * heads_dev + feature // (rows * wide_dev)
    order = (inside[:, None] * rows + (feature % rows)[:, None] == feature[None, :]).astype(LOW)

    def mixed(array):
        return nn(array.reshape(-1, width), order).astype(LOW).reshape(array.shape)

    def plain(array):
        return nt(array.reshape(-1, width), order).astype(LOW).reshape(array.shape)

    def by_place(array):
        return array.reshape((heads_dev, wide_dev) + array.shape[1:]).swapaxes(0, 1).reshape(array.shape)

    def by_owner(array):
        return array.reshape((wide_dev, heads_dev) + array.shape[1:]).swapaxes(0, 1).reshape(array.shape)

    def folded(weight):
        return weight.reshape(rows, heads_dev, wide_dev, folds, rows).transpose(0, 3, 2, 1, 4).reshape(rows, folds, width)

    def unfolded(parts):
        unit = jnp.arange(hidden, dtype=jnp.int32)
        owner, fold, row = unit // (folds * rows), unit // rows % folds, unit % rows
        at = (owner % wide_dev * heads_dev + owner // wide_dev) * rows + row
        total = 0.0
        for i, part in enumerate(parts):
            one_hot = ((feature[:, None] == at[None, :]) & (fold == i)[None, :]).astype(LOW)
            total = total + nn(jnp.concatenate(split_low(part, 3), axis=0), one_hot)
        high, middle, low = split_at(total, (rows,) * 3, 0)
        return high + (middle + low)

    small = packed([gain_in, gain_ffn, mamba_gain, conv_x, conv_bc], rows)
    small_cols = small.shape[1]
    pad = jnp.zeros((rows, LANES - heads - small_cols), LOW)
    in_shard = jnp.concatenate(
        [mamba_in_w, mamba_bc_w, mamba_dt_w, small, pad, mamba_gate_w, attn_q_w, attention_key_value_weight], axis=1
    )
    to_width = mixed(jnp.concatenate([ffn_down_w, mamba_out_w, attn_out_w], axis=0)).reshape(-1, rows, width)
    gate_folds, up_folds = folded(ffn_gate_w), folded(ffn_up_w)
    ffn_shard = []
    for i in range(folds):
        ffn_shard += [gate_folds[:, i], up_folds[:, i], to_width[i]]
    ffn_shard = jnp.concatenate(ffn_shard, axis=1)
    out_shard = jnp.concatenate([to_width[i] for i in range(folds, to_width.shape[0])], axis=1)
    x_pieces = mixed(hidden_in[:, 0])

    micro = jnp.minimum(lax.axis_index("head"), micro_count - 1)
    starts = pick(doc_starts, micro)
    block_base = wide_id * block_tok
    marks, docs_row, doc_here = marks_of(starts, block_base, block_tok, taps)
    key_doc = doc_index(starts, jnp.arange(block_tok * lax.axis_size("wide"), dtype=jnp.int32))
    masks = attend_masks(doc_here, key_doc, doc_starts.shape[1])
    mats = head_matrices(inner, heads)
    bias_row = lanes_row(dt_bias)
    rate_row = lanes_row(-jnp.exp(a_log))
    skip_row = jnp.repeat(d_skip, inner // heads)[None]
    in_rows = HeadRows(in_shard, micro_count)
    prepared = (marks, docs_row, masks, mats, bias_row, rate_row, skip_row, ffn_shard, out_shard, x_pieces)
    in_rows.got, prepared = tied(in_rows.got, prepared)
    marks, docs_row, masks, mats, bias_row, rate_row, skip_row, ffn_shard, out_shard, x_pieces = prepared
    in_rows, out_shard = tied(in_rows.end(), out_shard)
    w_in = gather_wide(in_rows)
    out_rows_all, x_pieces = tied(HeadRows(out_shard, micro_count).end(), x_pieces)
    x_low, ffn_shard = tied(ToBlocks(x_pieces).end(), ffn_shard)
    ffn_rows = HeadRows(ffn_shard, micro_count)
    w_in, out_rows_all = tied(w_in, out_rows_all)
    w_out = gather_wide(out_rows_all)
    x_tokens = x_low.astype(jnp.float32)

    small_at = scan_cols + heads
    w_scan, w_gate, w_qkv = split_at(w_in, (first_cols, inner, query_cols + kv_cols), 1)
    small_all = w_scan[:, small_at : small_at + small_cols].reshape(devices, -1).astype(jnp.float32)
    g_in, g_ffn, g_mamba, c_x, c_bc = split_at(
        small_all, (rows, rows, chan, taps * chan, taps * chan_bc), 1
    )
    gain_in_all = g_in.reshape(-1)
    gain_ffn_all = g_ffn.reshape(-1)
    g_mamba, c_x, c_bc = by_owner(g_mamba), by_owner(c_x), by_owner(c_bc)
    gain_mamba_row = g_mamba.reshape(1, -1)
    taps_all = jnp.concatenate(
        [
            c_x.reshape(devices, taps, chan).transpose(1, 0, 2).reshape(taps, -1),
            c_bc.reshape(devices, taps, chan_bc).transpose(1, 0, 2).reshape(taps, -1),
        ],
        axis=1,
    )
    cols = (inner, bc_cols, 0, inner // bc_cols, scan_cols // LANES)
    place = jnp.reshape(wide_id, (1,)).astype(jnp.int32)


    block_in = rms_scale(x_tokens, gain_in_all).astype(LOW)
    raw_qkv, block_in = tied(nn(block_in, w_qkv).astype(LOW), block_in)
    keys = Gathered(raw_qkv[:, query_cols:])
    keys.begin()
    keys.got, raw_scan, block_in = tied(keys.got, nn(block_in, w_scan), block_in)
    keys.end()
    rim = shifted(raw_scan[block_tok - 8 :, :scan_cols], "wide", 1)
    keys.begin()
    rim, raw_gate = tied(rim, nn(block_in, w_gate))
    rim = jnp.where(jnp.arange(8)[:, None] > 8 - taps, rim, 0.0)
    taps_ext = jnp.pad(taps_all, ((0, 8 - taps), (0, 0)))
    *feats, sent, total, decay_rows = mamba_local(raw_scan, rim, marks, taps_ext, bias_row, rate_row, cols, mats)
    keys.got, ffn_rows.got, sent = tied(keys.got, ffn_rows.got, sent)
    ffn_rows, w_out = tied(ffn_rows.end(), w_out)
    w_ffn = gather_wide(ffn_rows)
    keys.end()
    forward = Carried(sent, total, decay_rows, False)
    forward.begin()
    key_all = keys.rest()
    forward.end()
    q_rows = raw_qkv[:, :query_cols].T.reshape(QUERY_HEADS, HEAD_SIZE, block_tok)
    gy = ToBlocks(cotangent[:, 0])
    forward.begin()
    out_0, q_back_0 = attend(0, q_rows, key_all, masks, place)
    forward.got, gy.got, out_0, q_rows = tied(forward.got, gy.got, out_0, q_rows)
    forward.end()
    forward.sent, q_rows = tied(forward.sent, q_rows)
    forward.begin()
    out_1, q_back_1 = attend(1, q_rows, key_all, masks, place)
    forward.got, out_1 = tied(forward.got, out_1)
    state_in = forward.last()
    attn_low = jnp.concatenate([out_0, out_1], axis=0).reshape(query_cols, block_tok).astype(LOW)
    mamba_low, y_low, entry = mamba_mix(feats, raw_gate, marks, docs_row, state_in, skip_row, gain_mamba_row, mats)
    gy_plain = gy.end()
    d_out_low = mixed(gy_plain)
    out_both = jnp.concatenate(
        [w_out[:, i : i + width].reshape(devices, rows, width) for i in range(0, w_out.shape[1], width)], axis=1
    )
    out_both = by_owner(out_both)
    w_mamba_out = out_both[:, :out_rows].reshape(-1, width)
    w_attn_out = out_both[:, out_rows:].reshape(-1, width)

    resid = x_tokens + nn(mamba_low, w_mamba_out) + tn(attn_low, w_attn_out)
    normed_ffn, pull_ffn = jax.vjp(lambda values: rms_scale(values, gain_ffn_all), resid)
    ffn_in = normed_ffn.astype(LOW)
    fed, d_ffn_in, grad_ffn = feed_forward(ffn_in, d_out_low, gy_plain, w_ffn, folds, width)
    part_ffn = sum_wide(grad_ffn)
    out_low = (resid + fed).astype(LOW)
    (d_resid_norm,) = pull_ffn(d_ffn_in)
    d_resid = d_out_low.astype(jnp.float32) + d_resid_norm

    d_mix = d_resid.astype(LOW)
    d_gate_z, dy_low, sent_back, total, decay_rows = mamba_gate_back(
        nt(d_mix, w_mamba_out), y_low, raw_gate, feats, marks, gain_mamba_row, mats
    )
    backward = Carried(sent_back, total, decay_rows, True)
    backward.begin()
    d_attn = nt(w_attn_out, d_mix).astype(LOW).reshape(QUERY_HEADS, HEAD_SIZE, block_tok)
    backward.got, d_attn = tied(backward.got, d_attn)
    backward.end()
    backward.sent, d_attn = tied(backward.sent, d_attn)
    backward.begin()
    d_query_0, d_kv_0 = attend_back(0, q_back_0, out_0, d_attn, key_all, masks, place)
    backward.got, d_query_0, d_kv_0, d_attn = tied(backward.got, d_query_0, d_kv_0, d_attn)
    backward.end()
    backward.sent, d_attn, d_kv_0 = tied(backward.sent, d_attn, d_kv_0)
    backward.begin()
    core_0 = CoreSum(d_kv_0)
    d_query_1, d_kv_1 = attend_back(1, q_back_1, out_1, d_attn, key_all, masks, place)
    backward.got, core_0.got, d_query_1, d_kv_1 = tied(backward.got, core_0.got, d_query_1, d_kv_1)
    d_state = backward.last()
    d_state, d_kv_1, d_mix = tied(d_state, d_kv_1, d_mix)
    core_1 = CoreSum(d_kv_1)
    d_query = jnp.concatenate([d_query_0, d_query_1], axis=0).reshape(query_cols, block_tok).T
    d_mix_plain = plain(d_mix)
    grad_out = jnp.concatenate(
        [
            tn(mamba_low, d_mix_plain).astype(LOW).reshape(devices, out_rows, width),
            nn(attn_low, d_mix_plain).astype(LOW).reshape(devices, attn_rows, width),
        ],
        axis=1,
    ).reshape(devices, -1, rows, width)
    grad_out = by_place(grad_out)
    grad_gate = tn(block_in, d_gate_z).astype(LOW)
    early = jnp.concatenate(
        [grad_out[:, i].reshape(width, width) for i in range(grad_out.shape[1])] + [grad_gate], axis=1
    )
    core_1.got, early = tied(core_1.got, early)
    chip_sum = ChipSum(jnp.concatenate([core_0.end(), core_1.end()], axis=2))
    early, part_ffn = tied(early, part_ffn)
    part_early = sum_wide(early)
    own_ffn = HeadSum(part_ffn, micro_count)
    d_scan, grad_skip, grad_head, grad_taps, rim_back, edge = mamba_scan_back(
        feats, raw_scan, rim, taps_ext, marks, docs_row, dy_low, entry, d_state,
        skip_row, bias_row, rate_row, cols, mats,
    )
    chip_sum.got, own_ffn.got, d_scan, edge, rim_back, grad_taps, grad_head, grad_skip, d_query, out_low = tied(
        chip_sum.got, own_ffn.got, d_scan, edge, rim_back, grad_taps, grad_head, grad_skip, d_query, out_low
    )
    rim_came = shifted(rim_back, "wide", -1)
    out_back = FromBlocks(out_low, micro_count)
    d_kv = chip_sum.end()
    d_scan = lax.dynamic_update_slice(d_scan, (edge + rim_came).astype(LOW), (block_tok - 8, 0))
    grad_small = jnp.concatenate(
        [
            by_place(grad_taps[:taps, :inner].reshape(taps, devices, chan).transpose(1, 0, 2).reshape(devices, -1)),
            by_place(grad_taps[:taps, inner:].reshape(taps, devices, chan_bc).transpose(1, 0, 2).reshape(devices, -1)),
        ],
        axis=1,
    )
    grad_small = jnp.pad(grad_small, ((0, 0), (0, rows * small_cols - grad_small.shape[1])))
    grad_small = jnp.pad(
        grad_small.reshape(width, small_cols), ((0, 0), (heads, LANES - heads - small_cols))
    )
    late = last_grads(block_in, d_scan, d_query, d_kv, grad_small)

    out_back.got, late, part_early, d_scan, grad_head, grad_skip, own_ffn.got, own_ffn.own = tied(
        out_back.got, late, part_early, d_scan, grad_head, grad_skip, own_ffn.got, own_ffn.own
    )
    part_late = sum_wide(late)
    head_sums = jnp.concatenate(
        [grad_head[:2, :heads].reshape(-1), jnp.sum(grad_skip[0].reshape(heads, -1), axis=1)]
    )
    totals = EverySum(head_sums)
    totals.begin()
    totals.got, part_early, d_scan = tied(totals.got, part_early, d_scan)
    totals.end()
    own_early = HeadSum(part_early, micro_count)
    totals.begin()
    grad_x = input_back(d_scan, d_gate_z, d_query, d_kv, w_in, x_tokens, d_resid, gain_in_all[None])
    own_early.got, own_early.own, totals.got, grad_x = tied(own_early.got, own_early.own, totals.got, grad_x)
    totals.end()
    x_plain, own_ffn.got, own_ffn.own = tied(plain(grad_x), own_ffn.got, own_ffn.own)
    own_ffn = own_ffn.end()
    x_back = FromBlocks(x_plain, micro_count)
    totals.begin()
    g_ffn = split_at(own_ffn, (width,) * (3 * folds), 1)
    g_gate_w, g_up_w = unfolded(g_ffn[0::3]), unfolded(g_ffn[1::3])
    totals.got, g_gate_w, g_up_w = tied(totals.got, g_gate_w, g_up_w)
    totals.end()
    totals.begin()
    *g_out, g_gate = own_early.end((width,) * ((out_rows + attn_rows) // rows) + (inner,))
    out_done = plain(out_back.end())
    x_back.got, g_out, g_gate, out_done, part_late, totals.got, g_gate_w, g_up_w = tied(
        x_back.got, g_out, g_gate, out_done, part_late, totals.got, g_gate_w, g_up_w
    )
    totals.end()
    own_late = HeadSum(part_late, micro_count)
    summed = totals.rest()
    results = x_back.end()
    own_late.got, results = tied(own_late.got, results)
    per_head = summed[: 3 * heads].reshape(3, heads)
    gate_sum = jnp.sum(mamba_gate_w.astype(jnp.float32) * g_gate, axis=1, keepdims=True)
    summing = (lax.axis_index("head") < micro_count).astype(jnp.int32).reshape(1)
    g_x, g_bc, g_tail, g_q, g_kv, o_gain_in = owned_last(
        own_late.own,
        own_late.got,
        summing,
        gain_in[:, None],
        gate_sum,
        (mamba_in_w, mamba_bc_w, mamba_dt_w, attn_q_w, attention_key_value_weight),
        (inner, bc_cols, LANES, query_cols, kv_cols),
    )
    g_dt, g_small, _ = split_at(g_tail, (heads, small_cols, LANES - heads - small_cols), 1)
    o_conv_x, o_conv_bc, _ = split_at(
        g_small.reshape(-1), (taps * chan, taps * chan_bc, rows * small_cols - taps * (chan + chan_bc)), 0
    )
    g_mamba_out, g_attn_out = split_at(jnp.concatenate(g_out, axis=0), (out_rows, attn_rows), 0)
    def gain_grad(gain, pairs):
        total = 0.0
        for weight, grad in pairs:
            total = total + jnp.sum(weight.astype(jnp.float32) * grad, axis=1)
        return total / gain.astype(jnp.float32)

    o_gain_ffn = gain_grad(gain_ffn, ((ffn_gate_w, g_gate_w), (ffn_up_w, g_up_w)))
    o_gain_m = gain_grad(mamba_gain, ((mamba_out_w, g_mamba_out),))
    return (
        out_done[:, None],
        results[:, None],
        o_gain_in[:, 0],
        g_gate,
        g_x,
        g_bc,
        g_dt,
        per_head[0],
        per_head[1],
        per_head[2],
        o_conv_x.reshape(taps, chan),
        o_conv_bc.reshape(taps, chan_bc),
        o_gain_m,
        g_q,
        g_kv,
        g_mamba_out,
        g_attn_out,
        o_gain_ffn,
        g_gate_w,
        g_up_w,
        jnp.concatenate(g_ffn[2::3], axis=0),
    )


def solution(mesh):
    tokens = P(None, "wide", "head", None)
    matrix = P(ALL, None)
    vector = P(ALL)
    taps = P(None, ALL)
    in_specs = (
        (tokens, tokens, P(), vector)
        + (matrix,) * 4
        + (P(),) * 3
        + (taps, taps, vector)
        + (matrix,) * 4
        + (vector,)
        + (matrix,) * 3
    )
    out_specs = (
        (tokens, tokens, vector)
        + (matrix,) * 4
        + (P(),) * 3
        + (taps, taps, vector)
        + (matrix,) * 4
        + (vector,)
        + (matrix,) * 3
    )
    return jax.shard_map(
        per_device, mesh=mesh, in_specs=in_specs, out_specs=out_specs, check_vma=False
    )
```
